32 devices in a mesh: gx: 4 (over z), gy: 4 (over x, core), pa: 2 (over y).
Axes of the slice: x: 2, y: 2, z: 4, core: 2. Of those that a mesh axis runs over, the one named last changes fastest.
Arguments:
- conductivity: float32 [32, 512, 256], P('gx', 'gy', 'pa'), may hold values from 0.5 to 1
- stored_state: bfloat16 [32, 512, 256], P('gx', 'gy', 'pa'), may hold values from -4 to 5
- row_scales: float32 [32, 512], P('gx', 'gy'), may hold values from 0.5 to 4
- cotangent: float32 [32, 512, 256], P('gx', 'gy', 'pa'), may hold values from -5 to 6
- upper_bound: float32 [1], replicated, may hold values from 97 to 145
Outputs:
- grad_conductivity: float32 [32, 512, 256], P('gx', 'gy', 'pa')
- adjoint: float32 [32, 512, 256], P('gx', 'gy', 'pa')
- state_new: float32 [32, 512, 256], P('gx', 'gy', 'pa')
- residuals: float32 [2, 32, 512, 256], P(None, 'gx', 'gy', 'pa')
The draws below stay inside these ranges and needn't reach their ends.
All inputs are finite; a program needn't handle non-finite values.
Results may differ from the reference program's by a relative error of at most 0.0003.
Values may be sent and summed in bfloat16 or wider, within the bound.
No kernel may reach another device: no remote copies, remote signals or barrier semaphores. Data moves between devices by JAX's collectives and lax.ppermute only.
A program may use at most 128 MiB of HBM per device.

```python
import math
import jax
import jax.numpy as jnp

CZ = 128
CHEB = 16
NX = 32
NY = 512
NZ = 256


def smooth_pattern(shape_key):
    phases = jax.random.uniform(shape_key, (3,), jnp.float32, 0.0, 2.0 * math.pi)
    wave_first = jnp.cos(2.0 * math.pi * jnp.arange(NX, dtype=jnp.float32) / NX + phases[0])
    wave_second = jnp.cos(2.0 * math.pi * jnp.arange(NY, dtype=jnp.float32) / NY + phases[1])
    wave_third = jnp.cos(2.0 * math.pi * jnp.arange(NZ, dtype=jnp.float32) / NZ + phases[2])
    return wave_first[:, None, None] * wave_second[None, :, None] * wave_third[None, None, :]


def draw_stored_state(key, part):
    shape_key = jax.random.fold_in(key, 11)
    jitter_key = jax.random.fold_in(key, 12)
    pattern = smooth_pattern(shape_key)
    jitter = jax.random.normal(jitter_key, (NX, NY, NZ), jnp.float32)
    drawn = 1.0 + 0.4 * pattern + jitter
    return jnp.clip(drawn, -4.0, 5.0).astype(jnp.bfloat16)


def draw_cotangent(key, part):
    shape_key = jax.random.fold_in(key, 21)
    jitter_key = jax.random.fold_in(key, 22)
    pattern = smooth_pattern(shape_key)
    jitter = jax.random.normal(jitter_key, (NX, NY, NZ), jnp.float32)
    drawn = 0.8 + 0.3 * pattern + jitter
    return jnp.clip(drawn, -5.0, 6.0).astype(jnp.float32)


def level_of(key, dims, shards, least, largest):
    level, own = 1.0, jax.random.fold_in(key, 6)
    for position, blocks in shards:
        draws = jnp.exp(jax.random.uniform(jax.random.fold_in(own, position), (blocks,), jnp.float32, least / len(shards), largest / len(shards)))
        level = level * jnp.repeat(draws, dims[position] // blocks).reshape([-1 if axis == position else 1 for axis in range(len(dims))])
    return level


def setup_inputs(seed: int = 0) -> dict:
    splits = jax.random.split(jax.random.key(seed), 6)
    conductivity = jnp.clip(jnp.exp(math.log(1.0) - 0.6931472 * jax.random.uniform(splits[0], (NX, NY, NZ), jnp.float32) ** level_of(splits[0], (NX, NY, NZ), ((0, 4), (1, 4), (2, 2)), -0.2, 0.2)), 0.5, 1.0)
    stored_state = draw_stored_state(jax.random.fold_in(splits[5], 71), 0)
    row_scales = jnp.clip(jnp.exp(math.log(4.0) - 2.0794415 * jax.random.uniform(splits[2], (NX, NY), jnp.float32) ** level_of(splits[2], (NX, NY), ((0, 4), (1, 4)), -0.2, 0.2)), 0.5, 4.0)
    cotangent = draw_cotangent(jax.random.fold_in(splits[5], 71), 0)
    upper_bound = jnp.clip(jax.random.uniform(splits[4], (1,), jnp.float32, 97.0, 145.0), 97.0, 145.0)
    return {"conductivity": conductivity, "stored_state": stored_state, "row_scales": row_scales, "cotangent": cotangent, "upper_bound": upper_bound}


time_step = 8.0


def apply_operator(field, kappa):
    summed = jnp.zeros_like(field)
    for spatial in range(3):
        for shift in (1, -1):
            summed = summed + 0.5 * (kappa + jnp.roll(kappa, shift, spatial)) * (field - jnp.roll(field, shift, spatial))
    return field + time_step * summed


def chebyshev(rhs, kappa, upper):
    theta = 0.5 * (upper + 1.0)
    delta = 0.5 * (upper - 1.0)
    sigma = theta / delta
    rho = 1.0 / sigma
    solution = jnp.zeros_like(rhs)
    residual = rhs
    direction = rhs / theta
    for step in range(CHEB):
        solution = solution + direction
        residual = residual - apply_operator(direction, kappa)
        rho_next = 1.0 / (2.0 * sigma - rho)
        direction = rho_next * rho * direction + (2.0 * rho_next / delta) * residual
        rho = rho_next
    return solution, residual


def reference(conductivity, stored_state, row_scales, cotangent, upper_bound):
    upper = upper_bound[0]
    previous = jnp.roll(stored_state.astype(jnp.float32), CZ, 2) * row_scales[:, :, None]
    state_new, forward_res = chebyshev(previous, conductivity, upper)
    adjoint, adjoint_res = chebyshev(cotangent, conductivity, upper)
    summed = jnp.zeros_like(state_new)
    for spatial in range(3):
        for shift in (1, -1):
            summed = summed + (state_new - jnp.roll(state_new, shift, spatial)) * (adjoint - jnp.roll(adjoint, shift, spatial))
    grad_conductivity = -0.5 * time_step * summed
    return grad_conductivity, adjoint, state_new, jnp.stack((forward_res, adjoint_res))
```

```python
import functools

import jax
import jax.numpy as jnp
from jax import lax
from jax.experimental import pallas as pl
from jax.experimental.pallas import tpu as pltpu
from jax.sharding import PartitionSpec as P

CHEB = 16
LANES = 128
HALO = CHEB
TIME_STEP = 8.0
F32 = jnp.float32


def with_halo(cells, sides, width):
    for axis, dim in sides:
        count = lax.axis_size(axis)
        head = lax.slice_in_dim(cells, 0, width, axis=dim)
        tail = lax.slice_in_dim(cells, cells.shape[dim] - width, cells.shape[dim], axis=dim)
        cells = jnp.concatenate(
            [
                lax.ppermute(tail, axis, [(i, (i + 1) % count) for i in range(count)]),
                cells,
                lax.ppermute(head, axis, [((i + 1) % count, i) for i in range(count)]),
            ],
            axis=dim,
        )
    return cells


def region(arr, spatial, offset):
    extent = arr.shape[-3:]
    window = [slice(1, length - 1) for length in extent]
    window[spatial] = slice(offset, extent[spatial] - 2 + offset)
    leading = [slice(None)] * (arr.ndim - 3)
    return arr[tuple(leading + window)]


def apply_operator(padded, kpad):
    centre = region(padded, 0, 1)
    kcentre = region(kpad, 0, 1)
    summed = jnp.zeros_like(centre)
    for spatial in range(3):
        for offset in (0, 2):
            summed = summed + 0.5 * (kcentre + region(kpad, spatial, offset)) * (
                centre - region(padded, spatial, offset)
            )
    return centre + TIME_STEP * summed


def stepwise(conductivity, stored_state, row_scales, cotangent, upper_bound):
    upper = upper_bound[0]
    kpad = with_halo(conductivity, (("gx", 0), ("gy", 1), ("pa", 2)), 1)
    count = lax.axis_size("pa")
    partner = lax.ppermute(stored_state, "pa", [(i, (i + count // 2) % count) for i in range(count)])
    previous = partner.astype(F32) * row_scales[:, :, None]
    rhs = jnp.stack((previous, cotangent))
    theta = 0.5 * (upper + 1.0)
    delta = 0.5 * (upper - 1.0)
    sigma = theta / delta
    sides = (("gx", 1), ("gy", 2), ("pa", 3))

    def sweep(step, carry):
        solved, residual, direction, rho = carry
        padded = with_halo(direction, sides, 1)
        solved = solved + direction
        residual = residual - apply_operator(padded, kpad)
        rho_next = 1.0 / (2.0 * sigma - rho)
        direction = rho_next * rho * direction + 2.0 * rho_next / delta * residual
        return (solved, residual, direction, rho_next)

    start = (jnp.zeros_like(rhs), rhs, rhs / theta, 1.0 / sigma)
    solved, residual, _, _ = lax.fori_loop(0, CHEB, sweep, start)
    pair = with_halo(solved, sides, 1)
    centre = region(pair, 0, 1)
    summed = jnp.zeros_like(solved[0])
    for spatial in range(3):
        for offset in (0, 2):
            differ = centre - region(pair, spatial, offset)
            summed = summed + differ[0] * differ[1]
    return (-0.5 * TIME_STEP * summed, solved[1], solved[0], residual)


G = 4
BX = 8
BY = 128
BZ = 128
STRIP = BZ // G
NXL = G * BX // 2
TOP = 8 + HALO
ROWS = BY + 2 * TOP
MROWS = BY + 8


def lane_ids(rows):
    return lax.broadcasted_iota(jnp.int32, (rows, LANES), 1)


def turn(x, shift):
    return pltpu.roll(x, lax.rem(shift + 4 * LANES, LANES), 1)


def pack_kernel(strips, cond, stored, scales, cot, *outs):
    group = lane_ids(BY) // STRIP
    for a in range(2):
        planes = []
        for b in range(4):
            c = 4 * a + b
            planes.append(
                (cond[c], stored[c].astype(F32) * scales[c], cot[c])
            )
        for d in range(G):
            s = strips[d]
            for n in range(3):
                acc = turn(planes[0][n], -STRIP * s)
                for b in range(1, 4):
                    acc = jnp.where(group == b, turn(planes[b][n], STRIP * b - STRIP * s), acc)
                outs[d][n, a] = acc


def edge_kernel(sources, *refs):
    msgs, (left, right) = refs[:G], refs[G:]
    low = lax.rem(lane_ids(BY), STRIP) < STRIP // 2
    for n in range(3):
        for d in range(G):
            source = sources[d]
            first, second = msgs[d][n, 0], msgs[d][n, 1]
            left[n, source] = jnp.where(low, first, pltpu.roll(second, STRIP // 2, 1))
            right[n, source] = jnp.where(low, pltpu.roll(first, LANES - STRIP // 2, 1), second)


def build_kernel(sources, *refs):
    msgs, (from_left, from_right), (whole, head, tail) = refs[:G], refs[G : G + 2], refs[G + 2 :]
    lane = lane_ids(BY)
    for d in range(G):
        source = sources[d]
        half = 64 * (source // 2)
        first = BX * lax.rem(source, 2)
        place = lane - half
        for n in range(3):
            for a in range(2):
                own = msgs[d][n, a]
                lo = from_left[n, source]
                hi = from_right[n, source]
                for b in range(4):
                    val = jnp.where(
                        place < HALO,
                        turn(lo, half - 32 * b - 16 * a),
                        jnp.where(
                            place < HALO + STRIP,
                            turn(own, half + HALO - 32 * b),
                            turn(hi, half + HALO + STRIP - 32 * b - 16 * a),
                        ),
                    )
                    at = first + 4 * a + b
                    keep = (place >= 0) & (place < 64)
                    whole[n, at] = jnp.where(keep, val, whole[n, at])
    for n in range(3):
        for i in range(NXL):
            head[n, i] = whole[n, i, :HALO]
            tail[n, i] = whole[n, i, BY - HALO :]


def solve_kernel(homes, scalars, whole, above, below, *refs):
    outs = refs[:G]
    xs, rhs, kap, kx, ky, kz, diag = refs[G:]
    nf = 2
    zero8 = jnp.zeros((8, LANES), F32)
    for i in range(NXL):
        for n, dst in ((0, kap), (1, rhs.at[0]), (2, rhs.at[1])):
            dst[i, 0:8] = zero8
            dst[i, ROWS - 8 : ROWS] = zero8
            dst[i, 8:TOP] = above[n, i]
            dst[i, TOP : TOP + BY] = whole[n, i]
            dst[i, TOP + BY : ROWS - 8] = below[n, i]

    @pl.loop(0, ROWS // 8 - 2)
    def _(t):
        r = pl.multiple_of(8 + 8 * t, 8)
        now = kap[0, pl.ds(r, 8)]
        wrapped = pltpu.roll(now, 64, 1)
        for i in range(NXL):
            after = kap[i + 1, pl.ds(r, 8)] if i + 1 < NXL else wrapped
            kx[i, pl.ds(r, 8)] = 4.0 * (now + after)
            ky[i, pl.ds(r, 8)] = 4.0 * (now + kap[i, pl.ds(r + 1, 8)])
            kz[i, pl.ds(r, 8)] = 4.0 * (now + pltpu.roll(now, LANES - 1, 1))
            now = after

    for i in range(NXL):
        ky[i, 0:8] = zero8
    theta_inv = scalars[0, 0]

    @pl.loop(0, ROWS // 8 - 2)
    def _(t):
        r = pl.multiple_of(8 + 8 * t, 8)
        before = pltpu.roll(kx[NXL - 1, pl.ds(r, 8)], 64, 1)
        for i in range(NXL):
            fx = kx[i, pl.ds(r, 8)]
            fz = kz[i, pl.ds(r, 8)]
            total = fx + before + ky[i, pl.ds(r, 8)] + ky[i, pl.ds(r - 1, 8)]
            diag[i, pl.ds(r, 8)] = 1.0 + (total + (fz + pltpu.roll(fz, 1, 1)))
            before = fx
            for f in range(nf):
                xs[0, f, i, pl.ds(r, 8)] = rhs[f, i, pl.ds(r, 8)] * theta_inv
                xs[1, f, i, pl.ds(r, 8)] = zero8

    for i in range(NXL):
        for f in range(nf):
            for slot in range(2):
                xs[slot, f, i, 0:8] = zero8
                xs[slot, f, i, ROWS - 8 : ROWS] = zero8

    def sweep(k, first, count):
        alpha, beta = scalars[k, 0], scalars[k, 1]
        cur = lax.rem(k + 1, 2)
        new = lax.rem(k, 2)

        @pl.loop(0, count)
        def _(t):
            r = pl.multiple_of(first + 8 * t, 8)
            now = [xs[cur, f, 0, pl.ds(r, 8)] for f in range(nf)]
            wrapped = [pltpu.roll(x, 64, 1) for x in now]
            before = [pltpu.roll(xs[cur, f, NXL - 1, pl.ds(r, 8)], 64, 1) for f in range(nf)]
            fbefore = pltpu.roll(kx[NXL - 1, pl.ds(r, 8)], 64, 1)
            for i in range(NXL):
                fx = kx[i, pl.ds(r, 8)]
                fy = ky[i, pl.ds(r, 8)]
                fym = ky[i, pl.ds(r - 1, 8)]
                fz = kz[i, pl.ds(r, 8)]
                centre = (1.0 + alpha) - beta * diag[i, pl.ds(r, 8)]
                for f in range(nf):
                    x = now[f]
                    after = xs[cur, f, i + 1, pl.ds(r, 8)] if i + 1 < NXL else wrapped[f]
                    near = fx * after + fbefore * before[f]
                    near = near + (fy * xs[cur, f, i, pl.ds(r + 1, 8)] + fym * xs[cur, f, i, pl.ds(r - 1, 8)])
                    near = near + (fz * pltpu.roll(x, LANES - 1, 1) + pltpu.roll(fz * x, 1, 1))
                    near = near + rhs[f, i, pl.ds(r, 8)]
                    xs[new, f, i, pl.ds(r, 8)] = (
                        centre * x - alpha * xs[new, f, i, pl.ds(r, 8)] + beta * near
                    )
                    before[f] = x
                    now[f] = after
                fbefore = fx

    @pl.loop(1, CHEB // 2)
    def _(k):
        sweep(k, 8, ROWS // 8 - 2)

    @pl.loop(CHEB // 2, CHEB)
    def _(k):
        sweep(k, 16, ROWS // 8 - 4)

    last = (CHEB - 1) % 2
    lane = lane_ids(8)
    group = lane // STRIP
    sub = lax.broadcasted_iota(jnp.int32, (8, LANES), 0)

    for d in range(G):
        home = homes[d]
        half = 64 * (home // 2)
        i0 = BX * lax.rem(home, 2)
        down = lax.rem(BX * home + 31, 32)
        up = lax.rem(BX * home + 8, 32)

        def gather(f, a, row):
            if a < 2:
                acc = None
                for b in range(4):
                    val = turn(xs[last, f, i0 + 4 * a + b, pl.ds(row, 8)], 32 * b - half - HALO)
                    acc = val if b == 0 else jnp.where(group == b, val, acc)
                return acc
            acc = turn(xs[last, f, lax.rem(down, NXL), pl.ds(row, 8)], -64 * (down // NXL) - HALO)
            val = turn(xs[last, f, lax.rem(up, NXL), pl.ds(row, 8)], 32 - 64 * (up // NXL) - HALO)
            acc = jnp.where(group == 1, val, acc)
            for c in range(BX):
                plane = xs[last, f, i0 + c, pl.ds(row, 8)]
                acc = jnp.where(lane == 64 + c, turn(plane, 64 + c - half - HALO + 1), acc)
                acc = jnp.where(lane == 72 + c, turn(plane, 72 + c - half - HALO - STRIP), acc)
            return acc

        for f in range(nf):

            @pl.loop(0, BY // 8)
            def _(t):
                for a in range(3):
                    outs[d][f, a, pl.ds(pl.multiple_of(8 * t, 8), 8)] = gather(
                        f, a, pl.multiple_of(TOP + 8 * t, 8)
                    )

            for a in range(2):
                over = pltpu.roll(gather(f, a, TOP - 8), 1, 0)
                under = pltpu.roll(gather(f, a, TOP + BY), 1, 0)
                outs[d][f, a, BY : BY + 8] = jnp.where(sub == 0, over, under)
            outs[d][f, 2, BY : BY + 8] = zero8


def final_kernel(strips, m0, m1, m2, m3, cond, kdown, kup, kover, kunder, kzl, kzr, stored, scales, cot, grad, adjoint, state, residuals, xs, ends, kap):
    msgs = (m0, m1, m2, m3)
    lane = lane_ids(BY)
    group = lane // STRIP
    for f in range(2):
        for d in range(G):
            s = strips[d]
            mine = group == s
            ends[f, s] = msgs[d][f, 2, :BY]
            for a in range(2):
                for b in range(4):
                    at = 1 + 4 * a + b
                    val = turn(msgs[d][f, a, :BY], STRIP * s - STRIP * b)
                    xs[f, at, 8 : 8 + BY] = jnp.where(mine, val, xs[f, at, 8 : 8 + BY])
                    val = pltpu.roll(turn(msgs[d][f, a, BY : BY + 8], STRIP * s - STRIP * b), 7, 0)
                    xs[f, at, 0:8] = jnp.where(mine[:8], val, xs[f, at, 0:8])
                    xs[f, at, 8 + BY : 16 + BY] = jnp.where(mine[:8], val, xs[f, at, 8 + BY : 16 + BY])
            for at, b in ((0, 0), (1 + BX, 1)):
                val = turn(msgs[d][f, 2, :BY], STRIP * s - STRIP * b)
                xs[f, at, 8 : 8 + BY] = jnp.where(mine, val, xs[f, at, 8 : 8 + BY])
    zero8 = jnp.zeros((8, LANES), F32)
    sub = lax.broadcasted_iota(jnp.int32, (8, LANES), 0)
    kap[0, 8 : 8 + BY] = kdown[...]
    kap[1 + BX, 8 : 8 + BY] = kup[...]
    for c in range(BX):
        kap[1 + c, 8 : 8 + BY] = cond[c]
        kap[1 + c, 0:8] = jnp.broadcast_to(kover[c : c + 1], (8, LANES))
        kap[1 + c, 8 + BY : 16 + BY] = jnp.broadcast_to(kunder[c : c + 1], (8, LANES))
    lane = lane[:8]

    @pl.loop(0, BY // 8)
    def _(t):
        r = pl.multiple_of(8 * t, 8)
        r8 = pl.multiple_of(8 * t + 8, 8)
        for c in range(BX):
            k = kap[1 + c, pl.ds(r8, 8)]
            x = [xs[f, 1 + c, pl.ds(r8, 8)] for f in range(2)]
            total = [0.0, 0.0]
            product = 0.0

            def sides():
                for at in (c, c + 2):
                    yield kap[at, pl.ds(r8, 8)], [xs[f, at, pl.ds(r8, 8)] for f in range(2)]
                for off in (-1, 1):
                    yield kap[1 + c, pl.ds(r8 + off, 8)], [xs[f, 1 + c, pl.ds(r8 + off, 8)] for f in range(2)]
                yield (
                    jnp.where(lane == 0, kzl[c, pl.ds(r, 8)], pltpu.roll(k, 1, 1)),
                    [
                        jnp.where(
                            lane == 0,
                            pltpu.roll(ends[f, 0, pl.ds(r, 8)], 64 - c, 1),
                            pltpu.roll(x[f], 1, 1),
                        )
                        for f in range(2)
                    ],
                )
                yield (
                    jnp.where(lane == LANES - 1, kzr[c, pl.ds(r, 8)], pltpu.roll(k, LANES - 1, 1)),
                    [
                        jnp.where(
                            lane == LANES - 1,
                            pltpu.roll(ends[f, G - 1, pl.ds(r, 8)], LANES - 1 - 72 - c, 1),
                            pltpu.roll(x[f], LANES - 1, 1),
                        )
                        for f in range(2)
                    ],
                )

            for kn, xn in sides():
                face = k + kn
                differ = [x[f] - xn[f] for f in range(2)]
                product = product + differ[0] * differ[1]
                for f in range(2):
                    total[f] = total[f] + face * differ[f]
            grad[c, pl.ds(r, 8)] = (-0.5 * TIME_STEP) * product
            state[c, pl.ds(r, 8)] = x[0]
            adjoint[c, pl.ds(r, 8)] = x[1]
            previous = stored[c, pl.ds(r, 8)].astype(F32) * scales[c, pl.ds(r, 8)]
            residuals[0, c, pl.ds(r, 8)] = previous - (x[0] + (0.5 * TIME_STEP) * total[0])
            residuals[1, c, pl.ds(r, 8)] = cot[c, pl.ds(r, 8)] - (x[1] + (0.5 * TIME_STEP) * total[1])


def call(kernel, outs, smem, vmem, scratch=()):
    vm = pl.BlockSpec(memory_space=pltpu.VMEM)
    sm = pl.BlockSpec(memory_space=pltpu.SMEM)
    return pl.pallas_call(
        kernel,
        out_shape=[jax.ShapeDtypeStruct(shape, F32) for shape in outs],
        in_specs=[sm] * len(smem) + [vm] * len(vmem),
        out_specs=[vm] * len(outs),
        scratch_shapes=[pltpu.VMEM(shape, F32) for shape in scratch],
        compiler_params=pltpu.CompilerParams(vmem_limit_bytes=48 * 1024 * 1024),
    )(*smem, *vmem)


def shifted(x, axis, by):
    count = lax.axis_size(axis)
    return lax.ppermute(x, axis, [(i, (i + by) % count) for i in range(count)])


def around(x, by):
    order = [2 * g for g in range(G)] + [2 * g + 1 for g in reversed(range(G))]
    pairs = [(order[i], order[(i + by) % len(order)]) for i in range(len(order))]
    return lax.ppermute(x, ("gx", "pa"), pairs)


def chebyshev_scalars(upper):
    theta = 0.5 * (upper + 1.0)
    delta = 0.5 * (upper - 1.0)
    sigma = theta / delta
    rho = 1.0 / sigma
    rows = [(1.0 / theta, 0.0 * theta)]
    for _ in range(1, CHEB):
        rho_next = 1.0 / (2.0 * sigma - rho)
        rows.append((rho_next * rho, 2.0 * rho_next / delta))
        rho = rho_next
    return jnp.stack([jnp.stack(row) for row in rows])


def redistributed(conductivity, stored_state, row_scales, cotangent, upper_bound):
    g = lax.axis_index("gx")
    pa = lax.axis_index("pa")

    def strip_of(device):
        return jnp.where(pa == 0, device, G - 1 - device)

    steps = jnp.arange(G, dtype=jnp.int32)
    ahead = lax.rem(g + steps, G)
    behind = lax.rem(g - steps + G, G)
    scalars = chebyshev_scalars(upper_bound[0])
    stored = shifted(stored_state, "pa", 1)
    scales = row_scales[:, :, None]

    kdown = shifted(conductivity[BX - 1], "gx", 1)
    kup = shifted(conductivity[0], "gx", -1)
    kover = shifted(conductivity[:, BY - 1], "gy", 1)
    kunder = shifted(conductivity[:, 0], "gy", -1)
    kends = shifted(jnp.stack((conductivity[:, :, BZ - 1], conductivity[:, :, 0])), "pa", 1)

    brick = (3, 2, BY, LANES)
    parts = call(pack_kernel, [brick] * G, [strip_of(ahead)], [conductivity, stored, scales, cotangent])
    parts = [parts[0]] + [shifted(parts[d], "gx", d) for d in range(1, G)]
    edge = (3, G, BY, LANES)
    left, right = call(edge_kernel, [edge] * 2, [behind], parts)
    from_right, from_left = around(left, -1), around(right, 1)
    whole, head, tail = call(
        build_kernel,
        [(3, NXL, BY, LANES), (3, NXL, HALO, LANES), (3, NXL, HALO, LANES)],
        [behind],
        [*parts, from_left, from_right],
    )
    below, above = shifted(head, "gy", -1), shifted(tail, "gy", 1)
    field = (NXL, ROWS, LANES)
    solved = call(
        solve_kernel,
        [(2, 3, MROWS, LANES)] * G,
        [ahead, scalars],
        [whole, above, below],
        [(2, 2) + field, (2,) + field] + [field] * 5,
    )
    solved = [solved[0]] + [shifted(solved[d], "gx", d) for d in range(1, G)]
    out = (BX, BY, LANES)
    padded = (BX + 2, BY + 16, LANES)
    return call(
        final_kernel,
        [out, out, out, (2,) + out],
        [strip_of(behind)],
        [*solved, conductivity, kdown, kup, kover, kunder, kends[0][:, :, None], kends[1][:, :, None], stored, scales, cotangent],
        [(2,) + padded, (2, G, BY, LANES), padded],
    )


def body(conductivity, stored_state, row_scales, cotangent, upper_bound):
    strips_fit = (
        lax.axis_size("gx") == G
        and lax.axis_size("pa") == 2
        and conductivity.shape == (BX, BY, BZ)
    )
    run = redistributed if strips_fit else stepwise
    return tuple(run(conductivity, stored_state, row_scales, cotangent, upper_bound))


def solution(mesh):
    return jax.shard_map(
        body,
        mesh=mesh,
        in_specs=(
            P("gx", "gy", "pa"),
            P("gx", "gy", "pa"),
            P("gx", "gy"),
            P("gx", "gy", "pa"),
            P(),
        ),
        out_specs=(
            P("gx", "gy", "pa"),
            P("gx", "gy", "pa"),
            P("gx", "gy", "pa"),
            P(None, "gx", "gy", "pa"),
        ),
        check_vma=False,
    )
```

```python
import functools

import jax
import jax.numpy as jnp
from jax import lax
from jax.experimental import pallas as pl
from jax.experimental.pallas import tpu as pltpu
from jax.sharding import PartitionSpec as P

CHEB = 16
LANES = 128
HALO = CHEB
TIME_STEP = 8.0
F32 = jnp.float32


def with_halo(cells, sides, width):
    for axis, dim in sides:
        count = lax.axis_size(axis)
        head = lax.slice_in_dim(cells, 0, width, axis=dim)
        tail = lax.slice_in_dim(cells, cells.shape[dim] - width, cells.shape[dim], axis=dim)
        cells = jnp.concatenate(
            [
                lax.ppermute(tail, axis, [(i, (i + 1) % count) for i in range(count)]),
                cells,
                lax.ppermute(head, axis, [((i + 1) % count, i) for i in range(count)]),
            ],
            axis=dim,
        )
    return cells


def region(arr, spatial, offset):
    extent = arr.shape[-3:]
    window = [slice(1, length - 1) for length in extent]
    window[spatial] = slice(offset, extent[spatial] - 2 + offset)
    leading = [slice(None)] * (arr.ndim - 3)
    return arr[tuple(leading + window)]


def apply_operator(padded, kpad):
    centre = region(padded, 0, 1)
    kcentre = region(kpad, 0, 1)
    summed = jnp.zeros_like(centre)
    for spatial in range(3):
        for offset in (0, 2):
            summed = summed + 0.5 * (kcentre + region(kpad, spatial, offset)) * (
                centre - region(padded, spatial, offset)
            )
    return centre + TIME_STEP * summed


def stepwise(conductivity, stored_state, row_scales, cotangent, upper_bound):
    upper = upper_bound[0]
    kpad = with_halo(conductivity, (("gx", 0), ("gy", 1), ("pa", 2)), 1)
    count = lax.axis_size("pa")
    partner = lax.ppermute(stored_state, "pa", [(i, (i + count // 2) % count) for i in range(count)])
    previous = partner.astype(F32) * row_scales[:, :, None]
    rhs = jnp.stack((previous, cotangent))
    theta = 0.5 * (upper + 1.0)
    delta = 0.5 * (upper - 1.0)
    sigma = theta / delta
    sides = (("gx", 1), ("gy", 2), ("pa", 3))

    def sweep(step, carry):
        solved, residual, direction, rho = carry
        padded = with_halo(direction, sides, 1)
        solved = solved + direction
        residual = residual - apply_operator(padded, kpad)
        rho_next = 1.0 / (2.0 * sigma - rho)
        direction = rho_next * rho * direction + 2.0 * rho_next / delta * residual
        return (solved, residual, direction, rho_next)

    start = (jnp.zeros_like(rhs), rhs, rhs / theta, 1.0 / sigma)
    solved, residual, _, _ = lax.fori_loop(0, CHEB, sweep, start)
    pair = with_halo(solved, sides, 1)
    centre = region(pair, 0, 1)
    summed = jnp.zeros_like(solved[0])
    for spatial in range(3):
        for offset in (0, 2):
            differ = centre - region(pair, spatial, offset)
            summed = summed + differ[0] * differ[1]
    return (-0.5 * TIME_STEP * summed, solved[1], solved[0], residual)


G = 4
BX = 8
BY = 128
BZ = 128
STRIP = BZ // G
NXL = G * BX // 2
TOP = 8 + HALO
ROWS = BY + 2 * TOP
MROWS = BY + 8
TILE = 8

FIRST = (0, 8, 0, 8)
HALF = (0, 1, 1, 0)


def roll(x, by):
    by %= LANES
    return pltpu.roll(x, by, 1) if by else x


def group_of(rows, strip):
    lane = lax.broadcasted_iota(jnp.int32, (rows, LANES), 1)
    return lax.rem(lane // STRIP - strip + G, G)


def pick(group, parts):
    out = parts[0]
    for b in range(1, G):
        out = jnp.where(group == b, parts[b], out)
    return out


def pack_kernel(strips, cond, stored, scales, cot, *outs):
    groups = [group_of(BY, strips[d]) for d in range(G)]
    for a in range(2):
        for n in range(3):
            parts = []
            for b in range(4):
                c = 4 * a + b
                if n == 1:
                    plane = stored[c].astype(F32) * scales[c]
                else:
                    plane = (cond if n == 0 else cot)[c]
                parts.append(roll(plane, 32 * b))
            for d in range(G):
                outs[d][n, a] = pick(groups[d], parts)


def edge_kernel(places, *refs):
    msgs, (to_left, to_right, head, tail) = refs[:G], refs[G:]
    lane = lax.broadcasted_iota(jnp.int32, (BY, LANES), 1)
    low = lax.rem(lane, STRIP) < STRIP // 2
    for n in range(3):
        for d in range(G):
            first, second = msgs[d][n, 0], msgs[d][n, 1]
            to_left[n, places[0, d]] = jnp.where(low, first, roll(second, 16))
            to_right[n, places[1, d]] = jnp.where(low, roll(second, -16), first)
            for a in range(2):
                head[n, d, a] = msgs[d][n, a, :HALO]
                tail[n, d, a] = msgs[d][n, a, BY - HALO :]


def unpack(get_brick, get_edge, group, low, put):
    for first, da, db in ((0, 0, 2), (8, 3, 1)):
        ra, rb = get_edge(1, da), get_edge(1, db)
        la, lb = get_edge(0, da), get_edge(0, db)
        for a in range(2):
            if a == 0:
                x = jnp.where(low, ra, roll(lb, 64))
                y = jnp.where(low, roll(rb, 64), la)
            else:
                x = jnp.where(low, roll(ra, -16), roll(lb, 80))
                y = jnp.where(low, roll(rb, 48), roll(la, 16))
            own, other = get_brick(da, a), roll(get_brick(db, a), 64)
            for b in range(4):
                parts = (own, x, other, y)
                whole = pick(group, [parts[(q - b) % 4] for q in range(4)])
                put(first + 4 * a + b, roll(whole, -32 * b))


def solve_kernel(strip, scalars, b0, b1, b2, b3, from_left, from_right, above, above_edge, below, below_edge, *refs):
    nf = 2
    bricks = (b0, b1, b2, b3)
    outs = refs[:G]
    refs = refs[G:]
    xa, xb, xc, rhs, stage_a, stage_b = (refs[nf * j : nf * (j + 1)] for j in range(6))
    kap, kx, ky, kz, diag = refs[6 * nf :]
    zero = jnp.zeros((TILE, LANES), F32)
    lane = lax.broadcasted_iota(jnp.int32, (TILE, LANES), 1)
    group = group_of(TILE, strip[0])
    low = lax.rem(lane, STRIP) < STRIP // 2
    targets = (kap, rhs[0], rhs[1])

    @pl.loop(0, BY // TILE)
    def _(t):
        r = pl.multiple_of(TILE * t, TILE)
        to = pl.multiple_of(TOP + TILE * t, TILE)
        edges = (from_left, from_right)
        for n, dst in enumerate(targets):

            def put(i, val):
                dst[i, pl.ds(to, TILE)] = val

            unpack(
                lambda d, a: bricks[d][n, a, pl.ds(r, TILE)],
                lambda side, d: edges[side][n, d, pl.ds(r, TILE)],
                group,
                low,
                put,
            )

    @pl.loop(0, HALO // TILE)
    def _(t):
        r = pl.multiple_of(TILE * t, TILE)
        for brick, edge, start in ((above, above_edge, TOP - HALO), (below, below_edge, TOP + BY)):
            to = pl.multiple_of(start + TILE * t, TILE)
            for n, dst in enumerate(targets):

                def put(i, val):
                    dst[i, pl.ds(to, TILE)] = val

                unpack(
                    lambda d, a: brick[n, d, a, pl.ds(r, TILE)],
                    lambda side, d: edge[side, n, d, pl.ds(r, TILE)],
                    group,
                    low,
                    put,
                )

    for i in range(NXL):
        for dst in (kap, ky, kz) + tuple(rhs) + tuple(xa) + tuple(xb) + tuple(xc):
            dst[i, 0:TILE] = zero
            dst[i, ROWS - TILE : ROWS] = zero

    @pl.loop(0, ROWS // TILE - 2)
    def _(t):
        r = pl.multiple_of(TILE + TILE * t, TILE)
        now = kap[0, pl.ds(r, TILE)]
        wrapped = roll(now, 64)
        for i in range(NXL):
            after = kap[i + 1, pl.ds(r, TILE)] if i + 1 < NXL else wrapped
            kx[i, pl.ds(r, TILE)] = 4.0 * (now + after)
            ky[i, pl.ds(r, TILE)] = 4.0 * (now + kap[i, pl.ds(r + 1, TILE)])
            kz[i, pl.ds(r, TILE)] = 4.0 * (now + roll(now, -1))
            now = after

    theta_inv = scalars[0, 0]

    @pl.loop(0, ROWS // TILE - 2)
    def _(t):
        r = pl.multiple_of(TILE + TILE * t, TILE)
        before = roll(kx[NXL - 1, pl.ds(r, TILE)], 64)
        for i in range(NXL):
            fx = kx[i, pl.ds(r, TILE)]
            fz = kz[i, pl.ds(r, TILE)]
            total = fx + before + ky[i, pl.ds(r, TILE)] + ky[i, pl.ds(r - 1, TILE)]
            diag[i, pl.ds(r, TILE)] = 1.0 + (total + (fz + roll(fz, 1)))
            before = fx
            for f in range(nf):
                xb[f][i, pl.ds(r, TILE)] = rhs[f][i, pl.ds(r, TILE)] * theta_inv
                xa[f][i, pl.ds(r, TILE)] = zero

    def along_lanes(cur, stage, r):
        for i in range(NXL):
            fz = kz[i, pl.ds(r, TILE)]
            for f in range(nf):
                x = cur[f][i, pl.ds(r, TILE)]
                stage[f][i] = (fz * roll(x, -1) + roll(fz * x, 1)) + rhs[f][i, pl.ds(r, TILE)]

    def advance(alpha, beta, old, cur, new, stage, r):
        now = [cur[f][0, pl.ds(r, TILE)] for f in range(nf)]
        wrapped = [roll(x, 64) for x in now]
        before = [roll(cur[f][NXL - 1, pl.ds(r, TILE)], 64) for f in range(nf)]
        fbefore = roll(kx[NXL - 1, pl.ds(r, TILE)], 64)
        for i in range(NXL):
            fx = kx[i, pl.ds(r, TILE)]
            fy = ky[i, pl.ds(r, TILE)]
            fym = ky[i, pl.ds(r - 1, TILE)]
            centre = (1.0 + alpha) - beta * diag[i, pl.ds(r, TILE)]
            for f in range(nf):
                x = now[f]
                after = cur[f][i + 1, pl.ds(r, TILE)] if i + 1 < NXL else wrapped[f]
                near = fx * after + fbefore * before[f]
                near = near + (fy * cur[f][i, pl.ds(r + 1, TILE)] + fym * cur[f][i, pl.ds(r - 1, TILE)])
                near = near + stage[f][i]
                new[f][i, pl.ds(r, TILE)] = centre * x - alpha * old[f][i, pl.ds(r, TILE)] + beta * near
                before[f] = x
                now[f] = after
            fbefore = fx

    def sweep(k, old, cur, new, span):
        alpha, beta = scalars[k, 0], scalars[k, 1]
        along_lanes(cur, stage_a, span[0])

        @pl.loop(0, span[1] // 2)
        def _(t):
            r = pl.multiple_of(span[0] + 2 * TILE * t, TILE)
            along_lanes(cur, stage_b, r + TILE)
            advance(alpha, beta, old, cur, new, stage_a, r)
            along_lanes(cur, stage_a, r + 2 * TILE)
            advance(alpha, beta, old, cur, new, stage_b, r + TILE)

    def three(k, spans):
        sweep(k, xa, xb, xc, spans[0])
        sweep(k + 1, xb, xc, xa, spans[1])
        sweep(k + 2, xc, xa, xb, spans[2])

    wide = (TILE, ROWS // TILE - 2)
    narrow = (2 * TILE, ROWS // TILE - 4)

    @pl.loop(0, 2)
    def _(m):
        three(1 + 3 * m, (wide,) * 3)

    three(7, (wide, narrow, narrow))

    @pl.loop(0, 2)
    def _(m):
        three(10 + 3 * m, (narrow,) * 3)

    sub = lax.broadcasted_iota(jnp.int32, (TILE, LANES), 0)
    inner = lax.rem(lax.rem(lane - STRIP * strip[0] + 2 * LANES, LANES) + 1, 64)

    def near_edge(width):
        return (inner < width) | ((inner >= 33) & (inner < 33 + width))

    masks = [near_edge(1), near_edge(2), near_edge(4)]

    def main_rows(f, first, row):
        rolled = [roll(xb[f][first + c, pl.ds(row, TILE)], 32 * (c % 4)) for c in range(BX)]
        out = []
        for h in range(2):
            out.append([pick(group, [rolled[4 * a + (q - 2 * h) % 4] for q in range(4)]) for a in range(2)])
        return out

    def side_rows(f, pair, first, row):
        tree = [xb[f][first + c, pl.ds(row, TILE)] for c in range(BX)]
        for level in range(3):
            tree = [
                jnp.where(masks[level], tree[j], roll(tree[j + 1], 1 << level)) for j in range(0, len(tree), 2)
            ]
        ends = roll(tree[0], 1)
        out = []
        for h in range(2):
            d = pair + 2 * h
            down, up = (BX * d + 31) % 32, (BX * d + 8) % 32
            down = roll(xb[f][down % NXL, pl.ds(row, TILE)], 64 * (h + 1 - down // NXL))
            up = roll(xb[f][up % NXL, pl.ds(row, TILE)], 96 + 64 * (h - up // NXL))
            parts = (ends, ends, down, up)
            out.append(pick(group, [parts[(q - 2 * h) % 4] for q in range(4)]))
        return out

    for f in range(nf):
        for pair in range(2):
            first = 8 * pair

            @pl.loop(0, BY // TILE)
            def _(t):
                row = pl.multiple_of(TOP + TILE * t, TILE)
                to = pl.ds(pl.multiple_of(TILE * t, TILE), TILE)
                mains = main_rows(f, first, row)
                sides = side_rows(f, pair, first, row)
                for h in range(2):
                    for a in range(2):
                        outs[pair + 2 * h][f, a, to] = mains[h][a]
                    outs[pair + 2 * h][f, 2, to] = sides[h]

            over = main_rows(f, first, TOP - TILE)
            under = main_rows(f, first, TOP + BY)
            for h in range(2):
                for a in range(2):
                    outs[pair + 2 * h][f, a, BY:MROWS] = jnp.where(
                        sub == 0, pltpu.roll(over[h][a], 1, 0), pltpu.roll(under[h][a], 1, 0)
                    )
                outs[pair + 2 * h][f, 2, BY:MROWS] = zero


def final_kernel(strips, m0, m1, m2, m3, cond, kdown, kup, kover, kunder, kzl, kzr, stored, scales, cot, grad, adjoint, state, residuals, xs, ends, kap):
    msgs = (m0, m1, m2, m3)
    lane = lax.broadcasted_iota(jnp.int32, (TILE, LANES), 1)
    owner = [[group_of(TILE, strips[d] + b) == 0 for b in range(4)] for d in range(G)]

    def choose(parts, b):
        out = parts[0]
        for d in range(1, G):
            out = jnp.where(owner[d][b], parts[d], out)
        return out

    def bricks(f, a, row):
        return [roll(msgs[d][f, a, pl.ds(row, TILE)], -64 * (d // 2)) for d in range(G)]

    for f in range(2):

        @pl.loop(0, BY // TILE)
        def _(t):
            row = pl.multiple_of(TILE * t, TILE)
            to = pl.ds(pl.multiple_of(TILE + TILE * t, TILE), TILE)
            for a in range(2):
                parts = bricks(f, a, row)
                for b in range(4):
                    xs[f, 1 + 4 * a + b, to] = roll(choose(parts, b), -32 * b)
            parts = bricks(f, 2, row)
            for d in range(G):
                ends[f, strips[d], pl.ds(row, TILE)] = parts[d]
            xs[f, 0, to] = roll(choose(parts, 2), -64)
            xs[f, 1 + BX, to] = roll(choose(parts, 3), -96)

        for a in range(2):
            parts = bricks(f, a, BY)
            for b in range(4):
                val = pltpu.roll(roll(choose(parts, b), -32 * b), 7, 0)
                xs[f, 1 + 4 * a + b, 0:TILE] = val
                xs[f, 1 + 4 * a + b, TILE + BY : 2 * TILE + BY] = val
    kap[0, TILE : TILE + BY] = kdown[...]
    kap[1 + BX, TILE : TILE + BY] = kup[...]
    for c in range(BX):
        kap[1 + c, TILE : TILE + BY] = cond[c]
        kap[1 + c, 0:TILE] = jnp.broadcast_to(kover[c : c + 1], (TILE, LANES))
        kap[1 + c, TILE + BY : 2 * TILE + BY] = jnp.broadcast_to(kunder[c : c + 1], (TILE, LANES))

    @pl.loop(0, BY // TILE)
    def _(t):
        r = pl.multiple_of(TILE * t, TILE)
        r8 = pl.multiple_of(TILE * t + TILE, TILE)
        at_r = pl.ds(r, TILE)
        low = [ends[f, 0, at_r] for f in range(2)]
        high = [ends[f, G - 1, at_r] for f in range(2)]
        for c in range(BX):
            k = kap[1 + c, pl.ds(r8, TILE)]
            x = [xs[f, 1 + c, pl.ds(r8, TILE)] for f in range(2)]
            total = [0.0, 0.0]
            product = 0.0

            def sides():
                for at in (c, c + 2):
                    yield kap[at, pl.ds(r8, TILE)], [xs[f, at, pl.ds(r8, TILE)] for f in range(2)]
                for off in (-1, 1):
                    yield kap[1 + c, pl.ds(r8 + off, TILE)], [xs[f, 1 + c, pl.ds(r8 + off, TILE)] for f in range(2)]
                yield (
                    jnp.where(lane == 0, kzl[c, at_r], roll(k, 1)),
                    [jnp.where(lane == 0, roll(low[f], -c), roll(x[f], 1)) for f in range(2)],
                )
                yield (
                    jnp.where(lane == LANES - 1, kzr[c, at_r], roll(k, -1)),
                    [jnp.where(lane == LANES - 1, roll(high[f], 126 - c), roll(x[f], -1)) for f in range(2)],
                )

            for kn, xn in sides():
                face = k + kn
                differ = [x[f] - xn[f] for f in range(2)]
                product = product + differ[0] * differ[1]
                for f in range(2):
                    total[f] = total[f] + face * differ[f]
            grad[c, at_r] = (-0.5 * TIME_STEP) * product
            state[c, at_r] = x[0]
            adjoint[c, at_r] = x[1]
            previous = stored[c, pl.ds(r, TILE)].astype(F32) * scales[c, at_r]
            residuals[0, c, at_r] = previous - (x[0] + (0.5 * TIME_STEP) * total[0])
            residuals[1, c, at_r] = cot[c, at_r] - (x[1] + (0.5 * TIME_STEP) * total[1])


def call(kernel, outs, smem, vmem, scratch=()):
    vm = pl.BlockSpec(memory_space=pltpu.VMEM)
    sm = pl.BlockSpec(memory_space=pltpu.SMEM)
    return pl.pallas_call(
        kernel,
        out_shape=[jax.ShapeDtypeStruct(shape, F32) for shape in outs],
        in_specs=[sm] * len(smem) + [vm] * len(vmem),
        out_specs=[vm] * len(outs),
        scratch_shapes=[pltpu.VMEM(shape, F32) for shape in scratch],
        compiler_params=pltpu.CompilerParams(vmem_limit_bytes=48 * 1024 * 1024),
    )(*smem, *vmem)


def shifted(x, axis, by):
    count = lax.axis_size(axis)
    return lax.ppermute(x, axis, [(i, (i + by) % count) for i in range(count)])


def around(x, by):
    order = [2 * g for g in range(G)] + [2 * g + 1 for g in reversed(range(G))]
    pairs = [(order[i], order[(i + by) % len(order)]) for i in range(len(order))]
    return lax.ppermute(x, ("gx", "pa"), pairs)


def chebyshev_scalars(upper):
    theta = 0.5 * (upper + 1.0)
    delta = 0.5 * (upper - 1.0)
    sigma = theta / delta
    rho = 1.0 / sigma
    rows = [(1.0 / theta, 0.0 * theta)]
    for _ in range(1, CHEB):
        rho_next = 1.0 / (2.0 * sigma - rho)
        rows.append((rho_next * rho, 2.0 * rho_next / delta))
        rho = rho_next
    return jnp.stack([jnp.stack(row) for row in rows])


def redistributed(conductivity, stored_state, row_scales, cotangent, upper_bound):
    g = lax.axis_index("gx")
    pa = lax.axis_index("pa")

    def strip_of(device):
        return jnp.where(pa == 0, device, G - 1 - device)

    steps = jnp.arange(G, dtype=jnp.int32)
    ahead = lax.rem(g + steps, G)
    behind = lax.rem(g - steps + G, G)
    scalars = chebyshev_scalars(upper_bound[0])
    stored = shifted(stored_state, "pa", 1)
    scales = row_scales[:, :, None]

    kdown = shifted(conductivity[BX - 1], "gx", 1)
    kup = shifted(conductivity[0], "gx", -1)
    kover = shifted(conductivity[:, BY - 1], "gy", 1)
    kunder = shifted(conductivity[:, 0], "gy", -1)
    kends = shifted(jnp.stack((conductivity[:, :, BZ - 1], conductivity[:, :, 0])), "pa", 1)

    brick = (3, 2, BY, LANES)
    parts = call(pack_kernel, [brick] * G, [strip_of(ahead)], [conductivity, stored, scales, cotangent])
    parts = [parts[0]] + [shifted(parts[d], "gx", d) for d in range(1, G)]

    strip = strip_of(g)
    left_g = jnp.where(pa == 0, jnp.maximum(g - 1, 0), jnp.minimum(g + 1, G - 1))
    right_g = jnp.where(pa == 0, jnp.minimum(g + 1, G - 1), jnp.maximum(g - 1, 0))
    places = lax.rem(jnp.stack((left_g - g + steps, right_g - g + steps)) + G, G)
    edge = (3, G, BY, LANES)
    rim = (3, G, 2, HALO, LANES)
    to_left, to_right, head, tail = call(edge_kernel, [edge, edge, rim, rim], [places], parts)
    from_right, from_left = around(to_left, -1), around(to_right, 1)
    below, above = shifted(head, "gy", -1), shifted(tail, "gy", 1)
    edges = jnp.stack((from_left, from_right))
    below_edge = shifted(edges[:, :, :, :HALO], "gy", -1)
    above_edge = shifted(edges[:, :, :, BY - HALO :], "gy", 1)
    field = (NXL, ROWS, LANES)
    solved = call(
        solve_kernel,
        [(2, 3, MROWS, LANES)] * G,
        [strip[None], scalars],
        [*parts, from_left, from_right, above, above_edge, below, below_edge],
        [field] * 8 + [(NXL, TILE, LANES)] * 4 + [field] * 5,
    )
    solved = [solved[0]] + [shifted(solved[d], "gx", d) for d in range(1, G)]
    out = (BX, BY, LANES)
    padded = (BX + 2, BY + 16, LANES)
    return call(
        final_kernel,
        [out, out, out, (2,) + out],
        [strip_of(behind)],
        [*solved, conductivity, kdown, kup, kover, kunder, kends[0][:, :, None], kends[1][:, :, None], stored, scales, cotangent],
        [(2,) + padded, (2, G, BY, LANES), padded],
    )


def body(conductivity, stored_state, row_scales, cotangent, upper_bound):
    strips_fit = (
        lax.axis_size("gx") == G
        and lax.axis_size("pa") == 2
        and conductivity.shape == (BX, BY, BZ)
    )
    run = redistributed if strips_fit else stepwise
    return tuple(run(conductivity, stored_state, row_scales, cotangent, upper_bound))


def solution(mesh):
    return jax.shard_map(
        body,
        mesh=mesh,
        in_specs=(
            P("gx", "gy", "pa"),
            P("gx", "gy", "pa"),
            P("gx", "gy"),
            P("gx", "gy", "pa"),
            P(),
        ),
        out_specs=(
            P("gx", "gy", "pa"),
            P("gx", "gy", "pa"),
            P("gx", "gy", "pa"),
            P(None, "gx", "gy", "pa"),
        ),
        check_vma=False,
    )
```

```python
import functools

import jax
import jax.numpy as jnp
from jax import lax
from jax.experimental import pallas as pl
from jax.experimental.pallas import tpu as pltpu
from jax.sharding import PartitionSpec as P

CHEB = 16
LANES = 128
HALO = CHEB
TIME_STEP = 8.0
F32 = jnp.float32


def with_halo(cells, sides, width):
    for axis, dim in sides:
        count = lax.axis_size(axis)
        head = lax.slice_in_dim(cells, 0, width, axis=dim)
        tail = lax.slice_in_dim(cells, cells.shape[dim] - width, cells.shape[dim], axis=dim)
        cells = jnp.concatenate(
            [
                lax.ppermute(tail, axis, [(i, (i + 1) % count) for i in range(count)]),
                cells,
                lax.ppermute(head, axis, [((i + 1) % count, i) for i in range(count)]),
            ],
            axis=dim,
        )
    return cells


def region(arr, spatial, offset):
    extent = arr.shape[-3:]
    window = [slice(1, length - 1) for length in extent]
    window[spatial] = slice(offset, extent[spatial] - 2 + offset)
    leading = [slice(None)] * (arr.ndim - 3)
    return arr[tuple(leading + window)]


def apply_operator(padded, kpad):
    centre = region(padded, 0, 1)
    kcentre = region(kpad, 0, 1)
    summed = jnp.zeros_like(centre)
    for spatial in range(3):
        for offset in (0, 2):
            summed = summed + 0.5 * (kcentre + region(kpad, spatial, offset)) * (
                centre - region(padded, spatial, offset)
            )
    return centre + TIME_STEP * summed


def stepwise(conductivity, stored_state, row_scales, cotangent, upper_bound):
    upper = upper_bound[0]
    kpad = with_halo(conductivity, (("gx", 0), ("gy", 1), ("pa", 2)), 1)
    count = lax.axis_size("pa")
    partner = lax.ppermute(stored_state, "pa", [(i, (i + count // 2) % count) for i in range(count)])
    previous = partner.astype(F32) * row_scales[:, :, None]
    rhs = jnp.stack((previous, cotangent))
    theta = 0.5 * (upper + 1.0)
    delta = 0.5 * (upper - 1.0)
    sigma = theta / delta
    sides = (("gx", 1), ("gy", 2), ("pa", 3))

    def sweep(step, carry):
        solved, residual, direction, rho = carry
        padded = with_halo(direction, sides, 1)
        solved = solved + direction
        residual = residual - apply_operator(padded, kpad)
        rho_next = 1.0 / (2.0 * sigma - rho)
        direction = rho_next * rho * direction + 2.0 * rho_next / delta * residual
        return (solved, residual, direction, rho_next)

    start = (jnp.zeros_like(rhs), rhs, rhs / theta, 1.0 / sigma)
    solved, residual, _, _ = lax.fori_loop(0, CHEB, sweep, start)
    pair = with_halo(solved, sides, 1)
    centre = region(pair, 0, 1)
    summed = jnp.zeros_like(solved[0])
    for spatial in range(3):
        for offset in (0, 2):
            differ = centre - region(pair, spatial, offset)
            summed = summed + differ[0] * differ[1]
    return (-0.5 * TIME_STEP * summed, solved[1], solved[0], residual)


G = 4
BX = 8
BY = 128
BZ = 128
STRIP = BZ // G
TOP = 8 + HALO
ROWS = BY + 2 * TOP
MROWS = BY + 8
TILE = 8

BLOCK = (0, 3, 2, 1)
PLANES = BX


def roll(x, by):
    by %= LANES
    return pltpu.roll(x, by, 1) if by else x


def lanes_of(rows, strip):
    lane = lax.broadcasted_iota(jnp.int32, (rows, LANES), 1)
    return lax.rem(lane // STRIP - strip + 2 * G, G), lax.rem(lane, STRIP)


def pick(group, parts):
    out = parts[0]
    for b in range(1, G):
        out = jnp.where(group == b, parts[b], out)
    return out


def parity_order(transposed):
    src = lax.broadcasted_iota(jnp.int32, (LANES, LANES), 1 if transposed else 0)
    dst = lax.broadcasted_iota(jnp.int32, (LANES, LANES), 0 if transposed else 1)
    within = lax.rem(src, STRIP)
    place = src - within + 16 * lax.rem(within, 2) + within // 2
    return jnp.where(place == dst, 1.0, 0.0).astype(F32)


def reorder(x, order):
    return jnp.dot(x, order, precision=lax.Precision.HIGHEST, preferred_element_type=F32)


def pack_kernel(names, strips, *refs):
    ins, outs = refs[: len(refs) - G], refs[len(refs) - G :]
    order = parity_order(False)
    groups = [lanes_of(BY, strips[d])[0] for d in range(G)]
    for a in range(2):
        for n, name in enumerate(names):
            parts = []
            for b in range(4):
                c = 4 * a + b
                if name == "previous":
                    plane = ins[n][c].astype(F32) * ins[n + 1][c]
                else:
                    plane = ins[n][c]
                parts.append(roll(reorder(plane, order), 32 * b))
            for d in range(G):
                outs[d][n, a] = pick(groups[d], parts)


def edge_kernel(places, *refs):
    msgs, (to_left, to_right, head, tail) = refs[:G], refs[G:]
    lane = lax.broadcasted_iota(jnp.int32, (BY, LANES), 1)
    low = lax.rem(lane, 16) < 8
    for n in range(msgs[0].shape[0]):
        for d in range(G):
            first, second = msgs[d][n, 0], msgs[d][n, 1]
            to_left[n, places[0, d]] = jnp.where(low, first, roll(second, 8))
            to_right[n, places[1, d]] = jnp.where(low, roll(second, -8), first)
            for a in range(2):
                head[n, d, a] = msgs[d][n, a, :HALO]
                tail[n, d, a] = msgs[d][n, a, BY - HALO :]


def unpack(get_brick, get_edge, group, within, put):
    by_block = [BLOCK.index(q) for q in range(G)]
    edges = [[get_edge(side, d) for d in by_block] for side in range(2)]
    for a in range(2):
        far = 24 if a else 16
        own = [roll(get_brick(by_block[q], a), 32 * q) for q in range(G)]
        below = [roll(edges[0][q], 32 * q + far) for q in range(G)]
        above = [roll(edges[1][q], 32 * q - far) for q in range(G)]
        even = [
            jnp.where(within < 16, own[q], jnp.where(within < 24, above[q], below[(q + 1) % G])) for q in range(G)
        ]
        odd = [
            jnp.where(within < 8, above[(q - 1) % G], jnp.where(within < 16, below[q], own[q])) for q in range(G)
        ]
        for b in range(4):
            for e, parts in enumerate((even, odd)):
                whole = pick(group, [parts[(q - b) % G] for q in range(G)])
                put(4 * a + b, e, roll(whole, -32 * b - 16 * e))


def solve_kernel(nf, where, strip, scalars, *refs):
    stacks = []
    for _ in range(1 + max(stack for stack, _ in where)):
        stacks.append((refs[:G],) + tuple(refs[G : G + 6]))
        refs = refs[G + 6 :]
    outs = refs[:G]
    refs = refs[G:]
    xa, xb, xc, rhs, stage_a, stage_b = (refs[nf * j : nf * (j + 1)] for j in range(6))
    kap, kx, ky, kin, kout, diag = refs[6 * nf :]
    zero = jnp.zeros((TILE, LANES), F32)
    group, within = lanes_of(TILE, strip[0])
    targets = (kap,) + tuple(rhs)

    def put_at(dst, to):
        def put(i, e, val):
            dst[i, e, pl.ds(to, TILE)] = val

        return put

    @pl.loop(0, BY // TILE)
    def _(t):
        r = pl.multiple_of(TILE * t, TILE)
        to = pl.multiple_of(TOP + TILE * t, TILE)
        for dst, (stack, n) in zip(targets, where):
            bricks, from_left, from_right = stacks[stack][:3]
            sides = (from_left, from_right)
            unpack(
                lambda d, a: bricks[d][n, a, pl.ds(r, TILE)],
                lambda side, d: sides[side][n, d, pl.ds(r, TILE)],
                group,
                within,
                put_at(dst, to),
            )

    @pl.loop(0, HALO // TILE)
    def _(t):
        r = pl.multiple_of(TILE * t, TILE)
        for dst, (stack, n) in zip(targets, where):
            above, above_edge, below, below_edge = stacks[stack][3:]
            for brick, edge, start in ((above, above_edge, TOP - HALO), (below, below_edge, TOP + BY)):
                unpack(
                    lambda d, a: brick[n, d, a, pl.ds(r, TILE)],
                    lambda side, d: edge[side, n, d, pl.ds(r, TILE)],
                    group,
                    within,
                    put_at(dst, pl.multiple_of(start + TILE * t, TILE)),
                )

    for i in range(PLANES):
        for e in range(2):
            for dst in (kap, ky) + tuple(rhs) + tuple(xa) + tuple(xb) + tuple(xc):
                dst[i, e, 0:TILE] = zero
                dst[i, e, ROWS - TILE : ROWS] = zero
        for dst in (kin, kout):
            dst[i, 0:TILE] = zero
            dst[i, ROWS - TILE : ROWS] = zero

    @pl.loop(0, ROWS // TILE - 2)
    def _(t):
        r = pl.multiple_of(TILE + TILE * t, TILE)
        now = [kap[0, e, pl.ds(r, TILE)] for e in range(2)]
        wrapped = [roll(k, -32) for k in now]
        for i in range(PLANES):
            after = [kap[i + 1, e, pl.ds(r, TILE)] for e in range(2)] if i + 1 < PLANES else wrapped
            for e in range(2):
                kx[i, e, pl.ds(r, TILE)] = 4.0 * (now[e] + after[e])
                ky[i, e, pl.ds(r, TILE)] = 4.0 * (now[e] + kap[i, e, pl.ds(r + 1, TILE)])
            kin[i, pl.ds(r, TILE)] = 4.0 * (now[0] + now[1])
            kout[i, pl.ds(r, TILE)] = 4.0 * (now[1] + roll(now[0], -1))
            now = after

    theta_inv = scalars[0, 0]

    @pl.loop(0, ROWS // TILE - 2)
    def _(t):
        r = pl.multiple_of(TILE + TILE * t, TILE)
        before = [roll(kx[PLANES - 1, e, pl.ds(r, TILE)], 32) for e in range(2)]
        for i in range(PLANES):
            inner = kin[i, pl.ds(r, TILE)]
            outer = kout[i, pl.ds(r, TILE)]
            along = (inner + roll(outer, 1), inner + outer)
            for e in range(2):
                fx = kx[i, e, pl.ds(r, TILE)]
                total = fx + before[e] + ky[i, e, pl.ds(r, TILE)] + ky[i, e, pl.ds(r - 1, TILE)]
                diag[i, e, pl.ds(r, TILE)] = 1.0 + (total + along[e])
                before[e] = fx
                for f in range(nf):
                    xb[f][i, e, pl.ds(r, TILE)] = rhs[f][i, e, pl.ds(r, TILE)] * theta_inv
                    xa[f][i, e, pl.ds(r, TILE)] = zero

    def along_lanes(cur, stage, r):
        for i in range(PLANES):
            inner = kin[i, pl.ds(r, TILE)]
            outer = kout[i, pl.ds(r, TILE)]
            for f in range(nf):
                even, odd = (cur[f][i, e, pl.ds(r, TILE)] for e in range(2))
                stage[f][i, 0] = (inner * odd + roll(outer * odd, 1)) + rhs[f][i, 0, pl.ds(r, TILE)]
                stage[f][i, 1] = (inner * even + outer * roll(even, -1)) + rhs[f][i, 1, pl.ds(r, TILE)]

    def advance(alpha, beta, old, cur, new, stage, r):
        for e in range(2):
            now = [cur[f][0, e, pl.ds(r, TILE)] for f in range(nf)]
            wrapped = [roll(x, -32) for x in now]
            before = [roll(cur[f][PLANES - 1, e, pl.ds(r, TILE)], 32) for f in range(nf)]
            fbefore = roll(kx[PLANES - 1, e, pl.ds(r, TILE)], 32)
            for i in range(PLANES):
                fx = kx[i, e, pl.ds(r, TILE)]
                fy = ky[i, e, pl.ds(r, TILE)]
                fym = ky[i, e, pl.ds(r - 1, TILE)]
                centre = (1.0 + alpha) - beta * diag[i, e, pl.ds(r, TILE)]
                for f in range(nf):
                    x = now[f]
                    after = cur[f][i + 1, e, pl.ds(r, TILE)] if i + 1 < PLANES else wrapped[f]
                    near = fx * after + fbefore * before[f]
                    near = near + (fy * cur[f][i, e, pl.ds(r + 1, TILE)] + fym * cur[f][i, e, pl.ds(r - 1, TILE)])
                    near = near + stage[f][i, e]
                    new[f][i, e, pl.ds(r, TILE)] = centre * x - alpha * old[f][i, e, pl.ds(r, TILE)] + beta * near
                    before[f] = x
                    now[f] = after
                fbefore = fx

    def sweep(k, old, cur, new, span):
        alpha, beta = scalars[k, 0], scalars[k, 1]
        along_lanes(cur, stage_a, span[0])

        @pl.loop(0, span[1] // 2)
        def _(t):
            r = pl.multiple_of(span[0] + 2 * TILE * t, TILE)
            along_lanes(cur, stage_b, r + TILE)
            advance(alpha, beta, old, cur, new, stage_a, r)
            along_lanes(cur, stage_a, r + 2 * TILE)
            advance(alpha, beta, old, cur, new, stage_b, r + TILE)

    def three(k, spans):
        sweep(k, xa, xb, xc, spans[0])
        sweep(k + 1, xb, xc, xa, spans[1])
        sweep(k + 2, xc, xa, xb, spans[2])

    wide = (TILE, ROWS // TILE - 2)
    narrow = (2 * TILE, ROWS // TILE - 4)

    @pl.loop(0, 2)
    def _(m):
        three(1 + 3 * m, (wide,) * 3)

    three(7, (wide, narrow, narrow))

    @pl.loop(0, 2)
    def _(m):
        three(10 + 3 * m, (narrow,) * 3)

    def near_edge(width):
        below = lax.rem(within + 1, STRIP) < width
        return below | ((within >= 16) & (within < 16 + width))

    masks = [near_edge(1), near_edge(2), near_edge(4)]

    def pieces(f, row):
        out = []
        for i in range(PLANES):
            even, odd = (xb[f][i, e, pl.ds(row, TILE)] for e in range(2))
            out.append(jnp.where(within < 16, even, roll(odd, 16)))
        return out

    def main_rows(parts):
        parts = [roll(parts[i], 32 * (i % 4)) for i in range(PLANES)]
        return [[pick(group, [parts[4 * a + (q - d) % G] for q in range(G)]) for a in range(2)] for d in range(G)]

    def side_rows(f, parts, row):
        tree = [
            jnp.where(within == 31, xb[f][i, 1, pl.ds(row, TILE)], xb[f][i, 0, pl.ds(row, TILE)])
            for i in range(PLANES)
        ]
        for level in range(3):
            tree = [
                jnp.where(masks[level], tree[j], roll(tree[j + 1], 1 << level)) for j in range(0, len(tree), 2)
            ]
        ends = roll(tree[0], 1)
        groups = (ends, ends, roll(parts[PLANES - 1], 96), roll(parts[0], 64))
        return [pick(group, [groups[(q - d) % G] for q in range(G)]) for d in range(G)]

    @pl.loop(0, BY // TILE)
    def _(t):
        row = pl.multiple_of(TOP + TILE * t, TILE)
        to = pl.ds(pl.multiple_of(TILE * t, TILE), TILE)
        for f in range(nf):
            parts = pieces(f, row)
            mains, sides = main_rows(parts), side_rows(f, parts, row)
            for d in range(G):
                for a in range(2):
                    outs[d][f, a, to] = mains[d][a]
                outs[d][f, 2, to] = sides[d]

    sub = lax.broadcasted_iota(jnp.int32, (TILE, LANES), 0)
    for f in range(nf):
        over, under = main_rows(pieces(f, TOP - TILE)), main_rows(pieces(f, TOP + BY))
        for d in range(G):
            for a in range(2):
                outs[d][f, a, BY:MROWS] = jnp.where(
                    sub == 0, pltpu.roll(over[d][a], 1, 0), pltpu.roll(under[d][a], 1, 0)
                )
            outs[d][f, 2, BY:MROWS] = zero


def final_kernel(nstacks, strips, *refs):
    stacks = [refs[G * j : G * (j + 1)] for j in range(nstacks)]
    refs = refs[G * nstacks :]
    cond, kdown, kup, kover, kunder, kzl, kzr, stored, scales, cot = refs[:10]
    grad, adjoint, state, residuals, xs, ends, kap = refs[10:]
    fields = [(stack, n) for stack in stacks for n in range(2 // nstacks)]
    order = parity_order(True)
    wide = 4 * TILE

    def owners(rows):
        return [lanes_of(rows, strips[d])[0] for d in range(G)]

    def choose(owner, parts, b):
        out = parts[0]
        for d in range(1, G):
            out = jnp.where(owner[d] == b, parts[d], out)
        return out

    def bricks(f, a, row, rows):
        msgs, n = fields[f]
        return [roll(msgs[d][n, a, pl.ds(row, rows)], -32 * d) for d in range(G)]

    @pl.loop(0, BY // wide)
    def _(t):
        row = pl.multiple_of(wide * t, wide)
        to = pl.ds(pl.multiple_of(TILE + wide * t, TILE), wide)
        owner = owners(wide)
        for f in range(2):
            for a in range(2):
                parts = bricks(f, a, row, wide)
                for b in range(4):
                    xs[f, 1 + 4 * a + b, to] = reorder(roll(choose(owner, parts, b), -32 * b), order)
            parts = bricks(f, 2, row, wide)
            for d in range(G):
                ends[f, strips[d], pl.ds(row, wide)] = parts[d]
            xs[f, 0, to] = reorder(roll(choose(owner, parts, 2), -64), order)
            xs[f, 1 + BX, to] = reorder(roll(choose(owner, parts, 3), -96), order)

    owner = owners(TILE)
    for f in range(2):
        for a in range(2):
            parts = bricks(f, a, BY, TILE)
            for b in range(4):
                val = pltpu.roll(reorder(roll(choose(owner, parts, b), -32 * b), order), 7, 0)
                xs[f, 1 + 4 * a + b, 0:TILE] = val
                xs[f, 1 + 4 * a + b, TILE + BY : 2 * TILE + BY] = val
    kap[0, TILE : TILE + BY] = kdown[...]
    kap[1 + BX, TILE : TILE + BY] = kup[...]
    for c in range(BX):
        kap[1 + c, TILE : TILE + BY] = cond[c]
        kap[1 + c, 0:TILE] = jnp.broadcast_to(kover[c : c + 1], (TILE, LANES))
        kap[1 + c, TILE + BY : 2 * TILE + BY] = jnp.broadcast_to(kunder[c : c + 1], (TILE, LANES))
    lane = lax.broadcasted_iota(jnp.int32, (TILE, LANES), 1)

    @pl.loop(0, BY // TILE)
    def _(t):
        r = pl.multiple_of(TILE * t, TILE)
        r8 = pl.multiple_of(TILE * t + TILE, TILE)
        at_r = pl.ds(r, TILE)
        low = [ends[f, 0, at_r] for f in range(2)]
        high = [ends[f, G - 1, at_r] for f in range(2)]
        for c in range(BX):
            k = kap[1 + c, pl.ds(r8, TILE)]
            x = [xs[f, 1 + c, pl.ds(r8, TILE)] for f in range(2)]
            total = [0.0, 0.0]
            product = 0.0

            def sides():
                for at in (c, c + 2):
                    yield kap[at, pl.ds(r8, TILE)], [xs[f, at, pl.ds(r8, TILE)] for f in range(2)]
                for off in (-1, 1):
                    yield kap[1 + c, pl.ds(r8 + off, TILE)], [xs[f, 1 + c, pl.ds(r8 + off, TILE)] for f in range(2)]
                yield (
                    jnp.where(lane == 0, kzl[c, at_r], roll(k, 1)),
                    [jnp.where(lane == 0, roll(low[f], -c), roll(x[f], 1)) for f in range(2)],
                )
                yield (
                    jnp.where(lane == LANES - 1, kzr[c, at_r], roll(k, -1)),
                    [jnp.where(lane == LANES - 1, roll(high[f], 14 - c), roll(x[f], -1)) for f in range(2)],
                )

            for kn, xn in sides():
                face = k + kn
                differ = [x[f] - xn[f] for f in range(2)]
                product = product + differ[0] * differ[1]
                for f in range(2):
                    total[f] = total[f] + face * differ[f]
            grad[c, at_r] = (-0.5 * TIME_STEP) * product
            state[c, at_r] = x[0]
            adjoint[c, at_r] = x[1]
            previous = stored[c, pl.ds(r, TILE)].astype(F32) * scales[c, at_r]
            residuals[0, c, at_r] = previous - (x[0] + (0.5 * TIME_STEP) * total[0])
            residuals[1, c, at_r] = cot[c, at_r] - (x[1] + (0.5 * TIME_STEP) * total[1])


def call(kernel, outs, smem, vmem, scratch=()):
    vm = pl.BlockSpec(memory_space=pltpu.VMEM)
    sm = pl.BlockSpec(memory_space=pltpu.SMEM)
    return pl.pallas_call(
        kernel,
        out_shape=[jax.ShapeDtypeStruct(shape, F32) for shape in outs],
        in_specs=[sm] * len(smem) + [vm] * len(vmem),
        out_specs=[vm] * len(outs),
        scratch_shapes=[pltpu.VMEM(shape, F32) for shape in scratch],
        compiler_params=pltpu.CompilerParams(vmem_limit_bytes=48 * 1024 * 1024),
    )(*smem, *vmem)


def shifted(x, axis, by):
    count = lax.axis_size(axis)
    return lax.ppermute(x, axis, [(i, (i + by) % count) for i in range(count)])


def around(x, by):
    order = [2 * g for g in range(G)] + [2 * g + 1 for g in reversed(range(G))]
    pairs = [(order[i], order[(i + by) % len(order)]) for i in range(len(order))]
    return lax.ppermute(x, ("gx", "pa"), pairs)


def chebyshev_scalars(upper):
    theta = 0.5 * (upper + 1.0)
    delta = 0.5 * (upper - 1.0)
    sigma = theta / delta
    rho = 1.0 / sigma
    rows = [(1.0 / theta, 0.0 * theta)]
    for _ in range(1, CHEB):
        rho_next = 1.0 / (2.0 * sigma - rho)
        rows.append((rho_next * rho, 2.0 * rho_next / delta))
        rho = rho_next
    return jnp.stack([jnp.stack(row) for row in rows])


def redistributed(conductivity, stored_state, row_scales, cotangent, upper_bound):
    g = lax.axis_index("gx")
    pa = lax.axis_index("pa")

    def strip_of(device):
        return jnp.where(pa == 0, device, G - 1 - device)

    steps = jnp.arange(G, dtype=jnp.int32)
    ahead = lax.rem(g + steps, G)
    behind = lax.rem(g - steps + G, G)
    scalars = chebyshev_scalars(upper_bound[0])
    stored = shifted(stored_state, "pa", 1)
    scales = row_scales[:, :, None]

    kdown = shifted(conductivity[BX - 1], "gx", 1)
    kup = shifted(conductivity[0], "gx", -1)
    kover = shifted(conductivity[:, BY - 1], "gy", 1)
    kunder = shifted(conductivity[:, 0], "gy", -1)
    kends = shifted(jnp.stack((conductivity[:, :, BZ - 1], conductivity[:, :, 0])), "pa", 1)

    strip = strip_of(g)
    left_g = jnp.where(pa == 0, jnp.maximum(g - 1, 0), jnp.minimum(g + 1, G - 1))
    right_g = jnp.where(pa == 0, jnp.minimum(g + 1, G - 1), jnp.maximum(g - 1, 0))
    places = lax.rem(jnp.stack((left_g - g + steps, right_g - g + steps)) + G, G)

    def strips(names, arrays):
        count = len(names)
        pack = functools.partial(pack_kernel, names)
        parts = call(pack, [(count, 2, BY, LANES)] * G, [strip_of(ahead)], arrays)
        parts = [parts[0]] + [shifted(parts[d], "gx", d) for d in range(1, G)]
        edge = (count, G, BY, LANES)
        rim = (count, G, 2, HALO, LANES)
        to_left, to_right, head, tail = call(edge_kernel, [edge, edge, rim, rim], [places], parts)
        from_right, from_left = around(to_left, -1), around(to_right, 1)
        below, above = shifted(head, "gy", -1), shifted(tail, "gy", 1)
        edges = jnp.stack((from_left, from_right))
        below_edge = shifted(edges[:, :, :, :HALO], "gy", -1)
        above_edge = shifted(edges[:, :, :, BY - HALO :], "gy", 1)
        return [*parts, from_left, from_right, above, above_edge, below, below_edge]

    def solve(where, stacks):
        nf = len(where) - 1
        line = (PLANES, 2, ROWS, LANES)
        solved = call(
            functools.partial(solve_kernel, nf, where),
            [(nf, 3, MROWS, LANES)] * G,
            [strip[None], scalars],
            sum(stacks, []),
            [line] * (4 * nf)
            + [(PLANES, 2, TILE, LANES)] * (2 * nf)
            + [line] * 3
            + [(PLANES, ROWS, LANES)] * 2
            + [line],
        )
        return [solved[0]] + [shifted(solved[d], "gx", d) for d in range(1, G)]

    everything = strips(("conductivity", "cotangent", "previous"), [conductivity, cotangent, stored, scales])
    solved = solve(((0, 0), (0, 2), (0, 1)), [everything])
    out = (BX, BY, LANES)
    padded = (BX + 2, BY + 16, LANES)
    return call(
        functools.partial(final_kernel, 1),
        [out, out, out, (2,) + out],
        [strip_of(behind)],
        [*solved, conductivity, kdown, kup, kover, kunder, kends[0][:, :, None], kends[1][:, :, None], stored, scales, cotangent],
        [(2,) + padded, (2, G, BY, LANES), padded],
    )


def body(conductivity, stored_state, row_scales, cotangent, upper_bound):
    strips_fit = (
        lax.axis_size("gx") == G
        and lax.axis_size("pa") == 2
        and conductivity.shape == (BX, BY, BZ)
    )
    run = redistributed if strips_fit else stepwise
    return tuple(run(conductivity, stored_state, row_scales, cotangent, upper_bound))


def solution(mesh):
    return jax.shard_map(
        body,
        mesh=mesh,
        in_specs=(
            P("gx", "gy", "pa"),
            P("gx", "gy", "pa"),
            P("gx", "gy"),
            P("gx", "gy", "pa"),
            P(),
        ),
        out_specs=(
            P("gx", "gy", "pa"),
            P("gx", "gy", "pa"),
            P("gx", "gy", "pa"),
            P(None, "gx", "gy", "pa"),
        ),
        check_vma=False,
    )
```

```python
import functools

import jax
import jax.numpy as jnp
from jax import lax
from jax.experimental import pallas as pl
from jax.experimental.pallas import tpu as pltpu
from jax.sharding import PartitionSpec as P

CHEB = 16
LANES = 128
HALO = CHEB
TIME_STEP = 8.0
F32 = jnp.float32


def with_halo(cells, sides, width):
    for axis, dim in sides:
        count = lax.axis_size(axis)
        head = lax.slice_in_dim(cells, 0, width, axis=dim)
        tail = lax.slice_in_dim(cells, cells.shape[dim] - width, cells.shape[dim], axis=dim)
        cells = jnp.concatenate(
            [
                lax.ppermute(tail, axis, [(i, (i + 1) % count) for i in range(count)]),
                cells,
                lax.ppermute(head, axis, [((i + 1) % count, i) for i in range(count)]),
            ],
            axis=dim,
        )
    return cells


def region(arr, spatial, offset):
    extent = arr.shape[-3:]
    window = [slice(1, length - 1) for length in extent]
    window[spatial] = slice(offset, extent[spatial] - 2 + offset)
    leading = [slice(None)] * (arr.ndim - 3)
    return arr[tuple(leading + window)]


def apply_operator(padded, kpad):
    centre = region(padded, 0, 1)
    kcentre = region(kpad, 0, 1)
    summed = jnp.zeros_like(centre)
    for spatial in range(3):
        for offset in (0, 2):
            summed = summed + 0.5 * (kcentre + region(kpad, spatial, offset)) * (
                centre - region(padded, spatial, offset)
            )
    return centre + TIME_STEP * summed


def stepwise(conductivity, stored_state, row_scales, cotangent, upper_bound):
    upper = upper_bound[0]
    kpad = with_halo(conductivity, (("gx", 0), ("gy", 1), ("pa", 2)), 1)
    count = lax.axis_size("pa")
    partner = lax.ppermute(stored_state, "pa", [(i, (i + count // 2) % count) for i in range(count)])
    previous = partner.astype(F32) * row_scales[:, :, None]
    rhs = jnp.stack((previous, cotangent))
    theta = 0.5 * (upper + 1.0)
    delta = 0.5 * (upper - 1.0)
    sigma = theta / delta
    sides = (("gx", 1), ("gy", 2), ("pa", 3))

    def sweep(step, carry):
        solved, residual, direction, rho = carry
        padded = with_halo(direction, sides, 1)
        solved = solved + direction
        residual = residual - apply_operator(padded, kpad)
        rho_next = 1.0 / (2.0 * sigma - rho)
        direction = rho_next * rho * direction + 2.0 * rho_next / delta * residual
        return (solved, residual, direction, rho_next)

    start = (jnp.zeros_like(rhs), rhs, rhs / theta, 1.0 / sigma)
    solved, residual, _, _ = lax.fori_loop(0, CHEB, sweep, start)
    pair = with_halo(solved, sides, 1)
    centre = region(pair, 0, 1)
    summed = jnp.zeros_like(solved[0])
    for spatial in range(3):
        for offset in (0, 2):
            differ = centre - region(pair, spatial, offset)
            summed = summed + differ[0] * differ[1]
    return (-0.5 * TIME_STEP * summed, solved[1], solved[0], residual)


G = 4
BX = 8
BY = 128
BZ = 128
STRIP = BZ // G
TOP = 8 + HALO
ROWS = BY + 2 * TOP
MROWS = BY + 8
TILE = 8
CHUNK = 32

BLOCK = (0, 3, 2, 1)
PLANES = BX


def roll(x, by):
    by %= LANES
    return pltpu.roll(x, by, 1) if by else x


def lanes_of(rows, strip):
    lane = lax.broadcasted_iota(jnp.int32, (rows, LANES), 1)
    return lax.rem(lane // STRIP - strip + 2 * G, G), lax.rem(lane, STRIP)


def pick(group, parts):
    out = parts[0]
    for b in range(1, G):
        out = jnp.where(group == b, parts[b], out)
    return out


def parity_order(transposed):
    src = lax.broadcasted_iota(jnp.int32, (LANES, LANES), 1 if transposed else 0)
    dst = lax.broadcasted_iota(jnp.int32, (LANES, LANES), 0 if transposed else 1)
    within = lax.rem(src, STRIP)
    place = src - within + 16 * lax.rem(within, 2) + within // 2
    return jnp.where(place == dst, 1.0, 0.0).astype(jnp.bfloat16)


def reorder(x, order):
    if x.dtype == jnp.bfloat16:
        return jnp.dot(x, order, preferred_element_type=F32)
    high = x.astype(jnp.bfloat16)
    rest = x - high.astype(F32)
    middle = rest.astype(jnp.bfloat16)
    low = (rest - middle.astype(F32)).astype(jnp.bfloat16)
    return (
        jnp.dot(high, order, preferred_element_type=F32)
        + jnp.dot(middle, order, preferred_element_type=F32)
        + jnp.dot(low, order, preferred_element_type=F32)
    )


def pack_kernel(names, strips, *refs):
    ins, outs = refs[: len(refs) - G], refs[len(refs) - G :]
    order = parity_order(False)
    groups = [lanes_of(BY, strips[d])[0] for d in range(G)]
    for n, name in enumerate(names):
        for a in range(2):
            planes = reorder(ins[n][4 * a : 4 * a + 4].reshape(4 * BY, LANES), order)
            parts = []
            for b in range(4):
                plane = planes[BY * b : BY * (b + 1)]
                if name == "previous":
                    plane = plane * ins[n + 1][4 * a + b]
                parts.append(roll(plane, 32 * b))
            for d in range(G):
                outs[d][n, a] = pick(groups[d], parts)


def edge_kernel(places, *refs):
    msgs, (to_left, to_right, head, tail) = refs[:G], refs[G : G + 4]
    corners = refs[G + 4 :]
    lane = lax.broadcasted_iota(jnp.int32, (BY, LANES), 1)
    low = lax.rem(lane, 16) < 8
    rows = (slice(BY - HALO, BY), slice(0, HALO))
    for n in range(msgs[0].shape[0]):
        for d in range(G):
            first, second = msgs[d][n, 0], msgs[d][n, 1]
            edges = (jnp.where(low, first, roll(second, 8)), jnp.where(low, roll(second, -8), first))
            for side, out in enumerate((to_left, to_right)):
                out[n, places[side, d]] = edges[side]
                for way in range(2):
                    corners[2 * side + way][n, places[side, d]] = edges[side][rows[way]]
            for a in range(2):
                head[n, d, a] = msgs[d][n, a, :HALO]
                tail[n, d, a] = msgs[d][n, a, BY - HALO :]


def unpack(get_brick, get_edge, group, within, put):
    by_block = [BLOCK.index(q) for q in range(G)]
    edges = [[get_edge(side, d) for d in by_block] for side in range(2)]
    for a in range(2):
        far = 24 if a else 16
        own = [roll(get_brick(by_block[q], a), 32 * q) for q in range(G)]
        below = [roll(edges[0][q], 32 * q + far) for q in range(G)]
        above = [roll(edges[1][q], 32 * q - far) for q in range(G)]
        even = [
            jnp.where(within < 16, own[q], jnp.where(within < 24, above[q], below[(q + 1) % G])) for q in range(G)
        ]
        odd = [
            jnp.where(within < 8, above[(q - 1) % G], jnp.where(within < 16, below[q], own[q])) for q in range(G)
        ]
        for b in range(4):
            for e, parts in enumerate((even, odd)):
                whole = pick(group, [parts[(q - b) % G] for q in range(G)])
                put(4 * a + b, e, roll(whole, -32 * b - 16 * e))


def solve_kernel(nf, where, strip, scalars, *refs):
    stacks = []
    for _ in range(1 + max(stack for stack, _ in where)):
        stacks.append((refs[:G],) + tuple(refs[G : G + 8]))
        refs = refs[G + 8 :]
    outs = refs[:G]
    refs = refs[G:]
    xa, xb, xc, rhs, turned = (refs[nf * j : nf * (j + 1)] for j in range(5))
    kap, kx, ky, kin, kout, diag = refs[5 * nf :]
    zero = jnp.zeros((TILE, LANES), F32)
    targets = (kap,) + tuple(rhs)

    def put_at(dst, to, rows):
        def put(i, e, val):
            dst[i, e, pl.ds(to, rows)] = val

        return put

    @pl.loop(0, BY // CHUNK)
    def _(t):
        r = pl.multiple_of(CHUNK * t, CHUNK)
        to = pl.multiple_of(TOP + CHUNK * t, TILE)
        group, within = lanes_of(CHUNK, strip[0])
        for dst, (stack, n) in zip(targets, where):
            bricks, *sides = stacks[stack][:3]
            unpack(
                lambda d, a: bricks[d][n, a, pl.ds(r, CHUNK)],
                lambda side, d: sides[side][n, d, pl.ds(r, CHUNK)],
                group,
                within,
                put_at(dst, to, CHUNK),
            )

    for dst, (stack, n) in zip(targets, where):
        above, below, *corners = stacks[stack][3:]
        group_halo, within_halo = lanes_of(HALO, strip[0])
        for brick, edge, start in ((above, corners[:2], TOP - HALO), (below, corners[2:], TOP + BY)):
            unpack(
                lambda d, a: brick[n, d, a],
                lambda side, d: edge[side][n, d],
                group_halo,
                within_halo,
                put_at(dst, start, HALO),
            )

    for i in range(PLANES):
        for e in range(2):
            for dst in (kap, ky) + tuple(rhs) + tuple(xa) + tuple(xb) + tuple(xc):
                dst[i, e, 0:TILE] = zero
                dst[i, e, ROWS - TILE : ROWS] = zero
        for dst in (kin, kout):
            dst[i, 0:TILE] = zero
            dst[i, ROWS - TILE : ROWS] = zero

    theta_inv = scalars[0, 0]

    @pl.loop(0, (ROWS // TILE - 2) // 2)
    def _(t):
        rows = 2 * TILE
        r = pl.multiple_of(TILE + rows * t, TILE)
        at = pl.ds(r, rows)
        first = [kap[0, e, at] for e in range(2)]
        now = first
        before = [4.0 * (k + roll(kap[PLANES - 1, e, at], 32)) for e, k in enumerate(first)]
        for i in range(PLANES):
            after = [kap[i + 1, e, at] if i + 1 < PLANES else roll(first[e], -32) for e in range(2)]
            inner = 4.0 * (now[0] + now[1])
            outer = 4.0 * (now[1] + roll(now[0], -1))
            outer_before = 4.0 * (now[0] + roll(now[1], 1))
            kin[i, at] = inner
            kout[i, at] = outer
            along = (inner + outer_before, inner + outer)
            for e in range(2):
                fx = 4.0 * (now[e] + after[e])
                fy = 4.0 * (now[e] + kap[i, e, pl.ds(r + 1, rows)])
                fym = 4.0 * (now[e] + kap[i, e, pl.ds(r - 1, rows)])
                kx[i, e, at] = fx
                ky[i, e, at] = fy
                diag[i, e, at] = 1.0 + (fx + before[e] + (fy + fym) + along[e])
                before[e] = fx
                for f in range(nf):
                    xb[f][i, e, at] = rhs[f][i, e, at] * theta_inv
                    xa[f][i, e, at] = jnp.zeros((rows, LANES), F32)
            now = after

    def turn_lanes(cur, r):
        for f in range(nf):
            for i in range(PLANES):
                outer = kout[i, pl.ds(r, TILE)]
                turned[f][i, 0] = roll(outer * cur[f][i, 1, pl.ds(r, TILE)], 1)
                turned[f][i, 1] = roll(cur[f][i, 0, pl.ds(r, TILE)], -1)
            for e in range(2):
                last = kx[PLANES - 1, e, pl.ds(r, TILE)] * cur[f][PLANES - 1, e, pl.ds(r, TILE)]
                turned[f][PLANES, e] = roll(last, 32)
                turned[f][PLANES + 1, e] = roll(cur[f][0, e, pl.ds(r, TILE)], -32)

    def advance(alpha, beta, old, cur, new, r):
        now = [[cur[f][0, e, pl.ds(r, TILE)] for e in range(2)] for f in range(nf)]
        before = [None] * nf
        fbefore = None
        for i in range(PLANES):
            fx = [kx[i, e, pl.ds(r, TILE)] for e in range(2)]
            fy = [ky[i, e, pl.ds(r, TILE)] for e in range(2)]
            fym = [ky[i, e, pl.ds(r - 1, TILE)] for e in range(2)]
            inner = kin[i, pl.ds(r, TILE)]
            outer = kout[i, pl.ds(r, TILE)]
            centre = [(1.0 + alpha) - beta * diag[i, e, pl.ds(r, TILE)] for e in range(2)]
            for f in range(nf):
                if i + 1 < PLANES:
                    after = [cur[f][i + 1, e, pl.ds(r, TILE)] for e in range(2)]
                else:
                    after = [turned[f][PLANES + 1, e] for e in range(2)]
                for e in range(2):
                    x = now[f][e]
                    near = fy[e] * cur[f][i, e, pl.ds(r + 1, TILE)] + fym[e] * cur[f][i, e, pl.ds(r - 1, TILE)]
                    side = turned[f][i, e]
                    near = near + (inner * now[f][1 - e] + (outer * side if e else side))
                    behind = fbefore[e] * before[f][e] if i else turned[f][PLANES, e]
                    near = near + (fx[e] * after[e] + behind)
                    near = near + rhs[f][i, e, pl.ds(r, TILE)]
                    new[f][i, e, pl.ds(r, TILE)] = centre[e] * x - alpha * old[f][i, e, pl.ds(r, TILE)] + beta * near
                before[f] = now[f]
                now[f] = after
            fbefore = fx

    def sweep(k, old, cur, new, span):
        alpha, beta = scalars[k, 0], scalars[k, 1]
        turn_lanes(cur, span[0])

        @pl.loop(0, span[1] // span[2])
        def _(t):
            for u in range(span[2]):
                r = pl.multiple_of(span[0] + TILE * (span[2] * t + u), TILE)
                advance(alpha, beta, old, cur, new, r)
                turn_lanes(cur, r + TILE)

    def three(k, spans):
        sweep(k, xa, xb, xc, spans[0])
        sweep(k + 1, xb, xc, xa, spans[1])
        sweep(k + 2, xc, xa, xb, spans[2])

    wide = (TILE, ROWS // TILE - 2, 4)
    narrow = (2 * TILE, ROWS // TILE - 4, 3)

    @pl.loop(0, 2)
    def _(m):
        three(1 + 3 * m, (wide,) * 3)

    three(7, (wide, narrow, narrow))

    @pl.loop(0, 2)
    def _(m):
        three(10 + 3 * m, (narrow,) * 3)

    def give(f, row, rows):
        group, within = lanes_of(rows, strip[0])
        at = pl.ds(row, rows)
        whole = [[xb[f][i, e, at] for e in range(2)] for i in range(PLANES)]
        parts = [jnp.where(within < 16, even, roll(odd, 16)) for even, odd in whole]
        turned = [roll(parts[i], 32 * (i % 4)) for i in range(PLANES)]
        mains = [[pick(group, [turned[4 * a + (q - d) % G] for q in range(G)]) for a in range(2)] for d in range(G)]
        tree = [jnp.where(within == 31, odd, even) for even, odd in whole]
        for level in range(3):
            width = 1 << level
            keep = (lax.rem(within + 1, STRIP) < width) | ((within >= 16) & (within < 16 + width))
            tree = [jnp.where(keep, tree[j], roll(tree[j + 1], width)) for j in range(0, len(tree), 2)]
        ends = roll(tree[0], 1)
        groups = (ends, ends, roll(parts[PLANES - 1], 96), roll(parts[0], 64))
        sides = [pick(group, [groups[(q - d) % G] for q in range(G)]) for d in range(G)]
        return mains, sides

    @pl.loop(0, BY // CHUNK)
    def _(t):
        to = pl.ds(pl.multiple_of(CHUNK * t, CHUNK), CHUNK)
        for f in range(nf):
            mains, sides = give(f, pl.multiple_of(TOP + CHUNK * t, TILE), CHUNK)
            for d in range(G):
                for a in range(2):
                    outs[d][f, a, to] = mains[d][a]
                outs[d][f, 2, to] = sides[d]

    sub = lax.broadcasted_iota(jnp.int32, (TILE, LANES), 0)
    for f in range(nf):
        over, under = give(f, TOP - TILE, TILE)[0], give(f, TOP + BY, TILE)[0]
        for d in range(G):
            for a in range(2):
                outs[d][f, a, BY:MROWS] = jnp.where(
                    sub == 0, pltpu.roll(over[d][a], 1, 0), pltpu.roll(under[d][a], 1, 0)
                )
            outs[d][f, 2, BY:MROWS] = zero


def final_kernel(nstacks, strips, *refs):
    stacks = [refs[G * j : G * (j + 1)] for j in range(nstacks)]
    refs = refs[G * nstacks :]
    cond, kdown, kup, kover, kunder, kzl, kzr, stored, scales, cot = refs[:10]
    grad, adjoint, state, residuals, xs, ends, kap = refs[10:]
    fields = [(stack, n) for stack in stacks for n in range(2 // nstacks)]
    order = parity_order(True)

    def owners(rows):
        return [lanes_of(rows, strips[d])[0] for d in range(G)]

    def choose(owner, parts, b):
        out = parts[0]
        for d in range(1, G):
            out = jnp.where(owner[d] == b, parts[d], out)
        return out

    def bricks(f, a, row, rows):
        msgs, n = fields[f]
        return [roll(msgs[d][n, a, pl.ds(row, rows)], -32 * d) for d in range(G)]

    @pl.loop(0, BY // CHUNK)
    def _(t):
        row = pl.multiple_of(CHUNK * t, CHUNK)
        to = pl.ds(pl.multiple_of(TILE + CHUNK * t, TILE), CHUNK)
        owner = owners(CHUNK)
        for f in range(2):
            whole = []
            for a in range(2):
                parts = bricks(f, a, row, CHUNK)
                whole += [roll(choose(owner, parts, b), -32 * b) for b in range(4)]
            parts = bricks(f, 2, row, CHUNK)
            for d in range(G):
                ends[f, strips[d], pl.ds(row, CHUNK)] = parts[d]
            whole += [roll(choose(owner, parts, b), -32 * b) for b in (2, 3)]
            ordered = reorder(jnp.concatenate(whole, axis=0), order)
            for j, at in enumerate([*range(1, 1 + BX), 0, 1 + BX]):
                xs[f, at, to] = ordered[CHUNK * j : CHUNK * (j + 1)]

    owner = owners(TILE)
    for f in range(2):
        whole = []
        for a in range(2):
            parts = bricks(f, a, BY, TILE)
            whole += [roll(choose(owner, parts, b), -32 * b) for b in range(4)]
        ordered = reorder(jnp.concatenate(whole, axis=0), order)
        for c in range(BX):
            val = pltpu.roll(ordered[TILE * c : TILE * (c + 1)], 7, 0)
            xs[f, 1 + c, 0:TILE] = val
            xs[f, 1 + c, TILE + BY : 2 * TILE + BY] = val
    kap[0, TILE : TILE + BY] = kdown[...]
    kap[1 + BX, TILE : TILE + BY] = kup[...]
    for c in range(BX):
        kap[1 + c, TILE : TILE + BY] = cond[c]
        kap[1 + c, 0:TILE] = jnp.broadcast_to(kover[c : c + 1], (TILE, LANES))
        kap[1 + c, TILE + BY : 2 * TILE + BY] = jnp.broadcast_to(kunder[c : c + 1], (TILE, LANES))
    lane = lax.broadcasted_iota(jnp.int32, (TILE, LANES), 1)

    @pl.loop(0, BY // TILE)
    def _(t):
        r = pl.multiple_of(TILE * t, TILE)
        r8 = pl.multiple_of(TILE * t + TILE, TILE)
        at_r = pl.ds(r, TILE)
        low = [ends[f, 0, at_r] for f in range(2)]
        high = [ends[f, G - 1, at_r] for f in range(2)]
        for c in range(BX):
            k = kap[1 + c, pl.ds(r8, TILE)]
            x = [xs[f, 1 + c, pl.ds(r8, TILE)] for f in range(2)]
            total = [0.0, 0.0]
            product = 0.0

            def sides():
                for at in (c, c + 2):
                    yield kap[at, pl.ds(r8, TILE)], [xs[f, at, pl.ds(r8, TILE)] for f in range(2)]
                for off in (-1, 1):
                    yield kap[1 + c, pl.ds(r8 + off, TILE)], [xs[f, 1 + c, pl.ds(r8 + off, TILE)] for f in range(2)]
                yield (
                    jnp.where(lane == 0, kzl[c, at_r], roll(k, 1)),
                    [jnp.where(lane == 0, roll(low[f], -c), roll(x[f], 1)) for f in range(2)],
                )
                yield (
                    jnp.where(lane == LANES - 1, kzr[c, at_r], roll(k, -1)),
                    [jnp.where(lane == LANES - 1, roll(high[f], 14 - c), roll(x[f], -1)) for f in range(2)],
                )

            for kn, xn in sides():
                face = k + kn
                differ = [x[f] - xn[f] for f in range(2)]
                product = product + differ[0] * differ[1]
                for f in range(2):
                    total[f] = total[f] + face * differ[f]
            grad[c, at_r] = (-0.5 * TIME_STEP) * product
            state[c, at_r] = x[0]
            adjoint[c, at_r] = x[1]
            previous = stored[c, pl.ds(r, TILE)].astype(F32) * scales[c, at_r]
            residuals[0, c, at_r] = previous - (x[0] + (0.5 * TIME_STEP) * total[0])
            residuals[1, c, at_r] = cot[c, at_r] - (x[1] + (0.5 * TIME_STEP) * total[1])


def call(kernel, outs, smem, vmem, scratch=()):
    vm = pl.BlockSpec(memory_space=pltpu.VMEM)
    sm = pl.BlockSpec(memory_space=pltpu.SMEM)
    return pl.pallas_call(
        kernel,
        out_shape=[jax.ShapeDtypeStruct(shape, F32) for shape in outs],
        in_specs=[sm] * len(smem) + [vm] * len(vmem),
        out_specs=[vm] * len(outs),
        scratch_shapes=[pltpu.VMEM(shape, F32) for shape in scratch],
        compiler_params=pltpu.CompilerParams(vmem_limit_bytes=48 * 1024 * 1024),
    )(*smem, *vmem)


def shifted(x, axis, by):
    count = lax.axis_size(axis)
    return lax.ppermute(x, axis, [(i, (i + by) % count) for i in range(count)])


def around(x, by, rows=0):
    order = [(g, 0) for g in range(G)] + [(g, 1) for g in reversed(range(G))]
    count = lax.axis_size("gy")
    if rows == 0:
        pairs = [(2 * g + p, 2 * order[(i + by) % len(order)][0] + order[(i + by) % len(order)][1]) for i, (g, p) in enumerate(order)]
        return lax.ppermute(x, ("gx", "pa"), pairs)
    pairs = []
    for i, (g, p) in enumerate(order):
        to_g, to_p = order[(i + by) % len(order)]
        for y in range(count):
            pairs.append(((g * count + y) * 2 + p, (to_g * count + (y + rows) % count) * 2 + to_p))
    return lax.ppermute(x, ("gx", "gy", "pa"), pairs)


def chebyshev_scalars(upper):
    theta = 0.5 * (upper + 1.0)
    delta = 0.5 * (upper - 1.0)
    sigma = theta / delta
    rho = 1.0 / sigma
    rows = [(1.0 / theta, 0.0 * theta)]
    for _ in range(1, CHEB):
        rho_next = 1.0 / (2.0 * sigma - rho)
        rows.append((rho_next * rho, 2.0 * rho_next / delta))
        rho = rho_next
    return jnp.stack([jnp.stack(row) for row in rows])


def redistributed(conductivity, stored_state, row_scales, cotangent, upper_bound):
    g = lax.axis_index("gx")
    pa = lax.axis_index("pa")

    def strip_of(device):
        return jnp.where(pa == 0, device, G - 1 - device)

    steps = jnp.arange(G, dtype=jnp.int32)
    ahead = lax.rem(g + steps, G)
    behind = lax.rem(g - steps + G, G)
    scalars = chebyshev_scalars(upper_bound[0])
    stored = shifted(stored_state, "pa", 1)
    scales = row_scales[:, :, None]

    kdown = shifted(conductivity[BX - 1], "gx", 1)
    kup = shifted(conductivity[0], "gx", -1)
    kover = shifted(conductivity[:, BY - 1], "gy", 1)
    kunder = shifted(conductivity[:, 0], "gy", -1)
    kends = shifted(jnp.stack((conductivity[:, :, BZ - 1], conductivity[:, :, 0])), "pa", 1)

    strip = strip_of(g)
    left_g = jnp.where(pa == 0, jnp.maximum(g - 1, 0), jnp.minimum(g + 1, G - 1))
    right_g = jnp.where(pa == 0, jnp.minimum(g + 1, G - 1), jnp.maximum(g - 1, 0))
    places = lax.rem(jnp.stack((left_g - g + steps, right_g - g + steps)) + G, G)

    def strips(names, arrays):
        count = len(names)
        pack = functools.partial(pack_kernel, names)
        parts = call(pack, [(count, 2, BY, LANES)] * G, [strip_of(ahead)], arrays)
        parts = [parts[0]] + [shifted(parts[d], "gx", d) for d in range(1, G)]
        edge = (count, G, BY, LANES)
        rim = (count, G, 2, HALO, LANES)
        corner = (count, G, HALO, LANES)
        to_left, to_right, head, tail, left_down, left_up, right_down, right_up = call(
            edge_kernel, [edge, edge, rim, rim] + [corner] * 4, [places], parts
        )
        from_right, from_left = around(to_left, -1), around(to_right, 1)
        below, above = shifted(head, "gy", -1), shifted(tail, "gy", 1)
        corners = [
            around(right_down, 1, 1),
            around(left_down, -1, 1),
            around(right_up, 1, -1),
            around(left_up, -1, -1),
        ]
        return [*parts, from_left, from_right, above, below, *corners]

    def solve(where, stacks):
        nf = len(where) - 1
        line = (PLANES, 2, ROWS, LANES)
        solved = call(
            functools.partial(solve_kernel, nf, where),
            [(nf, 3, MROWS, LANES)] * G,
            [strip[None], scalars],
            sum(stacks, []),
            [line] * (4 * nf)
            + [(PLANES + 2, 2, TILE, LANES)] * nf
            + [line] * 3
            + [(PLANES, ROWS, LANES)] * 2
            + [line],
        )
        return [solved[0]] + [shifted(solved[d], "gx", d) for d in range(1, G)]

    first = strips(("conductivity", "cotangent"), [conductivity, cotangent])
    second = strips(("previous",), [stored, scales])
    solved_adjoint = solve(((0, 0), (0, 1)), [first])
    solved_state = solve(((0, 0), (1, 0)), [first, second])
    out = (BX, BY, LANES)
    padded = (BX + 2, BY + 16, LANES)
    return call(
        functools.partial(final_kernel, 2),
        [out, out, out, (2,) + out],
        [strip_of(behind)],
        [*solved_state, *solved_adjoint, conductivity, kdown, kup, kover, kunder, kends[0][:, :, None], kends[1][:, :, None], stored, scales, cotangent],
        [(2,) + padded, (2, G, BY, LANES), padded],
    )


def body(conductivity, stored_state, row_scales, cotangent, upper_bound):
    strips_fit = (
        lax.axis_size("gx") == G
        and lax.axis_size("pa") == 2
        and conductivity.shape == (BX, BY, BZ)
    )
    run = redistributed if strips_fit else stepwise
    return tuple(run(conductivity, stored_state, row_scales, cotangent, upper_bound))


def solution(mesh):
    return jax.shard_map(
        body,
        mesh=mesh,
        in_specs=(
            P("gx", "gy", "pa"),
            P("gx", "gy", "pa"),
            P("gx", "gy"),
            P("gx", "gy", "pa"),
            P(),
        ),
        out_specs=(
            P("gx", "gy", "pa"),
            P("gx", "gy", "pa"),
            P("gx", "gy", "pa"),
            P(None, "gx", "gy", "pa"),
        ),
        check_vma=False,
    )
```

```python
import functools

import jax
import jax.numpy as jnp
from jax import lax
from jax.experimental import pallas as pl
from jax.experimental.pallas import tpu as pltpu
from jax.sharding import PartitionSpec as P

CHEB = 16
LANES = 128
HALO = CHEB
TIME_STEP = 8.0
F32 = jnp.float32


def with_halo(cells, sides, width):
    for axis, dim in sides:
        count = lax.axis_size(axis)
        head = lax.slice_in_dim(cells, 0, width, axis=dim)
        tail = lax.slice_in_dim(cells, cells.shape[dim] - width, cells.shape[dim], axis=dim)
        cells = jnp.concatenate(
            [
                lax.ppermute(tail, axis, [(i, (i + 1) % count) for i in range(count)]),
                cells,
                lax.ppermute(head, axis, [((i + 1) % count, i) for i in range(count)]),
            ],
            axis=dim,
        )
    return cells


def region(arr, spatial, offset):
    extent = arr.shape[-3:]
    window = [slice(1, length - 1) for length in extent]
    window[spatial] = slice(offset, extent[spatial] - 2 + offset)
    leading = [slice(None)] * (arr.ndim - 3)
    return arr[tuple(leading + window)]


def apply_operator(padded, kpad):
    centre = region(padded, 0, 1)
    kcentre = region(kpad, 0, 1)
    summed = jnp.zeros_like(centre)
    for spatial in range(3):
        for offset in (0, 2):
            summed = summed + 0.5 * (kcentre + region(kpad, spatial, offset)) * (
                centre - region(padded, spatial, offset)
            )
    return centre + TIME_STEP * summed


def stepwise(conductivity, stored_state, row_scales, cotangent, upper_bound):
    upper = upper_bound[0]
    kpad = with_halo(conductivity, (("gx", 0), ("gy", 1), ("pa", 2)), 1)
    count = lax.axis_size("pa")
    partner = lax.ppermute(stored_state, "pa", [(i, (i + count // 2) % count) for i in range(count)])
    previous = partner.astype(F32) * row_scales[:, :, None]
    rhs = jnp.stack((previous, cotangent))
    theta = 0.5 * (upper + 1.0)
    delta = 0.5 * (upper - 1.0)
    sigma = theta / delta
    sides = (("gx", 1), ("gy", 2), ("pa", 3))

    def sweep(step, carry):
        solved, residual, direction, rho = carry
        padded = with_halo(direction, sides, 1)
        solved = solved + direction
        residual = residual - apply_operator(padded, kpad)
        rho_next = 1.0 / (2.0 * sigma - rho)
        direction = rho_next * rho * direction + 2.0 * rho_next / delta * residual
        return (solved, residual, direction, rho_next)

    start = (jnp.zeros_like(rhs), rhs, rhs / theta, 1.0 / sigma)
    solved, residual, _, _ = lax.fori_loop(0, CHEB, sweep, start)
    pair = with_halo(solved, sides, 1)
    centre = region(pair, 0, 1)
    summed = jnp.zeros_like(solved[0])
    for spatial in range(3):
        for offset in (0, 2):
            differ = centre - region(pair, spatial, offset)
            summed = summed + differ[0] * differ[1]
    return (-0.5 * TIME_STEP * summed, solved[1], solved[0], residual)


G = 4
BX = 8
BY = 128
BZ = 128
STRIP = BZ // G
TOP = 8 + HALO
ROWS = BY + 2 * TOP
EXTENDED = BY + 2 * HALO
GROUP = BY + 8
SIDES = 2 * GROUP
FIELD = SIDES + BY
KAP = FIELD + BY
BOTH = KAP + 16
TILE = 8
CHUNK = 32

BLOCK = (0, 3, 2, 1)
PLANES = BX


def roll(x, by):
    by %= LANES
    return pltpu.roll(x, by, 1) if by else x


def lanes_of(rows, strip):
    lane = lax.broadcasted_iota(jnp.int32, (rows, LANES), 1)
    return lax.rem(lane // STRIP - strip + 2 * G, G), lax.rem(lane, STRIP)


def pick(group, parts):
    out = parts[0]
    for b in range(1, G):
        out = jnp.where(group == b, parts[b], out)
    return out


def parity_order(transposed):
    src = lax.broadcasted_iota(jnp.int32, (LANES, LANES), 1 if transposed else 0)
    dst = lax.broadcasted_iota(jnp.int32, (LANES, LANES), 0 if transposed else 1)
    within = lax.rem(src, STRIP)
    place = src - within + 16 * lax.rem(within, 2) + within // 2
    return jnp.where(place == dst, 1.0, 0.0).astype(jnp.bfloat16)


def reorder(x, order):
    if x.dtype == jnp.bfloat16:
        return jnp.dot(x, order, preferred_element_type=F32)
    high = x.astype(jnp.bfloat16)
    rest = x - high.astype(F32)
    middle = rest.astype(jnp.bfloat16)
    low = (rest - middle.astype(F32)).astype(jnp.bfloat16)
    return (
        jnp.dot(high, order, preferred_element_type=F32)
        + jnp.dot(middle, order, preferred_element_type=F32)
        + jnp.dot(low, order, preferred_element_type=F32)
    )


def pack_kernel(strips, *refs):
    ins, outs = refs[: len(refs) - G], refs[len(refs) - G :]
    order = parity_order(False)
    groups = [lanes_of(BY, strips[d])[0] for d in range(G)]
    for n, array in enumerate(ins):
        for a in range(2):
            planes = reorder(array[4 * a : 4 * a + 4].reshape(4 * BY, LANES), order)
            parts = [roll(planes[BY * b : BY * (b + 1)], 32 * b) for b in range(4)]
            for d in range(G):
                outs[d][n, a] = pick(groups[d], parts)


def pack_previous_kernel(strips, stored, scales, above, below, *outs):
    order = parity_order(False)
    for rows, start, array in ((BY, HALO, stored), (HALO, 0, above), (HALO, HALO + BY, below)):
        groups = [lanes_of(rows, strips[d])[0] for d in range(G)]
        for a in range(2):
            planes = reorder(array[4 * a : 4 * a + 4].reshape(4 * rows, LANES), order)
            parts = []
            for b in range(4):
                plane = planes[rows * b : rows * (b + 1)]
                if array is stored:
                    plane = plane * scales[4 * a + b]
                parts.append(roll(plane, 32 * b))
            for d in range(G):
                outs[d][0, a, start : start + rows] = pick(groups[d], parts)


def edge_kernel(places, *refs):
    msgs, (to_left, to_right), rims = refs[:G], refs[G : G + 2], refs[G + 2 :]
    length = msgs[0].shape[2]
    lane = lax.broadcasted_iota(jnp.int32, (length, LANES), 1)
    low = lax.rem(lane, 16) < 8
    rows = (slice(length - HALO, length), slice(0, HALO))
    for n in range(msgs[0].shape[0]):
        for d in range(G):
            first, second = msgs[d][n, 0], msgs[d][n, 1]
            edges = (jnp.where(low, first, roll(second, 8)), jnp.where(low, roll(second, -8), first))
            for side, out in enumerate((to_left, to_right)):
                out[n, places[side, d]] = edges[side]
            if rims:
                head, tail, *corners = rims
                for side in range(2):
                    for way in range(2):
                        corners[2 * side + way][n, places[side, d]] = edges[side][rows[way]]
                for a in range(2):
                    head[n, d, a] = msgs[d][n, a, :HALO]
                    tail[n, d, a] = msgs[d][n, a, length - HALO :]


def unpack(get_brick, get_edge, group, within, put):
    by_block = [BLOCK.index(q) for q in range(G)]
    edges = [[get_edge(side, d) for d in by_block] for side in range(2)]
    for a in range(2):
        far = 24 if a else 16
        own = [roll(get_brick(by_block[q], a), 32 * q) for q in range(G)]
        below = [roll(edges[0][q], 32 * q + far) for q in range(G)]
        above = [roll(edges[1][q], 32 * q - far) for q in range(G)]
        even = [
            jnp.where(within < 16, own[q], jnp.where(within < 24, above[q], below[(q + 1) % G])) for q in range(G)
        ]
        odd = [
            jnp.where(within < 8, above[(q - 1) % G], jnp.where(within < 16, below[q], own[q])) for q in range(G)
        ]
        for b in range(4):
            for e, parts in enumerate((even, odd)):
                whole = pick(group, [parts[(q - b) % G] for q in range(G)])
                put(4 * a + b, e, roll(whole, -32 * b - 16 * e))


def solve_kernel(sizes, where, give_kap, strip, upper, *refs):
    stacks = []
    for size in sizes:
        stacks.append((refs[:G],) + tuple(refs[G:size]))
        refs = refs[size:]
    outs = refs[:G]
    rhs, xa, xb, xc, turned, kap, kx, ky, kin, kout, diag, steps = refs[G:]
    zero = jnp.zeros((TILE, LANES), F32)
    targets = (kap, rhs)

    theta = 0.5 * (jnp.full((TILE, LANES), upper[0]) + 1.0)
    delta = 0.5 * (jnp.full((TILE, LANES), upper[0]) - 1.0)
    sigma = theta / delta
    rho = 1.0 / sigma
    for k in range(1, CHEB):
        rho_next = 1.0 / (2.0 * sigma - rho)
        steps[k, 0] = rho_next * rho
        steps[k, 1] = 2.0 * rho_next / delta
        rho = rho_next
    theta_inv = 1.0 / (0.5 * (jnp.full((2 * TILE, LANES), upper[0]) + 1.0))

    def put_at(dst, to, rows):
        def put(i, e, val):
            dst[i, e, pl.ds(to, rows)] = val

        return put

    for dst, (stack, n) in zip(targets, where):
        bricks, *sides = stacks[stack][:3]
        start = TOP - (bricks[0].shape[2] - BY) // 2

        @pl.loop(0, bricks[0].shape[2] // CHUNK)
        def _(t):
            at = pl.ds(pl.multiple_of(CHUNK * t, CHUNK), CHUNK)
            group, within = lanes_of(CHUNK, strip[0])
            unpack(
                lambda d, a: bricks[d][n, a, at],
                lambda side, d: sides[side][n, d, at],
                group,
                within,
                put_at(dst, pl.multiple_of(start + CHUNK * t, TILE), CHUNK),
            )

        if stacks[stack][3:]:
            above, below, *corners = stacks[stack][3:]
            group_halo, within_halo = lanes_of(HALO, strip[0])
            for brick, edge, start in ((above, corners[:2], TOP - HALO), (below, corners[2:], TOP + BY)):
                unpack(
                    lambda d, a: brick[n, d, a],
                    lambda side, d: edge[side][n, d],
                    group_halo,
                    within_halo,
                    put_at(dst, start, HALO),
                )

    for i in range(PLANES):
        for e in range(2):
            for dst in (kap, ky, rhs, xa, xb, xc):
                dst[i, e, 0:TILE] = zero
                dst[i, e, ROWS - TILE : ROWS] = zero
        for dst in (kin, kout):
            dst[i, 0:TILE] = zero
            dst[i, ROWS - TILE : ROWS] = zero

    @pl.loop(0, (ROWS // TILE - 2) // 2)
    def _(t):
        rows = 2 * TILE
        r = pl.multiple_of(TILE + rows * t, TILE)
        at = pl.ds(r, rows)
        first = [kap[0, e, at] for e in range(2)]
        now = first
        before = [4.0 * (k + roll(kap[PLANES - 1, e, at], 32)) for e, k in enumerate(first)]
        for i in range(PLANES):
            after = [kap[i + 1, e, at] if i + 1 < PLANES else roll(first[e], -32) for e in range(2)]
            inner = 4.0 * (now[0] + now[1])
            outer = 4.0 * (now[1] + roll(now[0], -1))
            outer_before = 4.0 * (now[0] + roll(now[1], 1))
            kin[i, at] = inner
            kout[i, at] = outer
            along = (inner + outer_before, inner + outer)
            for e in range(2):
                fx = 4.0 * (now[e] + after[e])
                fy = 4.0 * (now[e] + kap[i, e, pl.ds(r + 1, rows)])
                fym = 4.0 * (now[e] + kap[i, e, pl.ds(r - 1, rows)])
                kx[i, e, at] = fx
                ky[i, e, at] = fy
                diag[i, e, at] = 1.0 + (fx + before[e] + (fy + fym) + along[e])
                before[e] = fx
                xb[i, e, at] = rhs[i, e, at] * theta_inv
                xa[i, e, at] = jnp.zeros((rows, LANES), F32)
            now = after

    def turn_lanes(cur, r):
        at = pl.ds(r, TILE)
        for i in range(PLANES):
            turned[i, 0] = roll(kout[i, at] * cur[i, 1, at], 1)
            turned[i, 1] = roll(cur[i, 0, at], -1)
        for e in range(2):
            turned[PLANES, e] = roll(kx[PLANES - 1, e, at] * cur[PLANES - 1, e, at], 32)
            turned[PLANES + 1, e] = roll(cur[0, e, at], -32)

    def advance(alpha, beta, old, cur, new, r):
        at = pl.ds(r, TILE)
        now = [cur[0, e, at] for e in range(2)]
        before = fbefore = None
        for i in range(PLANES):
            fx = [kx[i, e, at] for e in range(2)]
            inner, outer = kin[i, at], kout[i, at]
            if i + 1 < PLANES:
                after = [cur[i + 1, e, at] for e in range(2)]
            else:
                after = [turned[PLANES + 1, e] for e in range(2)]
            for e in range(2):
                near = ky[i, e, at] * cur[i, e, pl.ds(r + 1, TILE)]
                near = near + ky[i, e, pl.ds(r - 1, TILE)] * cur[i, e, pl.ds(r - 1, TILE)]
                side = turned[i, e]
                near = near + (inner * now[1 - e] + (outer * side if e else side))
                behind = fbefore[e] * before[e] if i else turned[PLANES, e]
                near = near + (fx[e] * after[e] + behind)
                near = near + rhs[i, e, at]
                centre = (1.0 + alpha) - beta * diag[i, e, at]
                new[i, e, at] = centre * now[e] - alpha * old[i, e, at] + beta * near
            before, now, fbefore = now, after, fx

    def sweep(k, old, cur, new, span):
        alpha, beta = steps[k, 0], steps[k, 1]
        turn_lanes(cur, span[0])

        @pl.loop(0, span[1] // span[2])
        def _(t):
            for u in range(span[2]):
                r = pl.multiple_of(span[0] + TILE * (span[2] * t + u), TILE)
                advance(alpha, beta, old, cur, new, r)
                turn_lanes(cur, r + TILE)

    def three(k, spans):
        sweep(k, xa, xb, xc, spans[0])
        sweep(k + 1, xb, xc, xa, spans[1])
        sweep(k + 2, xc, xa, xb, spans[2])

    wide = (TILE, ROWS // TILE - 2, 4)
    narrow = (2 * TILE, ROWS // TILE - 4, 3)

    @pl.loop(0, 2)
    def _(m):
        three(1 + 3 * m, (wide,) * 3)

    three(7, (wide, narrow, narrow))

    @pl.loop(0, 2)
    def _(m):
        three(10 + 3 * m, (narrow,) * 3)

    def mains(whole, group, within):
        parts = [jnp.where(within < 16, even, roll(odd, 16)) for even, odd in whole]
        turned = [roll(parts[i], 32 * (i % 4)) for i in range(PLANES)]
        return parts, [
            [pick(group, [turned[4 * a + (q - d) % G] for q in range(G)]) for a in range(2)] for d in range(G)
        ]

    def beside(whole, parts, group, within):
        tree = [jnp.where(within == 31, odd, even) for even, odd in whole]
        for level in range(3):
            width = 1 << level
            keep = (lax.rem(within + 1, STRIP) < width) | ((within >= 16) & (within < 16 + width))
            tree = [jnp.where(keep, tree[j], roll(tree[j + 1], width)) for j in range(0, len(tree), 2)]
        ends = roll(tree[0], 1)
        groups = (ends, ends, roll(parts[PLANES - 1], 96), roll(parts[0], 64))
        return [pick(group, [groups[(q - d) % G] for q in range(G)]) for d in range(G)]

    def load(field, row, rows):
        return [[field[i, e, pl.ds(row, rows)] for e in range(2)] for i in range(PLANES)]

    @pl.loop(0, BY // CHUNK)
    def _(t):
        row = pl.multiple_of(TOP + CHUNK * t, TILE)
        group, within = lanes_of(CHUNK, strip[0])

        def to(start):
            return pl.ds(pl.multiple_of(start + CHUNK * t, TILE), CHUNK)

        for field, start in ((xb, SIDES),) + (((kap, FIELD),) if give_kap else ()):
            whole = load(field, row, CHUNK)
            parts, main = mains(whole, group, within)
            sides = beside(whole, parts, group, within)
            for d in range(G):
                outs[d][to(start)] = sides[d]
                if field is xb:
                    for a in range(2):
                        outs[d][to(GROUP * a)] = main[d][a]

    sub = lax.broadcasted_iota(jnp.int32, (TILE, LANES), 0)
    group, within = lanes_of(TILE, strip[0])
    for field in (xb, kap) if give_kap else (xb,):
        over = mains(load(field, TOP - TILE, TILE), group, within)[1]
        under = mains(load(field, TOP + BY, TILE), group, within)[1]
        for d in range(G):
            for a in range(2):
                to = GROUP * a + BY if field is xb else KAP + TILE * a
                outs[d][to : to + TILE] = jnp.where(
                    sub == 0, pltpu.roll(over[d][a], 1, 0), pltpu.roll(under[d][a], 1, 0)
                )


def collect(strips, msgs, padded, ends, base, own):
    order = parity_order(True)

    def owners(rows):
        return [lanes_of(rows, strips[d])[0] for d in range(G)]

    def choose(owner, parts, b):
        out = parts[0]
        for d in range(1, G):
            out = jnp.where(owner[d] == b, parts[d], out)
        return roll(out, -32 * b)

    def bricks(row, rows):
        return [roll(msgs[d][pl.ds(row, rows)], -32 * d) for d in range(G)]

    sides_at, tiles_at = (SIDES, (BY, GROUP + BY)) if own is None else (FIELD, (KAP, KAP + TILE))

    @pl.loop(0, BY // CHUNK)
    def _(t):
        to = pl.ds(pl.multiple_of(TILE + CHUNK * t, TILE), CHUNK)
        owner = owners(CHUNK)
        whole, places = [], []
        if own is None:
            for a in range(2):
                parts = bricks(pl.multiple_of(GROUP * a + CHUNK * t, TILE), CHUNK)
                whole += [choose(owner, parts, b) for b in range(4)]
                places += [1 + 4 * a + b for b in range(4)]
        else:
            for c in range(BX):
                padded[1 + c, to] = own[c, pl.ds(pl.multiple_of(CHUNK * t, CHUNK), CHUNK)]
        parts = bricks(pl.multiple_of(sides_at + CHUNK * t, TILE), CHUNK)
        for side, end in enumerate((0, G - 1)):
            val = parts[0]
            for d in range(1, G):
                val = jnp.where(strips[d] == end, parts[d], val)
            ends[side, pl.ds(pl.multiple_of(CHUNK * t, CHUNK), CHUNK)] = val
        whole += [choose(owner, parts, b) for b in (2, 3)]
        places += [0, 1 + BX]
        ordered = reorder(jnp.concatenate(whole, axis=0), order)
        for j, at in enumerate(places):
            padded[at, to] = ordered[CHUNK * j : CHUNK * (j + 1)]

    owner = owners(TILE)
    whole = []
    for a in range(2):
        parts = bricks(tiles_at[a], TILE)
        whole += [choose(owner, parts, b) for b in range(4)]
    ordered = reorder(jnp.concatenate(whole, axis=0), order)
    for c in range(BX):
        val = pltpu.roll(ordered[TILE * c : TILE * (c + 1)], 7, 0)
        padded[1 + c, 0:TILE] = val
        padded[1 + c, TILE + BY : 2 * TILE + BY] = val


def around_cell(padded, ends, c, t):
    lane = lax.broadcasted_iota(jnp.int32, (TILE, LANES), 1)
    r = pl.multiple_of(TILE * t, TILE)
    r8 = pl.multiple_of(TILE * t + TILE, TILE)
    cell = padded[1 + c, pl.ds(r8, TILE)]
    low, high = (ends[side, pl.ds(r, TILE)] for side in range(2))
    return cell, (
        padded[c, pl.ds(r8, TILE)],
        padded[c + 2, pl.ds(r8, TILE)],
        padded[1 + c, pl.ds(r8 - 1, TILE)],
        padded[1 + c, pl.ds(r8 + 1, TILE)],
        jnp.where(lane == 0, roll(low, -c), roll(cell, 1)),
        jnp.where(lane == LANES - 1, roll(high, 14 - c), roll(cell, -1)),
    )


def adjoint_kernel(strips, m0, m1, m2, m3, cond, cot, adjoint, residual, padded, ends, kap, kends):
    collect(strips, (m0, m1, m2, m3), padded, ends, 0, None)
    collect(strips, (m0, m1, m2, m3), kap, kends, 0, cond)

    @pl.loop(0, BY // TILE)
    def _(t):
        at = pl.ds(pl.multiple_of(TILE * t, TILE), TILE)
        for c in range(BX):
            k, knear = around_cell(kap, kends, c, t)
            x, xnear = around_cell(padded, ends, c, t)
            total = 0.0
            for kn, xn in zip(knear, xnear):
                total = total + (k + kn) * (x - xn)
            adjoint[c, at] = x
            residual[c, at] = cot[c, at] - (x + (0.5 * TIME_STEP) * total)


def state_kernel(strips, m0, m1, m2, m3, stored, scales, adj, adj_ends, kap, kends, adj_residual, grad, state, residuals, padded, ends):
    collect(strips, (m0, m1, m2, m3), padded, ends, 0, None)

    @pl.loop(0, BY // TILE)
    def _(t):
        at = pl.ds(pl.multiple_of(TILE * t, TILE), TILE)
        for c in range(BX):
            k, knear = around_cell(kap, kends, c, t)
            x, xnear = around_cell(padded, ends, c, t)
            y, ynear = around_cell(adj, adj_ends, c, t)
            total = product = 0.0
            for kn, xn, yn in zip(knear, xnear, ynear):
                differ = x - xn
                total = total + (k + kn) * differ
                product = product + differ * (y - yn)
            grad[c, at] = (-0.5 * TIME_STEP) * product
            state[c, at] = x
            previous = stored[c, at].astype(F32) * scales[c, at]
            residuals[0, c, at] = previous - (x + (0.5 * TIME_STEP) * total)
            residuals[1, c, at] = adj_residual[c, at]


def call(kernel, outs, smem, vmem, scratch=(), micros=2):
    vm = pl.BlockSpec(memory_space=pltpu.VMEM)
    sm = pl.BlockSpec(memory_space=pltpu.SMEM)
    return pl.pallas_call(
        kernel,
        out_shape=[jax.ShapeDtypeStruct(shape, F32) for shape in outs],
        in_specs=[sm] * len(smem) + [vm] * len(vmem),
        out_specs=[vm] * len(outs),
        scratch_shapes=[pltpu.VMEM(shape, F32) for shape in scratch],
        compiler_params=pltpu.CompilerParams(vmem_limit_bytes=48 * 1024 * 1024),
        cost_estimate=pl.CostEstimate(flops=0, bytes_accessed=micros * 3_000_000, transcendentals=0),
    )(*smem, *vmem)


def shifted(x, axis, by):
    count = lax.axis_size(axis)
    return lax.ppermute(x, axis, [(i, (i + by) % count) for i in range(count)])


def around(x, by, rows=0):
    order = [(g, 0) for g in range(G)] + [(g, 1) for g in reversed(range(G))]
    count = lax.axis_size("gy")
    if rows == 0:
        pairs = [(2 * g + p, 2 * order[(i + by) % len(order)][0] + order[(i + by) % len(order)][1]) for i, (g, p) in enumerate(order)]
        return lax.ppermute(x, ("gx", "pa"), pairs)
    pairs = []
    for i, (g, p) in enumerate(order):
        to_g, to_p = order[(i + by) % len(order)]
        for y in range(count):
            pairs.append(((g * count + y) * 2 + p, (to_g * count + (y + rows) % count) * 2 + to_p))
    return lax.ppermute(x, ("gx", "gy", "pa"), pairs)


def redistributed(conductivity, stored_state, row_scales, cotangent, upper_bound):
    g = lax.axis_index("gx")
    pa = lax.axis_index("pa")

    def strip_of(device):
        return jnp.where(pa == 0, device, G - 1 - device)

    steps = jnp.arange(G, dtype=jnp.int32)
    ahead = lax.rem(g + steps, G)
    behind = lax.rem(g - steps + G, G)
    stored = shifted(stored_state, "pa", 1)
    scales = row_scales[:, :, None]

    strip = strip_of(g)
    left_g = jnp.where(pa == 0, jnp.maximum(g - 1, 0), jnp.minimum(g + 1, G - 1))
    right_g = jnp.where(pa == 0, jnp.minimum(g + 1, G - 1), jnp.maximum(g - 1, 0))
    places = lax.rem(jnp.stack((left_g - g + steps, right_g - g + steps)) + G, G)

    def strips(kernel, shape, arrays, with_rims):
        count, _, rows, _ = shape
        parts = call(kernel, [shape] * G, [strip_of(ahead)], arrays)
        parts = [parts[0]] + [shifted(parts[d], "gx", d) for d in range(1, G)]
        edge = (count, G, rows, LANES)
        rim = (count, G, 2, HALO, LANES)
        corner = (count, G, HALO, LANES)
        to_left, to_right, *rims = call(
            edge_kernel, [edge, edge] + ([rim, rim] + [corner] * 4 if with_rims else []), [places], parts
        )
        halos = [around(to_right, 1), around(to_left, -1)]
        if with_rims:
            head, tail, left_down, left_up, right_down, right_up = rims
            halos += [shifted(tail, "gy", 1), shifted(head, "gy", -1)]
            halos += [
                around(right_down, 1, 1),
                around(left_down, -1, 1),
                around(right_up, 1, -1),
                around(left_up, -1, -1),
            ]
        return [*parts, *halos]

    def solve(where, stacks, give_kap):
        line = (PLANES, 2, ROWS, LANES)
        half = (PLANES, ROWS, LANES)
        solved = call(
            functools.partial(solve_kernel, [len(stack) for stack in stacks], where, give_kap),
            [(BOTH if give_kap else FIELD, LANES)] * G,
            [strip[None], upper_bound],
            sum(stacks, []),
            [line] * 4
            + [(PLANES + 2, 2, TILE, LANES)]
            + [line] * 3
            + [half, half, line]
            + [(CHEB, 2, TILE, LANES)],
            micros=25,
        )
        return [solved[0]] + [shifted(solved[d], "gx", d) for d in range(1, G)]

    first = strips(pack_kernel, (2, 2, BY, LANES), [conductivity, cotangent], True)
    above = shifted(stored[:, BY - HALO :].astype(F32) * scales[:, BY - HALO :], "gy", 1)
    below = shifted(stored[:, :HALO].astype(F32) * scales[:, :HALO], "gy", -1)
    second = strips(pack_previous_kernel, (1, 2, EXTENDED, LANES), [stored, scales, above, below], False)
    solved_adjoint = solve(((0, 0), (0, 1)), [first], True)
    solved_state = solve(((0, 0), (1, 0)), [first, second], False)

    out = (BX, BY, LANES)
    padded = (BX + 2, BY + 16, LANES)
    ends = (2, BY, LANES)
    here = strip_of(behind)
    adjoint, adj_residual, adj, adj_ends, kap, kends = call(
        adjoint_kernel,
        [out, out, padded, ends, padded, ends],
        [here],
        [*solved_adjoint, conductivity, cotangent],
    )
    grad, state, residuals = call(
        state_kernel,
        [out, out, (2,) + out],
        [here],
        [*solved_state, stored, scales, adj, adj_ends, kap, kends, adj_residual],
        [padded, ends],
    )
    return grad, adjoint, state, residuals


def body(conductivity, stored_state, row_scales, cotangent, upper_bound):
    strips_fit = (
        lax.axis_size("gx") == G
        and lax.axis_size("pa") == 2
        and conductivity.shape == (BX, BY, BZ)
    )
    run = redistributed if strips_fit else stepwise
    return tuple(run(conductivity, stored_state, row_scales, cotangent, upper_bound))


def solution(mesh):
    return jax.shard_map(
        body,
        mesh=mesh,
        in_specs=(
            P("gx", "gy", "pa"),
            P("gx", "gy", "pa"),
            P("gx", "gy"),
            P("gx", "gy", "pa"),
            P(),
        ),
        out_specs=(
            P("gx", "gy", "pa"),
            P("gx", "gy", "pa"),
            P("gx", "gy", "pa"),
            P(None, "gx", "gy", "pa"),
        ),
        check_vma=False,
    )
```

```python
import functools

import jax
import jax.numpy as jnp
from jax import lax
from jax.experimental import pallas as pl
from jax.experimental.pallas import tpu as pltpu
from jax.sharding import PartitionSpec as P

CHEB = 16
LANES = 128
HALO = CHEB
TIME_STEP = 8.0
F32 = jnp.float32


def with_halo(cells, sides, width):
    for axis, dim in sides:
        count = lax.axis_size(axis)
        head = lax.slice_in_dim(cells, 0, width, axis=dim)
        tail = lax.slice_in_dim(cells, cells.shape[dim] - width, cells.shape[dim], axis=dim)
        cells = jnp.concatenate(
            [
                lax.ppermute(tail, axis, [(i, (i + 1) % count) for i in range(count)]),
                cells,
                lax.ppermute(head, axis, [((i + 1) % count, i) for i in range(count)]),
            ],
            axis=dim,
        )
    return cells


def region(arr, spatial, offset):
    extent = arr.shape[-3:]
    window = [slice(1, length - 1) for length in extent]
    window[spatial] = slice(offset, extent[spatial] - 2 + offset)
    leading = [slice(None)] * (arr.ndim - 3)
    return arr[tuple(leading + window)]


def apply_operator(padded, kpad):
    centre = region(padded, 0, 1)
    kcentre = region(kpad, 0, 1)
    summed = jnp.zeros_like(centre)
    for spatial in range(3):
        for offset in (0, 2):
            summed = summed + 0.5 * (kcentre + region(kpad, spatial, offset)) * (
                centre - region(padded, spatial, offset)
            )
    return centre + TIME_STEP * summed


def stepwise(conductivity, stored_state, row_scales, cotangent, upper_bound):
    upper = upper_bound[0]
    kpad = with_halo(conductivity, (("gx", 0), ("gy", 1), ("pa", 2)), 1)
    count = lax.axis_size("pa")
    partner = lax.ppermute(stored_state, "pa", [(i, (i + count // 2) % count) for i in range(count)])
    previous = partner.astype(F32) * row_scales[:, :, None]
    rhs = jnp.stack((previous, cotangent))
    theta = 0.5 * (upper + 1.0)
    delta = 0.5 * (upper - 1.0)
    sigma = theta / delta
    sides = (("gx", 1), ("gy", 2), ("pa", 3))

    def sweep(step, carry):
        solved, residual, direction, rho = carry
        padded = with_halo(direction, sides, 1)
        solved = solved + direction
        residual = residual - apply_operator(padded, kpad)
        rho_next = 1.0 / (2.0 * sigma - rho)
        direction = rho_next * rho * direction + 2.0 * rho_next / delta * residual
        return (solved, residual, direction, rho_next)

    start = (jnp.zeros_like(rhs), rhs, rhs / theta, 1.0 / sigma)
    solved, residual, _, _ = lax.fori_loop(0, CHEB, sweep, start)
    pair = with_halo(solved, sides, 1)
    centre = region(pair, 0, 1)
    summed = jnp.zeros_like(solved[0])
    for spatial in range(3):
        for offset in (0, 2):
            differ = centre - region(pair, spatial, offset)
            summed = summed + differ[0] * differ[1]
    return (-0.5 * TIME_STEP * summed, solved[1], solved[0], residual)


G = 4
BX = 8
BY = 128
BZ = 128
STRIP = BZ // G
TOP = 8 + HALO
ROWS = BY + 2 * TOP
EXTENDED = BY + 2 * HALO
GROUP = BY + 8
SIDES = 2 * GROUP
FIELD = SIDES + BY
KAP = FIELD + BY
BOTH = KAP + 16
TILE = 8
CHUNK = 32

BLOCK = (0, 3, 2, 1)
PLANES = BX


def roll(x, by):
    by %= LANES
    return pltpu.roll(x, by, 1) if by else x


def lanes_of(rows, strip):
    lane = lax.broadcasted_iota(jnp.int32, (rows, LANES), 1)
    return lax.rem(lane // STRIP - strip + 2 * G, G), lax.rem(lane, STRIP)


def pick(group, parts):
    out = parts[0]
    for b in range(1, G):
        out = jnp.where(group == b, parts[b], out)
    return out


def parity_order(transposed):
    src = lax.broadcasted_iota(jnp.int32, (LANES, LANES), 1 if transposed else 0)
    dst = lax.broadcasted_iota(jnp.int32, (LANES, LANES), 0 if transposed else 1)
    within = lax.rem(src, STRIP)
    place = src - within + 16 * lax.rem(within, 2) + within // 2
    return jnp.where(place == dst, 1.0, 0.0).astype(jnp.bfloat16)


def reorder(x, order):
    if x.dtype == jnp.bfloat16:
        return jnp.dot(x, order, preferred_element_type=F32)
    high = x.astype(jnp.bfloat16)
    rest = x - high.astype(F32)
    middle = rest.astype(jnp.bfloat16)
    low = (rest - middle.astype(F32)).astype(jnp.bfloat16)
    return (
        jnp.dot(high, order, preferred_element_type=F32)
        + jnp.dot(middle, order, preferred_element_type=F32)
        + jnp.dot(low, order, preferred_element_type=F32)
    )


def pack_kernel(strips, *refs):
    ins, outs = refs[: len(refs) - G], refs[len(refs) - G :]
    order = parity_order(False)
    groups = [lanes_of(BY, strips[d])[0] for d in range(G)]
    for n, array in enumerate(ins):
        for a in range(2):
            planes = reorder(array[4 * a : 4 * a + 4].reshape(4 * BY, LANES), order)
            parts = [roll(planes[BY * b : BY * (b + 1)], 32 * b) for b in range(4)]
            for d in range(G):
                outs[d][n, a] = pick(groups[d], parts)


def pack_previous_kernel(strips, both, above, below, *outs):
    src = lax.broadcasted_iota(jnp.int32, (2 * LANES, 2 * LANES), 0)
    dst = lax.broadcasted_iota(jnp.int32, (2 * LANES, 2 * LANES), 1)
    place = LANES * lax.rem(src, 2) + 64 * (src // LANES) + lax.rem(src, LANES) // 2
    order = jnp.where(place == dst, 1.0, 0.0).astype(jnp.bfloat16)

    def give(planes, rows, start):
        groups = [lanes_of(rows, strips[d])[0] for d in range(G)]
        for m in range(4):
            pieces = []
            for i in (2 * m, 2 * m + 1):
                pair = planes[rows * i : rows * (i + 1)]
                for e in range(2):
                    pieces.append(pair[:, LANES * e : LANES * (e + 1)])
            for d in range(G):
                turned = [pltpu.roll(pieces[k], lax.rem(16 * strips[d] + 32 * k + 8, LANES), 1) for k in range(4)]
                outs[d][m, pl.ds(start, rows)] = pick(groups[d], turned)

    @pl.loop(0, BY // CHUNK)
    def _(t):
        r = pl.multiple_of(CHUNK * t, CHUNK)
        halves = [both[half, :, pl.ds(r, CHUNK)].reshape(BX * CHUNK, LANES) for half in range(2)]
        give(reorder(jnp.concatenate(halves, axis=1), order), CHUNK, pl.multiple_of(HALO + CHUNK * t, HALO))

    for start, array in ((0, above), (HALO + BY, below)):
        halves = [array[half].reshape(BX * HALO, LANES) for half in range(2)]
        give(reorder(jnp.concatenate(halves, axis=1), order), HALO, start)


def edge_kernel(places, *refs):
    msgs, (to_left, to_right), rims = refs[:G], refs[G : G + 2], refs[G + 2 :]
    length = msgs[0].shape[2]
    lane = lax.broadcasted_iota(jnp.int32, (length, LANES), 1)
    low = lax.rem(lane, 16) < 8
    rows = (slice(length - HALO, length), slice(0, HALO))
    for n in range(msgs[0].shape[0]):
        for d in range(G):
            first, second = msgs[d][n, 0], msgs[d][n, 1]
            edges = (jnp.where(low, first, roll(second, 8)), jnp.where(low, roll(second, -8), first))
            for side, out in enumerate((to_left, to_right)):
                out[n, places[side, d]] = edges[side]
            if rims:
                head, tail, *corners = rims
                for side in range(2):
                    for way in range(2):
                        corners[2 * side + way][n, places[side, d]] = edges[side][rows[way]]
                for a in range(2):
                    head[n, d, a] = msgs[d][n, a, :HALO]
                    tail[n, d, a] = msgs[d][n, a, length - HALO :]


def unpack(get_brick, get_edge, group, within, put):
    by_block = [BLOCK.index(q) for q in range(G)]
    edges = [[get_edge(side, d) for d in by_block] for side in range(2)]
    for a in range(2):
        far = 24 if a else 16
        own = [roll(get_brick(by_block[q], a), 32 * q) for q in range(G)]
        below = [roll(edges[0][q], 32 * q + far) for q in range(G)]
        above = [roll(edges[1][q], 32 * q - far) for q in range(G)]
        even = [
            jnp.where(within < 16, own[q], jnp.where(within < 24, above[q], below[(q + 1) % G])) for q in range(G)
        ]
        odd = [
            jnp.where(within < 8, above[(q - 1) % G], jnp.where(within < 16, below[q], own[q])) for q in range(G)
        ]
        for b in range(4):
            for e, parts in enumerate((even, odd)):
                whole = pick(group, [parts[(q - b) % G] for q in range(G)])
                put(4 * a + b, e, roll(whole, -32 * b - 16 * e))


def unpack_strip(get, group, put):
    by_block = [BLOCK.index(q) for q in range(G)]
    for m in range(4):
        turned = [roll(get(by_block[q], m), 32 * q) for q in range(G)]
        for k in range(4):
            whole = pick(group, [turned[(q - k) % G] for q in range(G)])
            put(2 * m + k // 2, k % 2, roll(whole, -32 * k - 8))


def solve_kernel(sizes, give_kap, strip, upper, *refs):
    refs, finish = fetch(refs, sum(sizes))
    stacks = []
    for size in sizes:
        stacks.append((refs[:G],) + tuple(refs[G:size]))
        refs = refs[size:]
    outs = refs[:G]
    rhs, xa, xb, xc, turned, kap, kx, ky, kin, kout, diag, steps = refs[G:]
    zero = jnp.zeros((TILE, LANES), F32)
    targets = (kap, rhs)

    theta = 0.5 * (jnp.full((TILE, LANES), upper[0]) + 1.0)
    delta = 0.5 * (jnp.full((TILE, LANES), upper[0]) - 1.0)
    sigma = theta / delta
    rho = 1.0 / sigma
    for k in range(1, CHEB):
        rho_next = 1.0 / (2.0 * sigma - rho)
        steps[k, 0] = rho_next * rho
        steps[k, 1] = 2.0 * rho_next / delta
        rho = rho_next
    theta_inv = 1.0 / (0.5 * (jnp.full((2 * TILE, LANES), upper[0]) + 1.0))

    def put_at(dst, to, rows):
        def put(i, e, val):
            dst[i, e, pl.ds(to, rows)] = val

        return put

    for i in range(PLANES):
        for e in range(2):
            for dst in (kap, ky, rhs, xa, xb, xc):
                dst[i, e, 0:TILE] = zero
                dst[i, e, ROWS - TILE : ROWS] = zero
        for dst in (kin, kout):
            dst[i, 0:TILE] = zero
            dst[i, ROWS - TILE : ROWS] = zero

    finish()

    for n, dst in enumerate(targets):
        bricks, *sides = stacks[0][:3]
        if n == 1 and len(stacks) > 1:
            strips_here = stacks[1][0]

            @pl.loop(0, EXTENDED // CHUNK)
            def _(t):
                at = pl.ds(pl.multiple_of(CHUNK * t, CHUNK), CHUNK)
                group, _ = lanes_of(CHUNK, strip[0])
                unpack_strip(
                    lambda d, m: strips_here[d][m, at],
                    group,
                    put_at(dst, pl.multiple_of(TOP - HALO + CHUNK * t, TILE), CHUNK),
                )

            continue

        @pl.loop(0, BY // CHUNK)
        def _(t):
            at = pl.ds(pl.multiple_of(CHUNK * t, CHUNK), CHUNK)
            group, within = lanes_of(CHUNK, strip[0])
            unpack(
                lambda d, a: bricks[d][n, a, at],
                lambda side, d: sides[side][n, d, at],
                group,
                within,
                put_at(dst, pl.multiple_of(TOP + CHUNK * t, TILE), CHUNK),
            )

        above, below, *corners = stacks[0][3:]
        group_halo, within_halo = lanes_of(HALO, strip[0])
        for brick, edge, start in ((above, corners[:2], TOP - HALO), (below, corners[2:], TOP + BY)):
            unpack(
                lambda d, a: brick[n, d, a],
                lambda side, d: edge[side][n, d],
                group_halo,
                within_halo,
                put_at(dst, start, HALO),
            )

    @pl.loop(0, (ROWS // TILE - 2) // 2)
    def _(t):
        rows = 2 * TILE
        r = pl.multiple_of(TILE + rows * t, TILE)
        at = pl.ds(r, rows)
        first = [kap[0, e, at] for e in range(2)]
        now = first
        before = [4.0 * (k + roll(kap[PLANES - 1, e, at], 32)) for e, k in enumerate(first)]
        for i in range(PLANES):
            after = [kap[i + 1, e, at] if i + 1 < PLANES else roll(first[e], -32) for e in range(2)]
            inner = 4.0 * (now[0] + now[1])
            outer = 4.0 * (now[1] + roll(now[0], -1))
            outer_before = 4.0 * (now[0] + roll(now[1], 1))
            kin[i, at] = inner
            kout[i, at] = outer
            along = (inner + outer_before, inner + outer)
            for e in range(2):
                fx = 4.0 * (now[e] + after[e])
                fy = 4.0 * (now[e] + kap[i, e, pl.ds(r + 1, rows)])
                fym = 4.0 * (now[e] + kap[i, e, pl.ds(r - 1, rows)])
                kx[i, e, at] = fx
                ky[i, e, at] = fy
                diag[i, e, at] = 1.0 + (fx + before[e] + (fy + fym) + along[e])
                before[e] = fx
                xb[i, e, at] = rhs[i, e, at] * theta_inv
                xa[i, e, at] = jnp.zeros((rows, LANES), F32)
            now = after

    def turn_lanes(cur, r):
        at = pl.ds(r, TILE)
        for i in range(PLANES):
            turned[i, 0] = roll(kout[i, at] * cur[i, 1, at], 1)
            turned[i, 1] = roll(cur[i, 0, at], -1)
        for e in range(2):
            turned[PLANES, e] = roll(kx[PLANES - 1, e, at] * cur[PLANES - 1, e, at], 32)
            turned[PLANES + 1, e] = roll(cur[0, e, at], -32)

    def advance(alpha, beta, old, cur, new, r):
        at = pl.ds(r, TILE)
        now = [cur[0, e, at] for e in range(2)]
        before = fbefore = None
        for i in range(PLANES):
            fx = [kx[i, e, at] for e in range(2)]
            inner, outer = kin[i, at], kout[i, at]
            if i + 1 < PLANES:
                after = [cur[i + 1, e, at] for e in range(2)]
            else:
                after = [turned[PLANES + 1, e] for e in range(2)]
            for e in range(2):
                near = ky[i, e, at] * cur[i, e, pl.ds(r + 1, TILE)]
                near = near + ky[i, e, pl.ds(r - 1, TILE)] * cur[i, e, pl.ds(r - 1, TILE)]
                side = turned[i, e]
                near = near + (inner * now[1 - e] + (outer * side if e else side))
                behind = fbefore[e] * before[e] if i else turned[PLANES, e]
                near = near + (fx[e] * after[e] + behind)
                near = near + rhs[i, e, at]
                centre = (1.0 + alpha) - beta * diag[i, e, at]
                new[i, e, at] = centre * now[e] - alpha * old[i, e, at] + beta * near
            before, now, fbefore = now, after, fx

    def sweep(k, old, cur, new, span):
        alpha, beta = steps[k, 0], steps[k, 1]
        turn_lanes(cur, span[0])

        @pl.loop(0, span[1] // span[2])
        def _(t):
            for u in range(span[2]):
                r = pl.multiple_of(span[0] + TILE * (span[2] * t + u), TILE)
                advance(alpha, beta, old, cur, new, r)
                turn_lanes(cur, r + TILE)

    def three(k, spans):
        sweep(k, xa, xb, xc, spans[0])
        sweep(k + 1, xb, xc, xa, spans[1])
        sweep(k + 2, xc, xa, xb, spans[2])

    wide = (TILE, ROWS // TILE - 2, 4)
    narrow = (2 * TILE, ROWS // TILE - 4, 3)

    @pl.loop(0, 2)
    def _(m):
        three(1 + 3 * m, (wide,) * 3)

    three(7, (wide, narrow, narrow))

    @pl.loop(0, 2)
    def _(m):
        three(10 + 3 * m, (narrow,) * 3)

    def mains(whole, group, within):
        parts = [jnp.where(within < 16, even, roll(odd, 16)) for even, odd in whole]
        turned = [roll(parts[i], 32 * (i % 4)) for i in range(PLANES)]
        return parts, [
            [pick(group, [turned[4 * a + (q - d) % G] for q in range(G)]) for a in range(2)] for d in range(G)
        ]

    def beside(whole, parts, group, within):
        tree = [jnp.where(within == 31, odd, even) for even, odd in whole]
        for level in range(3):
            width = 1 << level
            keep = (lax.rem(within + 1, STRIP) < width) | ((within >= 16) & (within < 16 + width))
            tree = [jnp.where(keep, tree[j], roll(tree[j + 1], width)) for j in range(0, len(tree), 2)]
        ends = roll(tree[0], 1)
        groups = (ends, ends, roll(parts[PLANES - 1], 96), roll(parts[0], 64))
        return [pick(group, [groups[(q - d) % G] for q in range(G)]) for d in range(G)]

    def load(field, row, rows):
        return [[field[i, e, pl.ds(row, rows)] for e in range(2)] for i in range(PLANES)]

    @pl.loop(0, BY // CHUNK)
    def _(t):
        row = pl.multiple_of(TOP + CHUNK * t, TILE)
        group, within = lanes_of(CHUNK, strip[0])

        def to(start):
            return pl.ds(pl.multiple_of(start + CHUNK * t, TILE), CHUNK)

        for field, start in ((xb, SIDES),) + (((kap, FIELD),) if give_kap else ()):
            whole = load(field, row, CHUNK)
            parts, main = mains(whole, group, within)
            sides = beside(whole, parts, group, within)
            for d in range(G):
                outs[d][to(start)] = sides[d]
                if field is xb:
                    for a in range(2):
                        outs[d][to(GROUP * a)] = main[d][a]

    sub = lax.broadcasted_iota(jnp.int32, (TILE, LANES), 0)
    group, within = lanes_of(TILE, strip[0])
    for field in (xb, kap) if give_kap else (xb,):
        over = mains(load(field, TOP - TILE, TILE), group, within)[1]
        under = mains(load(field, TOP + BY, TILE), group, within)[1]
        for d in range(G):
            for a in range(2):
                to = GROUP * a + BY if field is xb else KAP + TILE * a
                outs[d][to : to + TILE] = jnp.where(
                    sub == 0, pltpu.roll(over[d][a], 1, 0), pltpu.roll(under[d][a], 1, 0)
                )


def collect(strips, msgs, padded, ends, base, own):
    order = parity_order(True)

    def owners(rows):
        return [lanes_of(rows, strips[d])[0] for d in range(G)]

    def choose(owner, parts, b):
        out = parts[0]
        for d in range(1, G):
            out = jnp.where(owner[d] == b, parts[d], out)
        return roll(out, -32 * b)

    def bricks(row, rows):
        return [roll(msgs[d][pl.ds(row, rows)], -32 * d) for d in range(G)]

    sides_at, tiles_at = (SIDES, (BY, GROUP + BY)) if own is None else (FIELD, (KAP, KAP + TILE))

    @pl.loop(0, BY // CHUNK)
    def _(t):
        to = pl.ds(pl.multiple_of(TILE + CHUNK * t, TILE), CHUNK)
        owner = owners(CHUNK)
        whole, places = [], []
        if own is None:
            for a in range(2):
                parts = bricks(pl.multiple_of(GROUP * a + CHUNK * t, TILE), CHUNK)
                whole += [choose(owner, parts, b) for b in range(4)]
                places += [1 + 4 * a + b for b in range(4)]
        else:
            for c in range(BX):
                padded[1 + c, to] = own[c, pl.ds(pl.multiple_of(CHUNK * t, CHUNK), CHUNK)]
        parts = bricks(pl.multiple_of(sides_at + CHUNK * t, TILE), CHUNK)
        for side, end in enumerate((0, G - 1)):
            val = parts[0]
            for d in range(1, G):
                val = jnp.where(strips[d] == end, parts[d], val)
            ends[side, pl.ds(pl.multiple_of(CHUNK * t, CHUNK), CHUNK)] = val
        whole += [choose(owner, parts, b) for b in (2, 3)]
        places += [0, 1 + BX]
        ordered = reorder(jnp.concatenate(whole, axis=0), order)
        for j, at in enumerate(places):
            padded[at, to] = ordered[CHUNK * j : CHUNK * (j + 1)]

    owner = owners(TILE)
    whole = []
    for a in range(2):
        parts = bricks(tiles_at[a], TILE)
        whole += [choose(owner, parts, b) for b in range(4)]
    ordered = reorder(jnp.concatenate(whole, axis=0), order)
    for c in range(BX):
        val = pltpu.roll(ordered[TILE * c : TILE * (c + 1)], 7, 0)
        padded[1 + c, 0:TILE] = val
        padded[1 + c, TILE + BY : 2 * TILE + BY] = val


def around_cell(padded, ends, c, t):
    lane = lax.broadcasted_iota(jnp.int32, (TILE, LANES), 1)
    r = pl.multiple_of(TILE * t, TILE)
    r8 = pl.multiple_of(TILE * t + TILE, TILE)
    cell = padded[1 + c, pl.ds(r8, TILE)]
    low, high = (ends[side, pl.ds(r, TILE)] for side in range(2))
    return cell, (
        padded[c, pl.ds(r8, TILE)],
        padded[c + 2, pl.ds(r8, TILE)],
        padded[1 + c, pl.ds(r8 - 1, TILE)],
        padded[1 + c, pl.ds(r8 + 1, TILE)],
        jnp.where(lane == 0, roll(low, -c), roll(cell, 1)),
        jnp.where(lane == LANES - 1, roll(high, 14 - c), roll(cell, -1)),
    )


def adjoint_kernel(strips, m0, m1, m2, m3, cond, cot, adjoint, residual, padded, ends, kap, kends):
    collect(strips, (m0, m1, m2, m3), padded, ends, 0, None)
    collect(strips, (m0, m1, m2, m3), kap, kends, 0, cond)

    @pl.loop(0, BY // TILE)
    def _(t):
        at = pl.ds(pl.multiple_of(TILE * t, TILE), TILE)
        for c in range(BX):
            k, knear = around_cell(kap, kends, c, t)
            x, xnear = around_cell(padded, ends, c, t)
            total = 0.0
            for kn, xn in zip(knear, xnear):
                total = total + (k + kn) * (x - xn)
            adjoint[c, at] = x
            residual[c, at] = cot[c, at] - (x + (0.5 * TIME_STEP) * total)


def state_kernel(strips, m0, m1, m2, m3, previous, adj, adj_ends, kap, kends, adj_residual, grad, state, residuals, padded, ends):
    collect(strips, (m0, m1, m2, m3), padded, ends, 0, None)

    @pl.loop(0, BY // TILE)
    def _(t):
        at = pl.ds(pl.multiple_of(TILE * t, TILE), TILE)
        for c in range(BX):
            k, knear = around_cell(kap, kends, c, t)
            x, xnear = around_cell(padded, ends, c, t)
            y, ynear = around_cell(adj, adj_ends, c, t)
            total = product = 0.0
            for kn, xn, yn in zip(knear, xnear, ynear):
                differ = x - xn
                total = total + (k + kn) * differ
                product = product + differ * (y - yn)
            grad[c, at] = (-0.5 * TIME_STEP) * product
            state[c, at] = x
            residuals[0, c, at] = previous[0, c, at] - (x + (0.5 * TIME_STEP) * total)
            residuals[1, c, at] = adj_residual[c, at]


def fetch(refs, count):
    away, here, sems = refs[:count], refs[len(refs) - count - 1 : -1], refs[-1]
    copies = [pltpu.make_async_copy(a, h, sems.at[j]) for j, (a, h) in enumerate(zip(away, here))]
    for copy in copies:
        copy.start()

    def finish():
        for copy in copies:
            copy.wait()

    return (*here, *refs[count : len(refs) - count - 1]), finish


def fetched(flags, smem, kernel, *refs):
    ins, rest = refs[smem : smem + len(flags)], refs[smem + len(flags) :]
    away = [ref for ref, flag in zip(ins, flags) if flag]
    inner, finish = fetch((*away, *rest), len(away))
    finish()
    here = iter(inner[: len(away)])
    ins = [next(here) if flag else ref for ref, flag in zip(ins, flags)]
    kernel(*refs[:smem], *ins, *inner[len(away) :])


def call(kernel, outs, smem, vmem, scratch=(), micros=2, fetches=False):
    vm = pl.BlockSpec(memory_space=pltpu.VMEM)
    sm = pl.BlockSpec(memory_space=pltpu.SMEM)
    hbm = pl.BlockSpec(memory_space=pltpu.HBM)
    flags = [x.shape[-1] == LANES for x in vmem]
    copies = [pltpu.VMEM(x.shape, x.dtype) for x, flag in zip(vmem, flags) if flag]
    return pl.pallas_call(
        kernel if fetches else functools.partial(fetched, flags, len(smem), kernel),
        out_shape=[jax.ShapeDtypeStruct(shape, F32) for shape in outs],
        in_specs=[sm] * len(smem) + [hbm if flag else vm for flag in flags],
        out_specs=[vm] * len(outs),
        scratch_shapes=[pltpu.VMEM(shape, F32) for shape in scratch]
        + copies
        + [pltpu.SemaphoreType.DMA((len(copies),))],
        compiler_params=pltpu.CompilerParams(vmem_limit_bytes=48 * 1024 * 1024),
        cost_estimate=pl.CostEstimate(flops=0, bytes_accessed=micros * 3_000_000, transcendentals=0),
    )(*smem, *vmem)


def shifted(x, axis, by):
    count = lax.axis_size(axis)
    return lax.ppermute(x, axis, [(i, (i + by) % count) for i in range(count)])


def around(x, by, rows=0):
    order = [(g, 0) for g in range(G)] + [(g, 1) for g in reversed(range(G))]
    count = lax.axis_size("gy")
    if rows == 0:
        pairs = [(2 * g + p, 2 * order[(i + by) % len(order)][0] + order[(i + by) % len(order)][1]) for i, (g, p) in enumerate(order)]
        return lax.ppermute(x, ("gx", "pa"), pairs)
    pairs = []
    for i, (g, p) in enumerate(order):
        to_g, to_p = order[(i + by) % len(order)]
        for y in range(count):
            pairs.append(((g * count + y) * 2 + p, (to_g * count + (y + rows) % count) * 2 + to_p))
    return lax.ppermute(x, ("gx", "gy", "pa"), pairs)


def redistributed(conductivity, stored_state, row_scales, cotangent, upper_bound):
    g = lax.axis_index("gx")
    pa = lax.axis_index("pa")

    def strip_of(device):
        return jnp.where(pa == 0, device, G - 1 - device)

    steps = jnp.arange(G, dtype=jnp.int32)
    ahead = lax.rem(g + steps, G)
    behind = lax.rem(g - steps + G, G)
    stored = shifted(stored_state, "pa", 1)
    scales = row_scales[:, :, None]

    strip = strip_of(g)
    left_g = jnp.where(pa == 0, jnp.maximum(g - 1, 0), jnp.minimum(g + 1, G - 1))
    right_g = jnp.where(pa == 0, jnp.minimum(g + 1, G - 1), jnp.maximum(g - 1, 0))
    places = lax.rem(jnp.stack((left_g - g + steps, right_g - g + steps)) + G, G)

    brick = (2, 2, BY, LANES)
    parts = call(pack_kernel, [brick] * G, [strip_of(ahead)], [conductivity, cotangent])
    parts = [parts[0]] + [shifted(parts[d], "gx", d) for d in range(1, G)]
    both = jnp.stack((stored, stored_state)).astype(F32) * scales
    above = shifted(both[:, :, BY - HALO :], "gy", 1)
    below = shifted(both[:, :, :HALO], "gy", -1)
    messages = call(
        pack_previous_kernel,
        [(4, EXTENDED, LANES)] * G,
        [strip_of(ahead)],
        [both, above, below],
    )
    parts, messages = lax.optimization_barrier((parts, messages))
    edge = (2, G, BY, LANES)
    rim = (2, G, 2, HALO, LANES)
    corner = (2, G, HALO, LANES)
    to_left, to_right, head, tail, left_down, left_up, right_down, right_up = call(
        edge_kernel, [edge, edge, rim, rim] + [corner] * 4, [places], parts
    )
    halos = [
        around(to_right, 1),
        around(to_left, -1),
        shifted(tail, "gy", 1),
        shifted(head, "gy", -1),
        around(right_down, 1, 1),
        around(left_down, -1, 1),
        around(right_up, 1, -1),
        around(left_up, -1, -1),
    ]

    messages, halos = lax.optimization_barrier((messages, halos))
    first = [*parts, *halos]
    second = [messages[0]] + [shifted(messages[d], "gx", d) for d in range(1, G)]

    def solve(stacks, give_kap):
        line = (PLANES, 2, ROWS, LANES)
        half = (PLANES, ROWS, LANES)
        solved = call(
            functools.partial(solve_kernel, [len(stack) for stack in stacks], give_kap),
            [(BOTH if give_kap else FIELD, LANES)] * G,
            [strip[None], upper_bound],
            sum(stacks, []),
            [line] * 4
            + [(PLANES + 2, 2, TILE, LANES)]
            + [line] * 3
            + [half, half, line]
            + [(CHEB, 2, TILE, LANES)],
            micros=25,
            fetches=True,
        )
        return [solved[0]] + [shifted(solved[d], "gx", d) for d in range(1, G)]

    solved_adjoint = solve([first], True)
    solved_state = solve([first, second], False)

    out = (BX, BY, LANES)
    padded = (BX + 2, BY + 16, LANES)
    ends = (2, BY, LANES)
    here = strip_of(behind)
    adjoint, adj_residual, adj, adj_ends, kap, kends = call(
        adjoint_kernel,
        [out, out, padded, ends, padded, ends],
        [here],
        [*solved_adjoint, conductivity, cotangent],
    )
    grad, state, residuals = call(
        state_kernel,
        [out, out, (2,) + out],
        [here],
        [*solved_state, both, adj, adj_ends, kap, kends, adj_residual],
        [padded, ends],
    )
    return grad, adjoint, state, residuals


def body(conductivity, stored_state, row_scales, cotangent, upper_bound):
    strips_fit = (
        lax.axis_size("gx") == G
        and lax.axis_size("pa") == 2
        and conductivity.shape == (BX, BY, BZ)
    )
    run = redistributed if strips_fit else stepwise
    return tuple(run(conductivity, stored_state, row_scales, cotangent, upper_bound))


def solution(mesh):
    return jax.shard_map(
        body,
        mesh=mesh,
        in_specs=(
            P("gx", "gy", "pa"),
            P("gx", "gy", "pa"),
            P("gx", "gy"),
            P("gx", "gy", "pa"),
            P(),
        ),
        out_specs=(
            P("gx", "gy", "pa"),
            P("gx", "gy", "pa"),
            P("gx", "gy", "pa"),
            P(None, "gx", "gy", "pa"),
        ),
        check_vma=False,
    )
```

```python
import functools

import jax
import jax.numpy as jnp
from jax import lax
from jax.experimental import pallas as pl
from jax.experimental.pallas import tpu as pltpu
from jax.sharding import PartitionSpec as P

CHEB = 16
LANES = 128
HALO = CHEB
TIME_STEP = 8.0
F32 = jnp.float32


def with_halo(cells, sides, width):
    for axis, dim in sides:
        count = lax.axis_size(axis)
        head = lax.slice_in_dim(cells, 0, width, axis=dim)
        tail = lax.slice_in_dim(cells, cells.shape[dim] - width, cells.shape[dim], axis=dim)
        cells = jnp.concatenate(
            [
                lax.ppermute(tail, axis, [(i, (i + 1) % count) for i in range(count)]),
                cells,
                lax.ppermute(head, axis, [((i + 1) % count, i) for i in range(count)]),
            ],
            axis=dim,
        )
    return cells


def region(arr, spatial, offset):
    extent = arr.shape[-3:]
    window = [slice(1, length - 1) for length in extent]
    window[spatial] = slice(offset, extent[spatial] - 2 + offset)
    leading = [slice(None)] * (arr.ndim - 3)
    return arr[tuple(leading + window)]


def apply_operator(padded, kpad):
    centre = region(padded, 0, 1)
    kcentre = region(kpad, 0, 1)
    summed = jnp.zeros_like(centre)
    for spatial in range(3):
        for offset in (0, 2):
            summed = summed + 0.5 * (kcentre + region(kpad, spatial, offset)) * (
                centre - region(padded, spatial, offset)
            )
    return centre + TIME_STEP * summed


def stepwise(conductivity, stored_state, row_scales, cotangent, upper_bound):
    upper = upper_bound[0]
    kpad = with_halo(conductivity, (("gx", 0), ("gy", 1), ("pa", 2)), 1)
    count = lax.axis_size("pa")
    partner = lax.ppermute(stored_state, "pa", [(i, (i + count // 2) % count) for i in range(count)])
    previous = partner.astype(F32) * row_scales[:, :, None]
    rhs = jnp.stack((previous, cotangent))
    theta = 0.5 * (upper + 1.0)
    delta = 0.5 * (upper - 1.0)
    sigma = theta / delta
    sides = (("gx", 1), ("gy", 2), ("pa", 3))

    def sweep(step, carry):
        solved, residual, direction, rho = carry
        padded = with_halo(direction, sides, 1)
        solved = solved + direction
        residual = residual - apply_operator(padded, kpad)
        rho_next = 1.0 / (2.0 * sigma - rho)
        direction = rho_next * rho * direction + 2.0 * rho_next / delta * residual
        return (solved, residual, direction, rho_next)

    start = (jnp.zeros_like(rhs), rhs, rhs / theta, 1.0 / sigma)
    solved, residual, _, _ = lax.fori_loop(0, CHEB, sweep, start)
    pair = with_halo(solved, sides, 1)
    centre = region(pair, 0, 1)
    summed = jnp.zeros_like(solved[0])
    for spatial in range(3):
        for offset in (0, 2):
            differ = centre - region(pair, spatial, offset)
            summed = summed + differ[0] * differ[1]
    return (-0.5 * TIME_STEP * summed, solved[1], solved[0], residual)


G = 4
BX = 8
BY = 128
BZ = 128
STRIP = BZ // G
TOP = 8 + HALO
ROWS = BY + 2 * TOP
EXTENDED = BY + 2 * HALO
GROUP = BY + 8
SIDES = 2 * GROUP
FIELD = SIDES + BY
KAP = FIELD + BY
BOTH = KAP + 16
TILE = 8
CHUNK = 32

BLOCK = (0, 3, 2, 1)
PLANES = BX


def roll(x, by):
    by %= LANES
    return pltpu.roll(x, by, 1) if by else x


def lanes_of(rows, strip):
    lane = lax.broadcasted_iota(jnp.int32, (rows, LANES), 1)
    return lax.rem(lane // STRIP - strip + 2 * G, G), lax.rem(lane, STRIP)


def pick(group, parts):
    out = parts[0]
    for b in range(1, G):
        out = jnp.where(group == b, parts[b], out)
    return out


def parity_order(transposed):
    src = lax.broadcasted_iota(jnp.int32, (LANES, LANES), 1 if transposed else 0)
    dst = lax.broadcasted_iota(jnp.int32, (LANES, LANES), 0 if transposed else 1)
    within = lax.rem(src, STRIP)
    place = src - within + 16 * lax.rem(within, 2) + within // 2
    return jnp.where(place == dst, 1.0, 0.0).astype(jnp.bfloat16)


def reorder(x, order):
    if x.dtype == jnp.bfloat16:
        return jnp.dot(x, order, preferred_element_type=F32)
    high = x.astype(jnp.bfloat16)
    rest = x - high.astype(F32)
    middle = rest.astype(jnp.bfloat16)
    low = (rest - middle.astype(F32)).astype(jnp.bfloat16)
    return (
        jnp.dot(high, order, preferred_element_type=F32)
        + jnp.dot(middle, order, preferred_element_type=F32)
        + jnp.dot(low, order, preferred_element_type=F32)
    )


def pack_kernel(strips, *refs):
    ins, outs = refs[: len(refs) - G], refs[len(refs) - G :]
    order = parity_order(False)
    groups = [lanes_of(BY, strips[d])[0] for d in range(G)]
    for n, array in enumerate(ins):
        for a in range(2):
            planes = reorder(array[4 * a : 4 * a + 4].reshape(4 * BY, LANES), order)
            parts = [roll(planes[BY * b : BY * (b + 1)], 32 * b) for b in range(4)]
            for d in range(G):
                outs[d][n, a] = pick(groups[d], parts)


def pack_previous_kernel(strips, both, above, below, *outs):
    src = lax.broadcasted_iota(jnp.int32, (2 * LANES, 2 * LANES), 0)
    dst = lax.broadcasted_iota(jnp.int32, (2 * LANES, 2 * LANES), 1)
    place = LANES * lax.rem(src, 2) + 64 * (src // LANES) + lax.rem(src, LANES) // 2
    order = jnp.where(place == dst, 1.0, 0.0).astype(jnp.bfloat16)

    def give(planes, rows, start):
        groups = [lanes_of(rows, strips[d])[0] for d in range(G)]
        for m in range(4):
            pieces = []
            for i in (2 * m, 2 * m + 1):
                pair = planes[rows * i : rows * (i + 1)]
                for e in range(2):
                    pieces.append(pair[:, LANES * e : LANES * (e + 1)])
            for d in range(G):
                turned = [pltpu.roll(pieces[k], lax.rem(16 * strips[d] + 32 * k + 8, LANES), 1) for k in range(4)]
                outs[d][m, pl.ds(start, rows)] = pick(groups[d], turned)

    @pl.loop(0, BY // CHUNK)
    def _(t):
        r = pl.multiple_of(CHUNK * t, CHUNK)
        halves = [both[half, :, pl.ds(r, CHUNK)].reshape(BX * CHUNK, LANES) for half in range(2)]
        give(reorder(jnp.concatenate(halves, axis=1), order), CHUNK, pl.multiple_of(HALO + CHUNK * t, HALO))

    for start, array in ((0, above), (HALO + BY, below)):
        halves = [array[half].reshape(BX * HALO, LANES) for half in range(2)]
        give(reorder(jnp.concatenate(halves, axis=1), order), HALO, start)


def edge_kernel(places, *refs):
    msgs, (to_left, to_right, head, tail) = refs[:G], refs[G:]
    lane = lax.broadcasted_iota(jnp.int32, (BY, LANES), 1)
    low = lax.rem(lane, 16) < 8
    for n in range(msgs[0].shape[0]):
        for d in range(G):
            first, second = msgs[d][n, 0], msgs[d][n, 1]
            to_left[n, places[0, d]] = jnp.where(low, first, roll(second, 8))
            to_right[n, places[1, d]] = jnp.where(low, roll(second, -8), first)
            for a in range(2):
                head[n, d, a] = msgs[d][n, a, :HALO]
                tail[n, d, a] = msgs[d][n, a, BY - HALO :]


def unpack(get_brick, get_edge, group, within, put):
    by_block = [BLOCK.index(q) for q in range(G)]
    edges = [[get_edge(side, d) for d in by_block] for side in range(2)]
    for a in range(2):
        far = 24 if a else 16
        own = [roll(get_brick(by_block[q], a), 32 * q) for q in range(G)]
        below = [roll(edges[0][q], 32 * q + far) for q in range(G)]
        above = [roll(edges[1][q], 32 * q - far) for q in range(G)]
        even = [
            jnp.where(within < 16, own[q], jnp.where(within < 24, above[q], below[(q + 1) % G])) for q in range(G)
        ]
        odd = [
            jnp.where(within < 8, above[(q - 1) % G], jnp.where(within < 16, below[q], own[q])) for q in range(G)
        ]
        for b in range(4):
            for e, parts in enumerate((even, odd)):
                whole = pick(group, [parts[(q - b) % G] for q in range(G)])
                put(4 * a + b, e, roll(whole, -32 * b - 16 * e))


def unpack_strip(get, group, put):
    by_block = [BLOCK.index(q) for q in range(G)]
    for m in range(4):
        turned = [roll(get(by_block[q], m), 32 * q) for q in range(G)]
        for k in range(4):
            whole = pick(group, [turned[(q - k) % G] for q in range(G)])
            put(2 * m + k // 2, k % 2, roll(whole, -32 * k - 8))


def solve_kernel(adjoint, strip, upper, *refs):
    if adjoint:
        bricks, (from_left, from_right, above, below, above_edge, below_edge) = refs[:G], refs[G : G + 6]
        outs, coefficients, (kap, *scratch) = refs[G + 6 : 2 * G + 6], refs[2 * G + 6 : 2 * G + 11], refs[2 * G + 11 :]
    else:
        strips_here, coefficients = refs[:G], refs[G : G + 5]
        outs, scratch = refs[G + 5 : 2 * G + 5], refs[2 * G + 5 :]
    kx, ky, kin, kout, diag = coefficients
    rhs, xa, xb, xc, turned, steps = scratch
    zero = jnp.zeros((TILE, LANES), F32)

    theta = 0.5 * (jnp.full((TILE, LANES), upper[0]) + 1.0)
    delta = 0.5 * (jnp.full((TILE, LANES), upper[0]) - 1.0)
    sigma = theta / delta
    rho = 1.0 / sigma
    for k in range(1, CHEB):
        rho_next = 1.0 / (2.0 * sigma - rho)
        steps[k, 0] = rho_next * rho
        steps[k, 1] = 2.0 * rho_next / delta
        rho = rho_next
    theta_inv = 1.0 / (0.5 * (jnp.full((2 * TILE, LANES), upper[0]) + 1.0))

    def put_at(dst, to, rows):
        def put(i, e, val):
            dst[i, e, pl.ds(to, rows)] = val

        return put

    for i in range(PLANES):
        for e in range(2):
            for dst in (rhs, xa, xb, xc) + ((kap, ky) if adjoint else ()):
                dst[i, e, 0:TILE] = zero
                dst[i, e, ROWS - TILE : ROWS] = zero
        for dst in (kin, kout) if adjoint else ():
            dst[i, 0:TILE] = zero
            dst[i, ROWS - TILE : ROWS] = zero

    if adjoint:
        sides, corners = (from_left, from_right), (above_edge, below_edge)

        @pl.loop(0, BY // CHUNK)
        def _(t):
            at = pl.ds(pl.multiple_of(CHUNK * t, CHUNK), CHUNK)
            group, within = lanes_of(CHUNK, strip[0])
            for n, dst in enumerate((kap, rhs)):
                unpack(
                    lambda d, a: bricks[d][n, a, at],
                    lambda side, d: sides[side][n, d, at],
                    group,
                    within,
                    put_at(dst, pl.multiple_of(TOP + CHUNK * t, TILE), CHUNK),
                )

        group_halo, within_halo = lanes_of(HALO, strip[0])
        for n, dst in enumerate((kap, rhs)):
            for brick, edge, start in ((above, above_edge, TOP - HALO), (below, below_edge, TOP + BY)):
                unpack(
                    lambda d, a: brick[n, d, a],
                    lambda side, d: edge[side, n, d],
                    group_halo,
                    within_halo,
                    put_at(dst, start, HALO),
                )
    else:

        @pl.loop(0, EXTENDED // CHUNK)
        def _(t):
            at = pl.ds(pl.multiple_of(CHUNK * t, CHUNK), CHUNK)
            group, _ = lanes_of(CHUNK, strip[0])
            unpack_strip(
                lambda d, m: strips_here[d][m, at],
                group,
                put_at(rhs, pl.multiple_of(TOP - HALO + CHUNK * t, TILE), CHUNK),
            )

    @pl.loop(0, (ROWS // TILE - 2) // 2)
    def _(t):
        rows = 2 * TILE
        r = pl.multiple_of(TILE + rows * t, TILE)
        at = pl.ds(r, rows)
        for i in range(PLANES):
            for e in range(2):
                xb[i, e, at] = rhs[i, e, at] * theta_inv
                xa[i, e, at] = jnp.zeros((rows, LANES), F32)
        if not adjoint:
            return
        first = [kap[0, e, at] for e in range(2)]
        now = first
        before = [4.0 * (k + roll(kap[PLANES - 1, e, at], 32)) for e, k in enumerate(first)]
        for i in range(PLANES):
            after = [kap[i + 1, e, at] if i + 1 < PLANES else roll(first[e], -32) for e in range(2)]
            inner = 4.0 * (now[0] + now[1])
            outer = 4.0 * (now[1] + roll(now[0], -1))
            outer_before = 4.0 * (now[0] + roll(now[1], 1))
            kin[i, at] = inner
            kout[i, at] = outer
            along = (inner + outer_before, inner + outer)
            for e in range(2):
                fx = 4.0 * (now[e] + after[e])
                fy = 4.0 * (now[e] + kap[i, e, pl.ds(r + 1, rows)])
                fym = 4.0 * (now[e] + kap[i, e, pl.ds(r - 1, rows)])
                kx[i, e, at] = fx
                ky[i, e, at] = fy
                diag[i, e, at] = 1.0 + (fx + before[e] + (fy + fym) + along[e])
                before[e] = fx
            now = after

    def turn_lanes(cur, r):
        at = pl.ds(r, TILE)
        for i in range(PLANES):
            turned[i, 0] = roll(kout[i, at] * cur[i, 1, at], 1)
            turned[i, 1] = roll(cur[i, 0, at], -1)
        for e in range(2):
            turned[PLANES, e] = roll(kx[PLANES - 1, e, at] * cur[PLANES - 1, e, at], 32)
            turned[PLANES + 1, e] = roll(cur[0, e, at], -32)

    def advance(alpha, beta, old, cur, new, r):
        at = pl.ds(r, TILE)
        now = [cur[0, e, at] for e in range(2)]
        before = fbefore = None
        for i in range(PLANES):
            fx = [kx[i, e, at] for e in range(2)]
            inner, outer = kin[i, at], kout[i, at]
            if i + 1 < PLANES:
                after = [cur[i + 1, e, at] for e in range(2)]
            else:
                after = [turned[PLANES + 1, e] for e in range(2)]
            for e in range(2):
                near = ky[i, e, at] * cur[i, e, pl.ds(r + 1, TILE)]
                near = near + ky[i, e, pl.ds(r - 1, TILE)] * cur[i, e, pl.ds(r - 1, TILE)]
                side = turned[i, e]
                near = near + (inner * now[1 - e] + (outer * side if e else side))
                behind = fbefore[e] * before[e] if i else turned[PLANES, e]
                near = near + (fx[e] * after[e] + behind)
                near = near + rhs[i, e, at]
                centre = (1.0 + alpha) - beta * diag[i, e, at]
                new[i, e, at] = centre * now[e] - alpha * old[i, e, at] + beta * near
            before, now, fbefore = now, after, fx

    def sweep(k, old, cur, new, span):
        alpha, beta = steps[k, 0], steps[k, 1]
        turn_lanes(cur, span[0])

        @pl.loop(0, span[1] // span[2])
        def _(t):
            for u in range(span[2]):
                r = pl.multiple_of(span[0] + TILE * (span[2] * t + u), TILE)
                advance(alpha, beta, old, cur, new, r)
                turn_lanes(cur, r + TILE)

    def three(k, spans):
        sweep(k, xa, xb, xc, spans[0])
        sweep(k + 1, xb, xc, xa, spans[1])
        sweep(k + 2, xc, xa, xb, spans[2])

    wide = (TILE, ROWS // TILE - 2, 4)
    narrow = (2 * TILE, ROWS // TILE - 4, 3)

    @pl.loop(0, 2)
    def _(m):
        three(1 + 3 * m, (wide,) * 3)

    three(7, (wide, narrow, narrow))

    @pl.loop(0, 2)
    def _(m):
        three(10 + 3 * m, (narrow,) * 3)

    def mains(whole, group, within):
        parts = [jnp.where(within < 16, even, roll(odd, 16)) for even, odd in whole]
        turned = [roll(parts[i], 32 * (i % 4)) for i in range(PLANES)]
        return parts, [
            [pick(group, [turned[4 * a + (q - d) % G] for q in range(G)]) for a in range(2)] for d in range(G)
        ]

    def beside(whole, parts, group, within):
        tree = [jnp.where(within == 31, odd, even) for even, odd in whole]
        for level in range(3):
            width = 1 << level
            keep = (lax.rem(within + 1, STRIP) < width) | ((within >= 16) & (within < 16 + width))
            tree = [jnp.where(keep, tree[j], roll(tree[j + 1], width)) for j in range(0, len(tree), 2)]
        ends = roll(tree[0], 1)
        groups = (ends, ends, roll(parts[PLANES - 1], 96), roll(parts[0], 64))
        return [pick(group, [groups[(q - d) % G] for q in range(G)]) for d in range(G)]

    def load(field, row, rows):
        return [[field[i, e, pl.ds(row, rows)] for e in range(2)] for i in range(PLANES)]

    @pl.loop(0, BY // CHUNK)
    def _(t):
        row = pl.multiple_of(TOP + CHUNK * t, TILE)
        group, within = lanes_of(CHUNK, strip[0])

        def to(start):
            return pl.ds(pl.multiple_of(start + CHUNK * t, TILE), CHUNK)

        for field, start in ((xb, SIDES),) + (((kap, FIELD),) if adjoint else ()):
            whole = load(field, row, CHUNK)
            parts, main = mains(whole, group, within)
            sides = beside(whole, parts, group, within)
            for d in range(G):
                outs[d][to(start)] = sides[d]
                if field is xb:
                    for a in range(2):
                        outs[d][to(GROUP * a)] = main[d][a]

    sub = lax.broadcasted_iota(jnp.int32, (TILE, LANES), 0)
    group, within = lanes_of(TILE, strip[0])
    for field in (xb, kap) if adjoint else (xb,):
        over = mains(load(field, TOP - TILE, TILE), group, within)[1]
        under = mains(load(field, TOP + BY, TILE), group, within)[1]
        for d in range(G):
            for a in range(2):
                to = GROUP * a + BY if field is xb else KAP + TILE * a
                outs[d][to : to + TILE] = jnp.where(
                    sub == 0, pltpu.roll(over[d][a], 1, 0), pltpu.roll(under[d][a], 1, 0)
                )


def collect(strips, msgs, padded, ends, base, own):
    order = parity_order(True)

    def owners(rows):
        return [lanes_of(rows, strips[d])[0] for d in range(G)]

    def choose(owner, parts, b):
        out = parts[0]
        for d in range(1, G):
            out = jnp.where(owner[d] == b, parts[d], out)
        return roll(out, -32 * b)

    def bricks(row, rows):
        return [roll(msgs[d][pl.ds(row, rows)], -32 * d) for d in range(G)]

    sides_at, tiles_at = (SIDES, (BY, GROUP + BY)) if own is None else (FIELD, (KAP, KAP + TILE))

    @pl.loop(0, BY // CHUNK)
    def _(t):
        to = pl.ds(pl.multiple_of(TILE + CHUNK * t, TILE), CHUNK)
        owner = owners(CHUNK)
        whole, places = [], []
        if own is None:
            for a in range(2):
                parts = bricks(pl.multiple_of(GROUP * a + CHUNK * t, TILE), CHUNK)
                whole += [choose(owner, parts, b) for b in range(4)]
                places += [1 + 4 * a + b for b in range(4)]
        else:
            for c in range(BX):
                padded[1 + c, to] = own[c, pl.ds(pl.multiple_of(CHUNK * t, CHUNK), CHUNK)]
        parts = bricks(pl.multiple_of(sides_at + CHUNK * t, TILE), CHUNK)
        for side, end in enumerate((0, G - 1)):
            val = parts[0]
            for d in range(1, G):
                val = jnp.where(strips[d] == end, parts[d], val)
            ends[side, pl.ds(pl.multiple_of(CHUNK * t, CHUNK), CHUNK)] = val
        whole += [choose(owner, parts, b) for b in (2, 3)]
        places += [0, 1 + BX]
        ordered = reorder(jnp.concatenate(whole, axis=0), order)
        for j, at in enumerate(places):
            padded[at, to] = ordered[CHUNK * j : CHUNK * (j + 1)]

    owner = owners(TILE)
    whole = []
    for a in range(2):
        parts = bricks(tiles_at[a], TILE)
        whole += [choose(owner, parts, b) for b in range(4)]
    ordered = reorder(jnp.concatenate(whole, axis=0), order)
    for c in range(BX):
        val = pltpu.roll(ordered[TILE * c : TILE * (c + 1)], 7, 0)
        padded[1 + c, 0:TILE] = val
        padded[1 + c, TILE + BY : 2 * TILE + BY] = val


def around_cell(padded, ends, c, t):
    lane = lax.broadcasted_iota(jnp.int32, (TILE, LANES), 1)
    r = pl.multiple_of(TILE * t, TILE)
    r8 = pl.multiple_of(TILE * t + TILE, TILE)
    cell = padded[1 + c, pl.ds(r8, TILE)]
    low, high = (ends[side, pl.ds(r, TILE)] for side in range(2))
    return cell, (
        padded[c, pl.ds(r8, TILE)],
        padded[c + 2, pl.ds(r8, TILE)],
        padded[1 + c, pl.ds(r8 - 1, TILE)],
        padded[1 + c, pl.ds(r8 + 1, TILE)],
        jnp.where(lane == 0, roll(low, -c), roll(cell, 1)),
        jnp.where(lane == LANES - 1, roll(high, 14 - c), roll(cell, -1)),
    )


def adjoint_kernel(strips, m0, m1, m2, m3, cond, cot, adjoint, residual, padded, ends, kap, kends):
    collect(strips, (m0, m1, m2, m3), padded, ends, 0, None)
    collect(strips, (m0, m1, m2, m3), kap, kends, 0, cond)

    @pl.loop(0, BY // TILE)
    def _(t):
        at = pl.ds(pl.multiple_of(TILE * t, TILE), TILE)
        for c in range(BX):
            k, knear = around_cell(kap, kends, c, t)
            x, xnear = around_cell(padded, ends, c, t)
            total = 0.0
            for kn, xn in zip(knear, xnear):
                total = total + (k + kn) * (x - xn)
            adjoint[c, at] = x
            residual[c, at] = cot[c, at] - (x + (0.5 * TIME_STEP) * total)


def state_kernel(strips, m0, m1, m2, m3, previous, adj, adj_ends, kap, kends, adj_residual, grad, state, residuals, padded, ends):
    collect(strips, (m0, m1, m2, m3), padded, ends, 0, None)

    @pl.loop(0, BY // TILE)
    def _(t):
        at = pl.ds(pl.multiple_of(TILE * t, TILE), TILE)
        for c in range(BX):
            k, knear = around_cell(kap, kends, c, t)
            x, xnear = around_cell(padded, ends, c, t)
            y, ynear = around_cell(adj, adj_ends, c, t)
            total = product = 0.0
            for kn, xn, yn in zip(knear, xnear, ynear):
                differ = x - xn
                total = total + (k + kn) * differ
                product = product + differ * (y - yn)
            grad[c, at] = (-0.5 * TIME_STEP) * product
            state[c, at] = x
            residuals[0, c, at] = previous[0, c, at] - (x + (0.5 * TIME_STEP) * total)
            residuals[1, c, at] = adj_residual[c, at]


def call(kernel, outs, smem, vmem, scratch=(), micros=2, mebibytes=16):
    vm = pl.BlockSpec(memory_space=pltpu.VMEM)
    sm = pl.BlockSpec(memory_space=pltpu.SMEM)
    return pl.pallas_call(
        kernel,
        out_shape=[jax.ShapeDtypeStruct(shape, F32) for shape in outs],
        in_specs=[sm] * len(smem) + [vm] * len(vmem),
        out_specs=[vm] * len(outs),
        scratch_shapes=[pltpu.VMEM(shape, F32) for shape in scratch],
        compiler_params=pltpu.CompilerParams(vmem_limit_bytes=mebibytes * 1024 * 1024),
        cost_estimate=pl.CostEstimate(flops=0, bytes_accessed=micros * 3_000_000, transcendentals=0),
    )(*smem, *vmem)


def shifted(x, axis, by):
    count = lax.axis_size(axis)
    return lax.ppermute(x, axis, [(i, (i + by) % count) for i in range(count)])


def around(x, by):
    order = [2 * g for g in range(G)] + [2 * g + 1 for g in reversed(range(G))]
    return lax.ppermute(x, ("gx", "pa"), [(at, order[(i + by) % len(order)]) for i, at in enumerate(order)])


def redistributed(conductivity, stored_state, row_scales, cotangent, upper_bound):
    g = lax.axis_index("gx")
    pa = lax.axis_index("pa")

    def strip_of(device):
        return jnp.where(pa == 0, device, G - 1 - device)

    steps = jnp.arange(G, dtype=jnp.int32)
    ahead = lax.rem(g + steps, G)
    behind = lax.rem(g - steps + G, G)
    strip = strip_of(g)
    left_g = jnp.where(pa == 0, jnp.maximum(g - 1, 0), jnp.minimum(g + 1, G - 1))
    right_g = jnp.where(pa == 0, jnp.minimum(g + 1, G - 1), jnp.maximum(g - 1, 0))
    places = lax.rem(jnp.stack((left_g - g + steps, right_g - g + steps)) + G, G)

    brick = (2, 2, BY, LANES)
    parts = call(pack_kernel, [brick] * G, [strip_of(ahead)], [conductivity, cotangent])
    parts, stored_state = lax.optimization_barrier((parts, stored_state))
    parts = [parts[0]] + [shifted(parts[d], "gx", d) for d in range(1, G)]
    stored = shifted(stored_state, "pa", 1)
    both = jnp.stack((stored, stored_state)).astype(F32) * row_scales[:, :, None]
    above = shifted(both[:, :, BY - HALO :], "gy", 1)
    below = shifted(both[:, :, :HALO], "gy", -1)
    messages = call(
        pack_previous_kernel,
        [(4, EXTENDED, LANES)] * G,
        [strip_of(ahead)],
        [both, above, below],
    )
    parts, messages = lax.optimization_barrier((parts, messages))
    edge = (2, G, BY, LANES)
    rim = (2, G, 2, HALO, LANES)
    to_left, to_right, head, tail = call(edge_kernel, [edge, edge, rim, rim], [places], parts)
    from_left, from_right = around(to_right, 1), around(to_left, -1)
    above, below = shifted(tail, "gy", 1), shifted(head, "gy", -1)
    edges = [jnp.stack((from_left[:, :, at], from_right[:, :, at])) for at in (slice(BY - HALO, BY), slice(0, HALO))]
    halos = [from_left, from_right, above, below, shifted(edges[0], "gy", 1), shifted(edges[1], "gy", -1)]
    messages, halos = lax.optimization_barrier((messages, halos))
    second = [messages[0]] + [shifted(messages[d], "gx", d) for d in range(1, G)]

    line = (PLANES, 2, ROWS, LANES)
    half = (PLANES, ROWS, LANES)
    lines = [line] * 4 + [(PLANES + 2, 2, TILE, LANES), (CHEB, 2, TILE, LANES)]
    setup = [strip[None], upper_bound]

    def home(solved):
        return [solved[0]] + [shifted(solved[d], "gx", d) for d in range(1, G)]

    *solved_adjoint, kx, ky, kin, kout, diag = call(
        functools.partial(solve_kernel, True),
        [(BOTH, LANES)] * G + [line, line, half, half, line],
        setup,
        [*parts, *halos],
        [line] + lines,
        micros=25,
        mebibytes=24,
    )
    solved_adjoint = home(solved_adjoint)
    solved_state = home(
        call(
            functools.partial(solve_kernel, False),
            [(FIELD, LANES)] * G,
            setup,
            [*second, kx, ky, kin, kout, diag],
            lines,
            micros=25,
            mebibytes=24,
        )
    )

    out = (BX, BY, LANES)
    padded = (BX + 2, BY + 16, LANES)
    ends = (2, BY, LANES)
    here = strip_of(behind)
    adjoint, adj_residual, adj, adj_ends, kap, kends = call(
        adjoint_kernel,
        [out, out, padded, ends, padded, ends],
        [here],
        [*solved_adjoint, conductivity, cotangent],
    )
    grad, state, residuals = call(
        state_kernel,
        [out, out, (2,) + out],
        [here],
        [*solved_state, both, adj, adj_ends, kap, kends, adj_residual],
        [padded, ends],
    )
    return grad, adjoint, state, residuals


def body(conductivity, stored_state, row_scales, cotangent, upper_bound):
    strips_fit = (
        lax.axis_size("gx") == G
        and lax.axis_size("pa") == 2
        and conductivity.shape == (BX, BY, BZ)
    )
    run = redistributed if strips_fit else stepwise
    return tuple(run(conductivity, stored_state, row_scales, cotangent, upper_bound))


def solution(mesh):
    return jax.shard_map(
        body,
        mesh=mesh,
        in_specs=(
            P("gx", "gy", "pa"),
            P("gx", "gy", "pa"),
            P("gx", "gy"),
            P("gx", "gy", "pa"),
            P(),
        ),
        out_specs=(
            P("gx", "gy", "pa"),
            P("gx", "gy", "pa"),
            P("gx", "gy", "pa"),
            P(None, "gx", "gy", "pa"),
        ),
        check_vma=False,
    )
```

```python
import functools

import jax
import jax.numpy as jnp
from jax import lax
from jax.experimental import pallas as pl
from jax.experimental.pallas import tpu as pltpu
from jax.sharding import PartitionSpec as P

CHEB = 16
LANES = 128
HALO = CHEB
TIME_STEP = 8.0
F32 = jnp.float32


def with_halo(cells, sides, width):
    for axis, dim in sides:
        count = lax.axis_size(axis)
        head = lax.slice_in_dim(cells, 0, width, axis=dim)
        tail = lax.slice_in_dim(cells, cells.shape[dim] - width, cells.shape[dim], axis=dim)
        cells = jnp.concatenate(
            [
                lax.ppermute(tail, axis, [(i, (i + 1) % count) for i in range(count)]),
                cells,
                lax.ppermute(head, axis, [((i + 1) % count, i) for i in range(count)]),
            ],
            axis=dim,
        )
    return cells


def region(arr, spatial, offset):
    extent = arr.shape[-3:]
    window = [slice(1, length - 1) for length in extent]
    window[spatial] = slice(offset, extent[spatial] - 2 + offset)
    leading = [slice(None)] * (arr.ndim - 3)
    return arr[tuple(leading + window)]


def apply_operator(padded, kpad):
    centre = region(padded, 0, 1)
    kcentre = region(kpad, 0, 1)
    summed = jnp.zeros_like(centre)
    for spatial in range(3):
        for offset in (0, 2):
            summed = summed + 0.5 * (kcentre + region(kpad, spatial, offset)) * (
                centre - region(padded, spatial, offset)
            )
    return centre + TIME_STEP * summed


def stepwise(conductivity, stored_state, row_scales, cotangent, upper_bound):
    upper = upper_bound[0]
    kpad = with_halo(conductivity, (("gx", 0), ("gy", 1), ("pa", 2)), 1)
    count = lax.axis_size("pa")
    partner = lax.ppermute(stored_state, "pa", [(i, (i + count // 2) % count) for i in range(count)])
    previous = partner.astype(F32) * row_scales[:, :, None]
    rhs = jnp.stack((previous, cotangent))
    theta = 0.5 * (upper + 1.0)
    delta = 0.5 * (upper - 1.0)
    sigma = theta / delta
    sides = (("gx", 1), ("gy", 2), ("pa", 3))

    def sweep(step, carry):
        solved, residual, direction, rho = carry
        padded = with_halo(direction, sides, 1)
        solved = solved + direction
        residual = residual - apply_operator(padded, kpad)
        rho_next = 1.0 / (2.0 * sigma - rho)
        direction = rho_next * rho * direction + 2.0 * rho_next / delta * residual
        return (solved, residual, direction, rho_next)

    start = (jnp.zeros_like(rhs), rhs, rhs / theta, 1.0 / sigma)
    solved, residual, _, _ = lax.fori_loop(0, CHEB, sweep, start)
    pair = with_halo(solved, sides, 1)
    centre = region(pair, 0, 1)
    summed = jnp.zeros_like(solved[0])
    for spatial in range(3):
        for offset in (0, 2):
            differ = centre - region(pair, spatial, offset)
            summed = summed + differ[0] * differ[1]
    return (-0.5 * TIME_STEP * summed, solved[1], solved[0], residual)


G = 4
BX = 8
BY = 128
BZ = 128
STRIP = BZ // G
TOP = 8 + HALO
ROWS = BY + 2 * TOP
EXTENDED = BY + 2 * HALO
GROUP = BY + 8
SIDES = 2 * GROUP
FIELD = SIDES + BY
KAP = FIELD + BY
BOTH = KAP + 16
TILE = 8
CHUNK = 32

BLOCK = (0, 3, 2, 1)
PLANES = BX


def roll(x, by):
    by %= LANES
    return pltpu.roll(x, by, 1) if by else x


def lanes_of(rows, strip):
    lane = lax.broadcasted_iota(jnp.int32, (rows, LANES), 1)
    return lax.rem(lane // STRIP - strip + 2 * G, G), lax.rem(lane, STRIP)


def pick(group, parts):
    out = parts[0]
    for b in range(1, G):
        out = jnp.where(group == b, parts[b], out)
    return out


def parity_order(transposed):
    src = lax.broadcasted_iota(jnp.int32, (LANES, LANES), 1 if transposed else 0)
    dst = lax.broadcasted_iota(jnp.int32, (LANES, LANES), 0 if transposed else 1)
    within = lax.rem(src, STRIP)
    place = src - within + 16 * lax.rem(within, 2) + within // 2
    return jnp.where(place == dst, 1.0, 0.0).astype(jnp.bfloat16)


def reorder(x, order):
    if x.dtype == jnp.bfloat16:
        return jnp.dot(x, order, preferred_element_type=F32)
    high = x.astype(jnp.bfloat16)
    rest = x - high.astype(F32)
    middle = rest.astype(jnp.bfloat16)
    low = (rest - middle.astype(F32)).astype(jnp.bfloat16)
    return (
        jnp.dot(high, order, preferred_element_type=F32)
        + jnp.dot(middle, order, preferred_element_type=F32)
        + jnp.dot(low, order, preferred_element_type=F32)
    )


def pack_kernel(strips, *refs):
    ins, outs = refs[: len(refs) - G], refs[len(refs) - G :]
    order = parity_order(False)
    groups = [lanes_of(BY, strips[d])[0] for d in range(G)]
    for n, array in enumerate(ins):
        for a in range(2):
            planes = reorder(array[4 * a : 4 * a + 4].reshape(4 * BY, LANES), order)
            parts = [roll(planes[BY * b : BY * (b + 1)], 32 * b) for b in range(4)]
            for d in range(G):
                outs[d][n, a] = pick(groups[d], parts)


def pack_previous_kernel(strips, both, above, below, *outs):
    src = lax.broadcasted_iota(jnp.int32, (2 * LANES, 2 * LANES), 0)
    dst = lax.broadcasted_iota(jnp.int32, (2 * LANES, 2 * LANES), 1)
    place = LANES * lax.rem(src, 2) + 64 * (src // LANES) + lax.rem(src, LANES) // 2
    order = jnp.where(place == dst, 1.0, 0.0).astype(jnp.bfloat16)

    def give(planes, rows, start):
        groups = [lanes_of(rows, strips[d])[0] for d in range(G)]
        for m in range(4):
            pieces = []
            for i in (2 * m, 2 * m + 1):
                pair = planes[rows * i : rows * (i + 1)]
                for e in range(2):
                    pieces.append(pair[:, LANES * e : LANES * (e + 1)])
            for d in range(G):
                turned = [pltpu.roll(pieces[k], lax.rem(16 * strips[d] + 32 * k + 8, LANES), 1) for k in range(4)]
                outs[d][m, pl.ds(start, rows)] = pick(groups[d], turned)

    @pl.loop(0, BY // CHUNK)
    def _(t):
        r = pl.multiple_of(CHUNK * t, CHUNK)
        halves = [both[half, :, pl.ds(r, CHUNK)].reshape(BX * CHUNK, LANES) for half in range(2)]
        give(reorder(jnp.concatenate(halves, axis=1), order), CHUNK, pl.multiple_of(HALO + CHUNK * t, HALO))

    for start, array in ((0, above), (HALO + BY, below)):
        halves = [array[half].reshape(BX * HALO, LANES) for half in range(2)]
        give(reorder(jnp.concatenate(halves, axis=1), order), HALO, start)


def edge_kernel(places, *refs):
    msgs, (to_left, to_right, head, tail) = refs[:G], refs[G:]
    lane = lax.broadcasted_iota(jnp.int32, (BY, LANES), 1)
    low = lax.rem(lane, 16) < 8
    for n in range(msgs[0].shape[0]):
        for d in range(G):
            first, second = msgs[d][n, 0], msgs[d][n, 1]
            to_left[n, places[0, d]] = jnp.where(low, first, roll(second, 8))
            to_right[n, places[1, d]] = jnp.where(low, roll(second, -8), first)
            for a in range(2):
                head[n, d, a] = msgs[d][n, a, :HALO]
                tail[n, d, a] = msgs[d][n, a, BY - HALO :]


def unpack(get_brick, get_edge, group, within, put):
    by_block = [BLOCK.index(q) for q in range(G)]
    edges = [[get_edge(side, d) for d in by_block] for side in range(2)]
    for a in range(2):
        far = 24 if a else 16
        own = [roll(get_brick(by_block[q], a), 32 * q) for q in range(G)]
        below = [roll(edges[0][q], 32 * q + far) for q in range(G)]
        above = [roll(edges[1][q], 32 * q - far) for q in range(G)]
        even = [
            jnp.where(within < 16, own[q], jnp.where(within < 24, above[q], below[(q + 1) % G])) for q in range(G)
        ]
        odd = [
            jnp.where(within < 8, above[(q - 1) % G], jnp.where(within < 16, below[q], own[q])) for q in range(G)
        ]
        for b in range(4):
            for e, parts in enumerate((even, odd)):
                whole = pick(group, [parts[(q - b) % G] for q in range(G)])
                put(4 * a + b, e, roll(whole, -32 * b - 16 * e))


def unpack_strip(get, group, put):
    by_block = [BLOCK.index(q) for q in range(G)]
    for m in range(4):
        turned = [roll(get(by_block[q], m), 32 * q) for q in range(G)]
        for k in range(4):
            whole = pick(group, [turned[(q - k) % G] for q in range(G)])
            put(2 * m + k // 2, k % 2, roll(whole, -32 * k - 8))


def solve_kernel(adjoint, strip, upper, *refs):
    if adjoint:
        bricks, (from_left, from_right, above, below, above_edge, below_edge) = refs[:G], refs[G : G + 6]
        outs, coefficients, (kap, *scratch) = refs[G + 6 : 2 * G + 6], refs[2 * G + 6 : 2 * G + 11], refs[2 * G + 11 :]
    else:
        strips_here, coefficients = refs[:G], refs[G : G + 5]
        outs, scratch = refs[G + 5 : 2 * G + 5], refs[2 * G + 5 :]
    kx, ky, kin, kout, diag = coefficients
    rhs, xa, xb, xc, turned, steps = scratch
    zero = jnp.zeros((TILE, LANES), F32)

    theta = 0.5 * (jnp.full((TILE, LANES), upper[0]) + 1.0)
    delta = 0.5 * (jnp.full((TILE, LANES), upper[0]) - 1.0)
    sigma = theta / delta
    rho = 1.0 / sigma
    for k in range(1, CHEB):
        rho_next = 1.0 / (2.0 * sigma - rho)
        steps[k, 0] = rho_next * rho
        steps[k, 1] = 2.0 * rho_next / delta
        rho = rho_next
    theta_inv = 1.0 / (0.5 * (jnp.full((2 * TILE, LANES), upper[0]) + 1.0))

    def put_at(dst, to, rows):
        def put(i, e, val):
            dst[i, e, pl.ds(to, rows)] = val

        return put

    for i in range(PLANES):
        for e in range(2):
            for dst in (rhs, xa, xb, xc) + ((kap, ky) if adjoint else ()):
                dst[i, e, 0:TILE] = zero
                dst[i, e, ROWS - TILE : ROWS] = zero
        for dst in (kin, kout) if adjoint else ():
            dst[i, 0:TILE] = zero
            dst[i, ROWS - TILE : ROWS] = zero

    if adjoint:
        sides, corners = (from_left, from_right), (above_edge, below_edge)

        @pl.loop(0, BY // CHUNK)
        def _(t):
            at = pl.ds(pl.multiple_of(CHUNK * t, CHUNK), CHUNK)
            group, within = lanes_of(CHUNK, strip[0])
            for n, dst in enumerate((kap, rhs)):
                unpack(
                    lambda d, a: bricks[d][n, a, at],
                    lambda side, d: sides[side][n, d, at],
                    group,
                    within,
                    put_at(dst, pl.multiple_of(TOP + CHUNK * t, TILE), CHUNK),
                )

        group_halo, within_halo = lanes_of(HALO, strip[0])
        for n, dst in enumerate((kap, rhs)):
            for brick, edge, start in ((above, above_edge, TOP - HALO), (below, below_edge, TOP + BY)):
                unpack(
                    lambda d, a: brick[n, d, a],
                    lambda side, d: edge[side, n, d],
                    group_halo,
                    within_halo,
                    put_at(dst, start, HALO),
                )
    else:

        @pl.loop(0, EXTENDED // CHUNK)
        def _(t):
            at = pl.ds(pl.multiple_of(CHUNK * t, CHUNK), CHUNK)
            group, _ = lanes_of(CHUNK, strip[0])
            unpack_strip(
                lambda d, m: strips_here[d][m, at],
                group,
                put_at(rhs, pl.multiple_of(TOP - HALO + CHUNK * t, TILE), CHUNK),
            )

    @pl.loop(0, (ROWS // TILE - 2) // 2)
    def _(t):
        rows = 2 * TILE
        r = pl.multiple_of(TILE + rows * t, TILE)
        at = pl.ds(r, rows)
        for i in range(PLANES):
            for e in range(2):
                xb[i, e, at] = rhs[i, e, at] * theta_inv
                xa[i, e, at] = jnp.zeros((rows, LANES), F32)
        if not adjoint:
            return
        first = [kap[0, e, at] for e in range(2)]
        now = first
        before = [4.0 * (k + roll(kap[PLANES - 1, e, at], 32)) for e, k in enumerate(first)]
        for i in range(PLANES):
            after = [kap[i + 1, e, at] if i + 1 < PLANES else roll(first[e], -32) for e in range(2)]
            inner = 4.0 * (now[0] + now[1])
            outer = 4.0 * (now[1] + roll(now[0], -1))
            outer_before = 4.0 * (now[0] + roll(now[1], 1))
            kin[i, at] = inner
            kout[i, at] = outer
            along = (inner + outer_before, inner + outer)
            for e in range(2):
                fx = 4.0 * (now[e] + after[e])
                fy = 4.0 * (now[e] + kap[i, e, pl.ds(r + 1, rows)])
                fym = 4.0 * (now[e] + kap[i, e, pl.ds(r - 1, rows)])
                kx[i, e, at] = fx
                ky[i, e, at] = fy
                diag[i, e, at] = 1.0 + (fx + before[e] + (fy + fym) + along[e])
                before[e] = fx
            now = after

    def turn_lanes(cur, r):
        at = pl.ds(r, TILE)
        for i in range(PLANES):
            turned[i, 0] = roll(kout[i, at] * cur[i, 1, at], 1)
            turned[i, 1] = roll(cur[i, 0, at], -1)
        for e in range(2):
            turned[PLANES, e] = roll(kx[PLANES - 1, e, at] * cur[PLANES - 1, e, at], 32)
            turned[PLANES + 1, e] = roll(cur[0, e, at], -32)

    def advance(alpha, beta, old, cur, new, r):
        at = pl.ds(r, TILE)
        now = [cur[0, e, at] for e in range(2)]
        before = fbefore = None
        for i in range(PLANES):
            fx = [kx[i, e, at] for e in range(2)]
            inner, outer = kin[i, at], kout[i, at]
            if i + 1 < PLANES:
                after = [cur[i + 1, e, at] for e in range(2)]
            else:
                after = [turned[PLANES + 1, e] for e in range(2)]
            for e in range(2):
                near = ky[i, e, at] * cur[i, e, pl.ds(r + 1, TILE)]
                near = near + ky[i, e, pl.ds(r - 1, TILE)] * cur[i, e, pl.ds(r - 1, TILE)]
                side = turned[i, e]
                near = near + (inner * now[1 - e] + (outer * side if e else side))
                behind = fbefore[e] * before[e] if i else turned[PLANES, e]
                near = near + (fx[e] * after[e] + behind)
                near = near + rhs[i, e, at]
                centre = (1.0 + alpha) - beta * diag[i, e, at]
                new[i, e, at] = centre * now[e] - alpha * old[i, e, at] + beta * near
            before, now, fbefore = now, after, fx

    def sweep(k, old, cur, new, span):
        alpha, beta = steps[k, 0], steps[k, 1]
        turn_lanes(cur, span[0])

        @pl.loop(0, span[1] // span[2])
        def _(t):
            for u in range(span[2]):
                r = pl.multiple_of(span[0] + TILE * (span[2] * t + u), TILE)
                advance(alpha, beta, old, cur, new, r)
                turn_lanes(cur, r + TILE)

    def three(k, spans):
        sweep(k, xa, xb, xc, spans[0])
        sweep(k + 1, xb, xc, xa, spans[1])
        sweep(k + 2, xc, xa, xb, spans[2])

    wide = (TILE, ROWS // TILE - 2, ROWS // TILE - 2)
    narrow = (2 * TILE, ROWS // TILE - 4, ROWS // TILE - 4)

    @pl.loop(0, 2)
    def _(m):
        three(1 + 3 * m, (wide,) * 3)

    three(7, (wide, narrow, narrow))

    @pl.loop(0, 2)
    def _(m):
        three(10 + 3 * m, (narrow,) * 3)

    def mains(whole, group, within):
        parts = [jnp.where(within < 16, even, roll(odd, 16)) for even, odd in whole]
        turned = [roll(parts[i], 32 * (i % 4)) for i in range(PLANES)]
        return parts, [
            [pick(group, [turned[4 * a + (q - d) % G] for q in range(G)]) for a in range(2)] for d in range(G)
        ]

    def beside(whole, parts, group, within):
        tree = [jnp.where(within == 31, odd, even) for even, odd in whole]
        for level in range(3):
            width = 1 << level
            keep = (lax.rem(within + 1, STRIP) < width) | ((within >= 16) & (within < 16 + width))
            tree = [jnp.where(keep, tree[j], roll(tree[j + 1], width)) for j in range(0, len(tree), 2)]
        ends = roll(tree[0], 1)
        groups = (ends, ends, roll(parts[PLANES - 1], 96), roll(parts[0], 64))
        return [pick(group, [groups[(q - d) % G] for q in range(G)]) for d in range(G)]

    def load(field, row, rows):
        return [[field[i, e, pl.ds(row, rows)] for e in range(2)] for i in range(PLANES)]

    @pl.loop(0, BY // CHUNK)
    def _(t):
        row = pl.multiple_of(TOP + CHUNK * t, TILE)
        group, within = lanes_of(CHUNK, strip[0])

        def to(start):
            return pl.ds(pl.multiple_of(start + CHUNK * t, TILE), CHUNK)

        for field, start in ((xb, SIDES),) + (((kap, FIELD),) if adjoint else ()):
            whole = load(field, row, CHUNK)
            parts, main = mains(whole, group, within)
            sides = beside(whole, parts, group, within)
            for d in range(G):
                outs[d][to(start)] = sides[d]
                if field is xb:
                    for a in range(2):
                        outs[d][to(GROUP * a)] = main[d][a]

    sub = lax.broadcasted_iota(jnp.int32, (TILE, LANES), 0)
    group, within = lanes_of(TILE, strip[0])
    for field in (xb, kap) if adjoint else (xb,):
        over = mains(load(field, TOP - TILE, TILE), group, within)[1]
        under = mains(load(field, TOP + BY, TILE), group, within)[1]
        for d in range(G):
            for a in range(2):
                to = GROUP * a + BY if field is xb else KAP + TILE * a
                outs[d][to : to + TILE] = jnp.where(
                    sub == 0, pltpu.roll(over[d][a], 1, 0), pltpu.roll(under[d][a], 1, 0)
                )


def collect(strips, msgs, padded, ends, base, own):
    order = parity_order(True)

    def owners(rows):
        return [lanes_of(rows, strips[d])[0] for d in range(G)]

    def choose(owner, parts, b):
        out = parts[0]
        for d in range(1, G):
            out = jnp.where(owner[d] == b, parts[d], out)
        return roll(out, -32 * b)

    def bricks(row, rows):
        return [roll(msgs[d][pl.ds(row, rows)], -32 * d) for d in range(G)]

    sides_at, tiles_at = (SIDES, (BY, GROUP + BY)) if own is None else (FIELD, (KAP, KAP + TILE))

    @pl.loop(0, BY // CHUNK)
    def _(t):
        to = pl.ds(pl.multiple_of(TILE + CHUNK * t, TILE), CHUNK)
        owner = owners(CHUNK)
        whole, places = [], []
        if own is None:
            for a in range(2):
                parts = bricks(pl.multiple_of(GROUP * a + CHUNK * t, TILE), CHUNK)
                whole += [choose(owner, parts, b) for b in range(4)]
                places += [1 + 4 * a + b for b in range(4)]
        else:
            for c in range(BX):
                padded[1 + c, to] = own[c, pl.ds(pl.multiple_of(CHUNK * t, CHUNK), CHUNK)]
        parts = bricks(pl.multiple_of(sides_at + CHUNK * t, TILE), CHUNK)
        for side, end in enumerate((0, G - 1)):
            val = parts[0]
            for d in range(1, G):
                val = jnp.where(strips[d] == end, parts[d], val)
            ends[side, pl.ds(pl.multiple_of(CHUNK * t, CHUNK), CHUNK)] = val
        whole += [choose(owner, parts, b) for b in (2, 3)]
        places += [0, 1 + BX]
        ordered = reorder(jnp.concatenate(whole, axis=0), order)
        for j, at in enumerate(places):
            padded[at, to] = ordered[CHUNK * j : CHUNK * (j + 1)]

    owner = owners(TILE)
    whole = []
    for a in range(2):
        parts = bricks(tiles_at[a], TILE)
        whole += [choose(owner, parts, b) for b in range(4)]
    ordered = reorder(jnp.concatenate(whole, axis=0), order)
    for c in range(BX):
        val = pltpu.roll(ordered[TILE * c : TILE * (c + 1)], 7, 0)
        padded[1 + c, 0:TILE] = val
        padded[1 + c, TILE + BY : 2 * TILE + BY] = val


def around_cell(padded, ends, c, t):
    lane = lax.broadcasted_iota(jnp.int32, (TILE, LANES), 1)
    r = pl.multiple_of(TILE * t, TILE)
    r8 = pl.multiple_of(TILE * t + TILE, TILE)
    cell = padded[1 + c, pl.ds(r8, TILE)]
    low, high = (ends[side, pl.ds(r, TILE)] for side in range(2))
    return cell, (
        padded[c, pl.ds(r8, TILE)],
        padded[c + 2, pl.ds(r8, TILE)],
        padded[1 + c, pl.ds(r8 - 1, TILE)],
        padded[1 + c, pl.ds(r8 + 1, TILE)],
        jnp.where(lane == 0, roll(low, -c), roll(cell, 1)),
        jnp.where(lane == LANES - 1, roll(high, 14 - c), roll(cell, -1)),
    )


def adjoint_kernel(strips, m0, m1, m2, m3, cond, cot, adjoint, residual, padded, ends, kap, kends):
    collect(strips, (m0, m1, m2, m3), padded, ends, 0, None)
    collect(strips, (m0, m1, m2, m3), kap, kends, 0, cond)

    @pl.loop(0, BY // TILE)
    def _(t):
        at = pl.ds(pl.multiple_of(TILE * t, TILE), TILE)
        for c in range(BX):
            k, knear = around_cell(kap, kends, c, t)
            x, xnear = around_cell(padded, ends, c, t)
            total = 0.0
            for kn, xn in zip(knear, xnear):
                total = total + (k + kn) * (x - xn)
            adjoint[c, at] = x
            residual[c, at] = cot[c, at] - (x + (0.5 * TIME_STEP) * total)


def state_kernel(strips, m0, m1, m2, m3, previous, adj, adj_ends, kap, kends, adj_residual, grad, state, residuals, padded, ends):
    collect(strips, (m0, m1, m2, m3), padded, ends, 0, None)

    @pl.loop(0, BY // TILE)
    def _(t):
        at = pl.ds(pl.multiple_of(TILE * t, TILE), TILE)
        for c in range(BX):
            k, knear = around_cell(kap, kends, c, t)
            x, xnear = around_cell(padded, ends, c, t)
            y, ynear = around_cell(adj, adj_ends, c, t)
            total = product = 0.0
            for kn, xn, yn in zip(knear, xnear, ynear):
                differ = x - xn
                total = total + (k + kn) * differ
                product = product + differ * (y - yn)
            grad[c, at] = (-0.5 * TIME_STEP) * product
            state[c, at] = x
            residuals[0, c, at] = previous[0, c, at] - (x + (0.5 * TIME_STEP) * total)
            residuals[1, c, at] = adj_residual[c, at]


def call(kernel, outs, smem, vmem, scratch=(), micros=2, mebibytes=16):
    vm = pl.BlockSpec(memory_space=pltpu.VMEM)
    sm = pl.BlockSpec(memory_space=pltpu.SMEM)
    return pl.pallas_call(
        kernel,
        out_shape=[jax.ShapeDtypeStruct(shape, F32) for shape in outs],
        in_specs=[sm] * len(smem) + [vm] * len(vmem),
        out_specs=[vm] * len(outs),
        scratch_shapes=[pltpu.VMEM(shape, F32) for shape in scratch],
        compiler_params=pltpu.CompilerParams(vmem_limit_bytes=mebibytes * 1024 * 1024),
        cost_estimate=pl.CostEstimate(flops=0, bytes_accessed=micros * 3_000_000, transcendentals=0),
    )(*smem, *vmem)


def shifted(x, axis, by):
    count = lax.axis_size(axis)
    return lax.ppermute(x, axis, [(i, (i + by) % count) for i in range(count)])


def around(x, by):
    order = [2 * g for g in range(G)] + [2 * g + 1 for g in reversed(range(G))]
    return lax.ppermute(x, ("gx", "pa"), [(at, order[(i + by) % len(order)]) for i, at in enumerate(order)])


def redistributed(conductivity, stored_state, row_scales, cotangent, upper_bound):
    g = lax.axis_index("gx")
    pa = lax.axis_index("pa")

    def strip_of(device):
        return jnp.where(pa == 0, device, G - 1 - device)

    steps = jnp.arange(G, dtype=jnp.int32)
    ahead = lax.rem(g + steps, G)
    behind = lax.rem(g - steps + G, G)
    strip = strip_of(g)
    left_g = jnp.where(pa == 0, jnp.maximum(g - 1, 0), jnp.minimum(g + 1, G - 1))
    right_g = jnp.where(pa == 0, jnp.minimum(g + 1, G - 1), jnp.maximum(g - 1, 0))
    places = lax.rem(jnp.stack((left_g - g + steps, right_g - g + steps)) + G, G)

    brick = (2, 2, BY, LANES)
    parts = call(pack_kernel, [brick] * G, [strip_of(ahead)], [conductivity, cotangent])
    parts, stored_state = lax.optimization_barrier((parts, stored_state))
    parts = [parts[0]] + [shifted(parts[d], "gx", d) for d in range(1, G)]
    stored = shifted(stored_state, "pa", 1)
    both = jnp.stack((stored, stored_state)).astype(F32) * row_scales[:, :, None]
    above = shifted(both[:, :, BY - HALO :], "gy", 1)
    below = shifted(both[:, :, :HALO], "gy", -1)
    messages = call(
        pack_previous_kernel,
        [(4, EXTENDED, LANES)] * G,
        [strip_of(ahead)],
        [both, above, below],
    )
    parts, messages = lax.optimization_barrier((parts, messages))
    edge = (2, G, BY, LANES)
    rim = (2, G, 2, HALO, LANES)
    to_left, to_right, head, tail = call(edge_kernel, [edge, edge, rim, rim], [places], parts)
    from_left, from_right = around(to_right, 1), around(to_left, -1)
    above, below = shifted(tail, "gy", 1), shifted(head, "gy", -1)
    edges = [jnp.stack((from_left[:, :, at], from_right[:, :, at])) for at in (slice(BY - HALO, BY), slice(0, HALO))]
    halos = [from_left, from_right, above, below, shifted(edges[0], "gy", 1), shifted(edges[1], "gy", -1)]
    messages, halos[0] = lax.optimization_barrier((messages, halos[0]))
    second = [messages[0]] + [shifted(messages[d], "gx", d) for d in range(1, G)]

    line = (PLANES, 2, ROWS, LANES)
    half = (PLANES, ROWS, LANES)
    lines = [line] * 4 + [(PLANES + 2, 2, TILE, LANES), (CHEB, 2, TILE, LANES)]
    setup = [strip[None], upper_bound]

    def home(solved):
        return [solved[0]] + [shifted(solved[d], "gx", d) for d in range(1, G)]

    *solved_adjoint, kx, ky, kin, kout, diag = call(
        functools.partial(solve_kernel, True),
        [(BOTH, LANES)] * G + [line, line, half, half, line],
        setup,
        [*parts, *halos],
        [line] + lines,
        micros=25,
        mebibytes=24,
    )
    solved_adjoint = home(solved_adjoint)
    solved_state = home(
        call(
            functools.partial(solve_kernel, False),
            [(FIELD, LANES)] * G,
            setup,
            [*second, kx, ky, kin, kout, diag],
            lines,
            micros=25,
            mebibytes=24,
        )
    )

    out = (BX, BY, LANES)
    padded = (BX + 2, BY + 16, LANES)
    ends = (2, BY, LANES)
    here = strip_of(behind)
    adjoint, adj_residual, adj, adj_ends, kap, kends = call(
        adjoint_kernel,
        [out, out, padded, ends, padded, ends],
        [here],
        [*solved_adjoint, conductivity, cotangent],
    )
    grad, state, residuals = call(
        state_kernel,
        [out, out, (2,) + out],
        [here],
        [*solved_state, both, adj, adj_ends, kap, kends, adj_residual],
        [padded, ends],
    )
    return grad, adjoint, state, residuals


def body(conductivity, stored_state, row_scales, cotangent, upper_bound):
    strips_fit = (
        lax.axis_size("gx") == G
        and lax.axis_size("pa") == 2
        and conductivity.shape == (BX, BY, BZ)
    )
    run = redistributed if strips_fit else stepwise
    return tuple(run(conductivity, stored_state, row_scales, cotangent, upper_bound))


def solution(mesh):
    return jax.shard_map(
        body,
        mesh=mesh,
        in_specs=(
            P("gx", "gy", "pa"),
            P("gx", "gy", "pa"),
            P("gx", "gy"),
            P("gx", "gy", "pa"),
            P(),
        ),
        out_specs=(
            P("gx", "gy", "pa"),
            P("gx", "gy", "pa"),
            P("gx", "gy", "pa"),
            P(None, "gx", "gy", "pa"),
        ),
        check_vma=False,
    )
```

```python
import functools

import jax
import jax.numpy as jnp
from jax import lax
from jax.experimental import pallas as pl
from jax.experimental.pallas import tpu as pltpu
from jax.sharding import PartitionSpec as P

CHEB = 16
LANES = 128
HALO = CHEB
TIME_STEP = 8.0
F32 = jnp.float32


def with_halo(cells, sides, width):
    for axis, dim in sides:
        count = lax.axis_size(axis)
        head = lax.slice_in_dim(cells, 0, width, axis=dim)
        tail = lax.slice_in_dim(cells, cells.shape[dim] - width, cells.shape[dim], axis=dim)
        cells = jnp.concatenate(
            [
                lax.ppermute(tail, axis, [(i, (i + 1) % count) for i in range(count)]),
                cells,
                lax.ppermute(head, axis, [((i + 1) % count, i) for i in range(count)]),
            ],
            axis=dim,
        )
    return cells


def region(arr, spatial, offset):
    extent = arr.shape[-3:]
    window = [slice(1, length - 1) for length in extent]
    window[spatial] = slice(offset, extent[spatial] - 2 + offset)
    leading = [slice(None)] * (arr.ndim - 3)
    return arr[tuple(leading + window)]


def apply_operator(padded, kpad):
    centre = region(padded, 0, 1)
    kcentre = region(kpad, 0, 1)
    summed = jnp.zeros_like(centre)
    for spatial in range(3):
        for offset in (0, 2):
            summed = summed + 0.5 * (kcentre + region(kpad, spatial, offset)) * (
                centre - region(padded, spatial, offset)
            )
    return centre + TIME_STEP * summed


def stepwise(conductivity, stored_state, row_scales, cotangent, upper_bound):
    upper = upper_bound[0]
    kpad = with_halo(conductivity, (("gx", 0), ("gy", 1), ("pa", 2)), 1)
    count = lax.axis_size("pa")
    partner = lax.ppermute(stored_state, "pa", [(i, (i + count // 2) % count) for i in range(count)])
    previous = partner.astype(F32) * row_scales[:, :, None]
    rhs = jnp.stack((previous, cotangent))
    theta = 0.5 * (upper + 1.0)
    delta = 0.5 * (upper - 1.0)
    sigma = theta / delta
    sides = (("gx", 1), ("gy", 2), ("pa", 3))

    def sweep(step, carry):
        solved, residual, direction, rho = carry
        padded = with_halo(direction, sides, 1)
        solved = solved + direction
        residual = residual - apply_operator(padded, kpad)
        rho_next = 1.0 / (2.0 * sigma - rho)
        direction = rho_next * rho * direction + 2.0 * rho_next / delta * residual
        return (solved, residual, direction, rho_next)

    start = (jnp.zeros_like(rhs), rhs, rhs / theta, 1.0 / sigma)
    solved, residual, _, _ = lax.fori_loop(0, CHEB, sweep, start)
    pair = with_halo(solved, sides, 1)
    centre = region(pair, 0, 1)
    summed = jnp.zeros_like(solved[0])
    for spatial in range(3):
        for offset in (0, 2):
            differ = centre - region(pair, spatial, offset)
            summed = summed + differ[0] * differ[1]
    return (-0.5 * TIME_STEP * summed, solved[1], solved[0], residual)


G = 4
BX = 8
BY = 128
BZ = 128
STRIP = BZ // G
TOP = 8 + HALO
ROWS = BY + 2 * TOP
EXTENDED = BY + 2 * HALO
GROUP = BY + 8
SIDES = 2 * GROUP
FIELD = SIDES + BY
KAP = FIELD + BY
BOTH = KAP + 16
TILE = 8
CHUNK = 32
WIDE = 16

BLOCK = (0, 3, 2, 1)
PLANES = BX


def roll(x, by):
    by %= LANES
    return pltpu.roll(x, by, 1) if by else x


def lanes_of(rows, strip):
    lane = lax.broadcasted_iota(jnp.int32, (rows, LANES), 1)
    return lax.rem(lane // STRIP - strip + 2 * G, G), lax.rem(lane, STRIP)


def pick(group, parts):
    out = parts[0]
    for b in range(1, G):
        out = jnp.where(group == b, parts[b], out)
    return out


def parity_order(transposed):
    src = lax.broadcasted_iota(jnp.int32, (LANES, LANES), 1 if transposed else 0)
    dst = lax.broadcasted_iota(jnp.int32, (LANES, LANES), 0 if transposed else 1)
    within = lax.rem(src, STRIP)
    place = src - within + 16 * lax.rem(within, 2) + within // 2
    return jnp.where(place == dst, 1.0, 0.0).astype(jnp.bfloat16)


def reorder(x, order):
    if x.dtype == jnp.bfloat16:
        return jnp.dot(x, order, preferred_element_type=F32)
    high = x.astype(jnp.bfloat16)
    rest = x - high.astype(F32)
    middle = rest.astype(jnp.bfloat16)
    low = (rest - middle.astype(F32)).astype(jnp.bfloat16)
    return (
        jnp.dot(high, order, preferred_element_type=F32)
        + jnp.dot(middle, order, preferred_element_type=F32)
        + jnp.dot(low, order, preferred_element_type=F32)
    )


def pack_kernel(strips, *refs):
    ins, outs = refs[: len(refs) - G], refs[len(refs) - G :]
    order = parity_order(False)
    groups = [lanes_of(BY, strips[d])[0] for d in range(G)]
    for n, array in enumerate(ins):
        for a in range(2):
            planes = reorder(array[4 * a : 4 * a + 4].reshape(4 * BY, LANES), order)
            parts = [roll(planes[BY * b : BY * (b + 1)], 32 * b) for b in range(4)]
            for d in range(G):
                outs[d][n, a] = pick(groups[d], parts)


def pack_previous_kernel(strips, both, above, below, *outs):
    src = lax.broadcasted_iota(jnp.int32, (2 * LANES, 2 * LANES), 0)
    dst = lax.broadcasted_iota(jnp.int32, (2 * LANES, 2 * LANES), 1)
    place = LANES * lax.rem(src, 2) + 64 * (src // LANES) + lax.rem(src, LANES) // 2
    order = jnp.where(place == dst, 1.0, 0.0).astype(jnp.bfloat16)

    def give(planes, rows, start):
        groups = [lanes_of(rows, strips[d])[0] for d in range(G)]
        for m in range(4):
            pieces = []
            for i in (2 * m, 2 * m + 1):
                pair = planes[rows * i : rows * (i + 1)]
                for e in range(2):
                    pieces.append(pair[:, LANES * e : LANES * (e + 1)])
            for d in range(G):
                turned = [pltpu.roll(pieces[k], lax.rem(16 * strips[d] + 32 * k + 8, LANES), 1) for k in range(4)]
                outs[d][m, pl.ds(start, rows)] = pick(groups[d], turned)

    @pl.loop(0, BY // CHUNK)
    def _(t):
        r = pl.multiple_of(CHUNK * t, CHUNK)
        halves = [both[half, :, pl.ds(r, CHUNK)].reshape(BX * CHUNK, LANES) for half in range(2)]
        give(reorder(jnp.concatenate(halves, axis=1), order), CHUNK, pl.multiple_of(HALO + CHUNK * t, HALO))

    for start, array in ((0, above), (HALO + BY, below)):
        halves = [array[half].reshape(BX * HALO, LANES) for half in range(2)]
        give(reorder(jnp.concatenate(halves, axis=1), order), HALO, start)


def edge_kernel(places, *refs):
    msgs, (to_left, to_right, head, tail) = refs[:G], refs[G:]
    lane = lax.broadcasted_iota(jnp.int32, (BY, LANES), 1)
    low = lax.rem(lane, 16) < 8
    for n in range(msgs[0].shape[0]):
        for d in range(G):
            first, second = msgs[d][n, 0], msgs[d][n, 1]
            to_left[n, places[0, d]] = jnp.where(low, first, roll(second, 8))
            to_right[n, places[1, d]] = jnp.where(low, roll(second, -8), first)
            for a in range(2):
                head[n, d, a] = msgs[d][n, a, :HALO]
                tail[n, d, a] = msgs[d][n, a, BY - HALO :]


def unpack(get_brick, get_edge, group, within, put):
    by_block = [BLOCK.index(q) for q in range(G)]
    edges = [[get_edge(side, d) for d in by_block] for side in range(2)]
    for a in range(2):
        far = 24 if a else 16
        own = [roll(get_brick(by_block[q], a), 32 * q) for q in range(G)]
        below = [roll(edges[0][q], 32 * q + far) for q in range(G)]
        above = [roll(edges[1][q], 32 * q - far) for q in range(G)]
        even = [
            jnp.where(within < 16, own[q], jnp.where(within < 24, above[q], below[(q + 1) % G])) for q in range(G)
        ]
        odd = [
            jnp.where(within < 8, above[(q - 1) % G], jnp.where(within < 16, below[q], own[q])) for q in range(G)
        ]
        for b in range(4):
            for e, parts in enumerate((even, odd)):
                whole = pick(group, [parts[(q - b) % G] for q in range(G)])
                put(4 * a + b, e, roll(whole, -32 * b - 16 * e))


def unpack_strip(get, group, put):
    by_block = [BLOCK.index(q) for q in range(G)]
    for m in range(4):
        turned = [roll(get(by_block[q], m), 32 * q) for q in range(G)]
        for k in range(4):
            whole = pick(group, [turned[(q - k) % G] for q in range(G)])
            put(2 * m + k // 2, k % 2, roll(whole, -32 * k - 8))


def solve_kernel(adjoint, strip, upper, *refs):
    if adjoint:
        bricks, (from_left, from_right, above, below, above_edge, below_edge) = refs[:G], refs[G : G + 6]
        outs, coefficients, (kap, *scratch) = refs[G + 6 : 2 * G + 6], refs[2 * G + 6 : 2 * G + 11], refs[2 * G + 11 :]
    else:
        strips_here, coefficients = refs[:G], refs[G : G + 5]
        outs, scratch = refs[G + 5 : 2 * G + 5], refs[2 * G + 5 :]
    kx, ky, kin, kout, diag = coefficients
    rhs, xa, xb, xc, turned, steps = scratch
    zero = jnp.zeros((TILE, LANES), F32)

    theta = 0.5 * (jnp.full((TILE, LANES), upper[0]) + 1.0)
    delta = 0.5 * (jnp.full((TILE, LANES), upper[0]) - 1.0)
    sigma = theta / delta
    rho = 1.0 / sigma
    for k in range(1, CHEB):
        rho_next = 1.0 / (2.0 * sigma - rho)
        steps[k, 0] = rho_next * rho
        steps[k, 1] = 2.0 * rho_next / delta
        rho = rho_next
    theta_inv = 1.0 / (0.5 * (jnp.full((2 * TILE, LANES), upper[0]) + 1.0))

    def put_at(dst, to, rows):
        def put(i, e, val):
            dst[i, e, pl.ds(to, rows)] = val

        return put

    for i in range(PLANES):
        for e in range(2):
            for dst in (rhs, xa, xb, xc) + ((kap, ky) if adjoint else ()):
                dst[i, e, 0:TILE] = zero
                dst[i, e, ROWS - TILE : ROWS] = zero
        for dst in (kin, kout) if adjoint else ():
            dst[i, 0:TILE] = zero
            dst[i, ROWS - TILE : ROWS] = zero

    if adjoint:
        sides, corners = (from_left, from_right), (above_edge, below_edge)

        @pl.loop(0, BY // CHUNK)
        def _(t):
            at = pl.ds(pl.multiple_of(CHUNK * t, CHUNK), CHUNK)
            group, within = lanes_of(CHUNK, strip[0])
            for n, dst in enumerate((kap, rhs)):
                unpack(
                    lambda d, a: bricks[d][n, a, at],
                    lambda side, d: sides[side][n, d, at],
                    group,
                    within,
                    put_at(dst, pl.multiple_of(TOP + CHUNK * t, TILE), CHUNK),
                )

        group_halo, within_halo = lanes_of(HALO, strip[0])
        for n, dst in enumerate((kap, rhs)):
            for brick, edge, start in ((above, above_edge, TOP - HALO), (below, below_edge, TOP + BY)):
                unpack(
                    lambda d, a: brick[n, d, a],
                    lambda side, d: edge[side, n, d],
                    group_halo,
                    within_halo,
                    put_at(dst, start, HALO),
                )
    else:

        @pl.loop(0, EXTENDED // CHUNK)
        def _(t):
            at = pl.ds(pl.multiple_of(CHUNK * t, CHUNK), CHUNK)
            group, _ = lanes_of(CHUNK, strip[0])
            unpack_strip(
                lambda d, m: strips_here[d][m, at],
                group,
                put_at(rhs, pl.multiple_of(TOP - HALO + CHUNK * t, TILE), CHUNK),
            )

    @pl.loop(0, (ROWS // TILE - 2) // 2)
    def _(t):
        rows = 2 * TILE
        r = pl.multiple_of(TILE + rows * t, TILE)
        at = pl.ds(r, rows)
        for i in range(PLANES):
            for e in range(2):
                xb[i, e, at] = rhs[i, e, at] * theta_inv
                xa[i, e, at] = jnp.zeros((rows, LANES), F32)
        if not adjoint:
            return
        first = [kap[0, e, at] for e in range(2)]
        now = first
        before = [4.0 * (k + roll(kap[PLANES - 1, e, at], 32)) for e, k in enumerate(first)]
        for i in range(PLANES):
            after = [kap[i + 1, e, at] if i + 1 < PLANES else roll(first[e], -32) for e in range(2)]
            inner = 4.0 * (now[0] + now[1])
            outer = 4.0 * (now[1] + roll(now[0], -1))
            outer_before = 4.0 * (now[0] + roll(now[1], 1))
            kin[i, at] = inner
            kout[i, at] = outer
            along = (inner + outer_before, inner + outer)
            for e in range(2):
                fx = 4.0 * (now[e] + after[e])
                fy = 4.0 * (now[e] + kap[i, e, pl.ds(r + 1, rows)])
                fym = 4.0 * (now[e] + kap[i, e, pl.ds(r - 1, rows)])
                kx[i, e, at] = fx
                ky[i, e, at] = fy
                diag[i, e, at] = 1.0 + (fx + before[e] + (fy + fym) + along[e])
                before[e] = fx
            now = after

    def turn_lanes(cur, r):
        at = pl.ds(r, TILE)
        for i in range(PLANES):
            turned[i, 0] = roll(kout[i, at] * cur[i, 1, at], 1)
            turned[i, 1] = roll(cur[i, 0, at], -1)
        for e in range(2):
            turned[PLANES, e] = roll(kx[PLANES - 1, e, at] * cur[PLANES - 1, e, at], 32)
            turned[PLANES + 1, e] = roll(cur[0, e, at], -32)

    def advance(alpha, beta, old, cur, new, r):
        at = pl.ds(r, TILE)
        now = [cur[0, e, at] for e in range(2)]
        before = fbefore = None
        for i in range(PLANES):
            fx = [kx[i, e, at] for e in range(2)]
            inner, outer = kin[i, at], kout[i, at]
            if i + 1 < PLANES:
                after = [cur[i + 1, e, at] for e in range(2)]
            else:
                after = [turned[PLANES + 1, e] for e in range(2)]
            for e in range(2):
                near = ky[i, e, at] * cur[i, e, pl.ds(r + 1, TILE)]
                near = near + ky[i, e, pl.ds(r - 1, TILE)] * cur[i, e, pl.ds(r - 1, TILE)]
                side = turned[i, e]
                near = near + (inner * now[1 - e] + (outer * side if e else side))
                behind = fbefore[e] * before[e] if i else turned[PLANES, e]
                near = near + (fx[e] * after[e] + behind)
                near = near + rhs[i, e, at]
                centre = (1.0 + alpha) - beta * diag[i, e, at]
                new[i, e, at] = centre * now[e] - alpha * old[i, e, at] + beta * near
            before, now, fbefore = now, after, fx

    def sweep(k, old, cur, new, span):
        alpha, beta = steps[k, 0], steps[k, 1]
        turn_lanes(cur, span[0])

        @pl.loop(0, span[1] // span[2])
        def _(t):
            for u in range(span[2]):
                r = pl.multiple_of(span[0] + TILE * (span[2] * t + u), TILE)
                advance(alpha, beta, old, cur, new, r)
                turn_lanes(cur, r + TILE)

    def three(k, spans):
        sweep(k, xa, xb, xc, spans[0])
        sweep(k + 1, xb, xc, xa, spans[1])
        sweep(k + 2, xc, xa, xb, spans[2])

    wide = (TILE, ROWS // TILE - 2, 4)
    narrow = (2 * TILE, ROWS // TILE - 4, 3)

    @pl.loop(0, 2)
    def _(m):
        three(1 + 3 * m, (wide,) * 3)

    three(7, (wide, narrow, narrow))

    @pl.loop(0, 2)
    def _(m):
        three(10 + 3 * m, (narrow,) * 3)

    def mains(whole, group, within):
        parts = [jnp.where(within < 16, even, roll(odd, 16)) for even, odd in whole]
        turned = [roll(parts[i], 32 * (i % 4)) for i in range(PLANES)]
        return parts, [
            [pick(group, [turned[4 * a + (q - d) % G] for q in range(G)]) for a in range(2)] for d in range(G)
        ]

    def beside(whole, parts, group, within):
        tree = [jnp.where(within == 31, odd, even) for even, odd in whole]
        for level in range(3):
            width = 1 << level
            keep = (lax.rem(within + 1, STRIP) < width) | ((within >= 16) & (within < 16 + width))
            tree = [jnp.where(keep, tree[j], roll(tree[j + 1], width)) for j in range(0, len(tree), 2)]
        ends = roll(tree[0], 1)
        groups = (ends, ends, roll(parts[PLANES - 1], 96), roll(parts[0], 64))
        return [pick(group, [groups[(q - d) % G] for q in range(G)]) for d in range(G)]

    def load(field, row, rows):
        return [[field[i, e, pl.ds(row, rows)] for e in range(2)] for i in range(PLANES)]

    @pl.loop(0, BY // CHUNK)
    def _(t):
        row = pl.multiple_of(TOP + CHUNK * t, TILE)
        group, within = lanes_of(CHUNK, strip[0])

        def to(start):
            return pl.ds(pl.multiple_of(start + CHUNK * t, TILE), CHUNK)

        for field, start in ((xb, SIDES),) + (((kap, FIELD),) if adjoint else ()):
            whole = load(field, row, CHUNK)
            parts, main = mains(whole, group, within)
            sides = beside(whole, parts, group, within)
            for d in range(G):
                outs[d][to(start)] = sides[d]
                if field is xb:
                    for a in range(2):
                        outs[d][to(GROUP * a)] = main[d][a]

    sub = lax.broadcasted_iota(jnp.int32, (TILE, LANES), 0)
    group, within = lanes_of(TILE, strip[0])
    for field in (xb, kap) if adjoint else (xb,):
        over = mains(load(field, TOP - TILE, TILE), group, within)[1]
        under = mains(load(field, TOP + BY, TILE), group, within)[1]
        for d in range(G):
            for a in range(2):
                to = GROUP * a + BY if field is xb else KAP + TILE * a
                outs[d][to : to + TILE] = jnp.where(
                    sub == 0, pltpu.roll(over[d][a], 1, 0), pltpu.roll(under[d][a], 1, 0)
                )


def collect(strips, msgs, padded, ends, base, own):
    order = parity_order(True)

    def owners(rows):
        return [lanes_of(rows, strips[d])[0] for d in range(G)]

    def choose(owner, parts, b):
        out = parts[0]
        for d in range(1, G):
            out = jnp.where(owner[d] == b, parts[d], out)
        return roll(out, -32 * b)

    def bricks(row, rows):
        return [roll(msgs[d][pl.ds(row, rows)], -32 * d) for d in range(G)]

    sides_at, tiles_at = (SIDES, (BY, GROUP + BY)) if own is None else (FIELD, (KAP, KAP + TILE))

    @pl.loop(0, BY // CHUNK)
    def _(t):
        to = pl.ds(pl.multiple_of(TILE + CHUNK * t, TILE), CHUNK)
        owner = owners(CHUNK)
        whole, places = [], []
        if own is None:
            for a in range(2):
                parts = bricks(pl.multiple_of(GROUP * a + CHUNK * t, TILE), CHUNK)
                whole += [choose(owner, parts, b) for b in range(4)]
                places += [1 + 4 * a + b for b in range(4)]
        else:
            for c in range(BX):
                padded[1 + c, to] = own[c, pl.ds(pl.multiple_of(CHUNK * t, CHUNK), CHUNK)]
        parts = bricks(pl.multiple_of(sides_at + CHUNK * t, TILE), CHUNK)
        for side, end in enumerate((0, G - 1)):
            val = parts[0]
            for d in range(1, G):
                val = jnp.where(strips[d] == end, parts[d], val)
            ends[side, pl.ds(pl.multiple_of(CHUNK * t, CHUNK), CHUNK)] = val
        whole += [choose(owner, parts, b) for b in (2, 3)]
        places += [0, 1 + BX]
        ordered = reorder(jnp.concatenate(whole, axis=0), order)
        for j, at in enumerate(places):
            padded[at, to] = ordered[CHUNK * j : CHUNK * (j + 1)]

    owner = owners(TILE)
    whole = []
    for a in range(2):
        parts = bricks(tiles_at[a], TILE)
        whole += [choose(owner, parts, b) for b in range(4)]
    ordered = reorder(jnp.concatenate(whole, axis=0), order)
    for c in range(BX):
        val = pltpu.roll(ordered[TILE * c : TILE * (c + 1)], 7, 0)
        padded[1 + c, 0:TILE] = val
        padded[1 + c, TILE + BY : 2 * TILE + BY] = val


def across(padded, c, t):
    r8 = pl.multiple_of(WIDE * t + TILE, TILE)
    return padded[1 + c, pl.ds(r8, WIDE)], [
        padded[c, pl.ds(r8, WIDE)],
        padded[c + 2, pl.ds(r8, WIDE)],
        padded[1 + c, pl.ds(r8 - 1, WIDE)],
        padded[1 + c, pl.ds(r8 + 1, WIDE)],
    ]


def along(cell, ends, c, t):
    lane = lax.broadcasted_iota(jnp.int32, (WIDE, LANES), 1)
    low, high = (ends[side, pl.ds(pl.multiple_of(WIDE * t, WIDE), WIDE)] for side in range(2))
    return [
        jnp.where(lane == 0, roll(low, -c), roll(cell, 1)),
        jnp.where(lane == LANES - 1, roll(high, 14 - c), roll(cell, -1)),
    ]


def adjoint_kernel(strips, m0, m1, m2, m3, cond, cot, adjoint, residual, padded, kap, faces, differences, ends, kends):
    collect(strips, (m0, m1, m2, m3), padded, ends, 0, None)
    collect(strips, (m0, m1, m2, m3), kap, kends, 0, cond)

    @pl.loop(0, BY // WIDE)
    def _(t):
        at = pl.ds(pl.multiple_of(WIDE * t, WIDE), WIDE)
        for c in range(BX):
            k, knear = across(kap, c, t)
            x, xnear = across(padded, c, t)
            total = 0.0
            for kn, xn in zip(knear, xnear):
                total = total + (k + kn) * (x - xn)
            for side, (kn, xn) in enumerate(zip(along(k, kends, c, t), along(x, ends, c, t))):
                face, differ = k + kn, x - xn
                faces[side, c, at] = face
                differences[side, c, at] = differ
                total = total + face * differ
            adjoint[c, at] = x
            residual[c, at] = cot[c, at] - (x + (0.5 * TIME_STEP) * total)


def state_kernel(strips, m0, m1, m2, m3, previous, adj, kap, faces, differences, adj_residual, grad, state, residuals, padded, ends):
    collect(strips, (m0, m1, m2, m3), padded, ends, 0, None)

    @pl.loop(0, BY // WIDE)
    def _(t):
        at = pl.ds(pl.multiple_of(WIDE * t, WIDE), WIDE)
        for c in range(BX):
            k, knear = across(kap, c, t)
            x, xnear = across(padded, c, t)
            y, ynear = across(adj, c, t)
            total = product = 0.0
            for kn, xn, yn in zip(knear, xnear, ynear):
                differ = x - xn
                total = total + (k + kn) * differ
                product = product + differ * (y - yn)
            for side, xn in enumerate(along(x, ends, c, t)):
                differ = x - xn
                total = total + faces[side, c, at] * differ
                product = product + differ * differences[side, c, at]
            grad[c, at] = (-0.5 * TIME_STEP) * product
            state[c, at] = x
            residuals[0, c, at] = previous[0, c, at] - (x + (0.5 * TIME_STEP) * total)
            residuals[1, c, at] = adj_residual[c, at]


def call(kernel, outs, smem, vmem, scratch=(), micros=2, mebibytes=16):
    vm = pl.BlockSpec(memory_space=pltpu.VMEM)
    sm = pl.BlockSpec(memory_space=pltpu.SMEM)
    return pl.pallas_call(
        kernel,
        out_shape=[jax.ShapeDtypeStruct(shape, F32) for shape in outs],
        in_specs=[sm] * len(smem) + [vm] * len(vmem),
        out_specs=[vm] * len(outs),
        scratch_shapes=[pltpu.VMEM(shape, F32) for shape in scratch],
        compiler_params=pltpu.CompilerParams(vmem_limit_bytes=mebibytes * 1024 * 1024),
        cost_estimate=pl.CostEstimate(flops=0, bytes_accessed=micros * 3_000_000, transcendentals=0),
    )(*smem, *vmem)


def shifted(x, axis, by):
    count = lax.axis_size(axis)
    return lax.ppermute(x, axis, [(i, (i + by) % count) for i in range(count)])


def around(x, by):
    order = [2 * g for g in range(G)] + [2 * g + 1 for g in reversed(range(G))]
    return lax.ppermute(x, ("gx", "pa"), [(at, order[(i + by) % len(order)]) for i, at in enumerate(order)])


def redistributed(conductivity, stored_state, row_scales, cotangent, upper_bound):
    g = lax.axis_index("gx")
    pa = lax.axis_index("pa")

    def strip_of(device):
        return jnp.where(pa == 0, device, G - 1 - device)

    steps = jnp.arange(G, dtype=jnp.int32)
    ahead = lax.rem(g + steps, G)
    behind = lax.rem(g - steps + G, G)
    strip = strip_of(g)
    left_g = jnp.where(pa == 0, jnp.maximum(g - 1, 0), jnp.minimum(g + 1, G - 1))
    right_g = jnp.where(pa == 0, jnp.minimum(g + 1, G - 1), jnp.maximum(g - 1, 0))
    places = lax.rem(jnp.stack((left_g - g + steps, right_g - g + steps)) + G, G)

    brick = (2, 2, BY, LANES)
    parts = call(pack_kernel, [brick] * G, [strip_of(ahead)], [conductivity, cotangent])
    parts, stored_state = lax.optimization_barrier((parts, stored_state))
    parts = [parts[0]] + [shifted(parts[d], "gx", d) for d in range(1, G)]
    stored = shifted(stored_state, "pa", 1)
    both = jnp.stack((stored, stored_state)).astype(F32) * row_scales[:, :, None]
    above_rows = shifted(both[:, :, BY - HALO :], "gy", 1)
    below_rows = shifted(both[:, :, :HALO], "gy", -1)
    parts, above_rows, below_rows = lax.optimization_barrier((parts, above_rows, below_rows))
    edge = (2, G, BY, LANES)
    rim = (2, G, 2, HALO, LANES)
    to_left, to_right, head, tail = call(edge_kernel, [edge, edge, rim, rim], [places], parts)
    to_left, below_rows = lax.optimization_barrier((to_left, below_rows))
    messages = call(
        pack_previous_kernel,
        [(4, EXTENDED, LANES)] * G,
        [strip_of(ahead)],
        [both, above_rows, below_rows],
    )
    from_left, from_right = around(to_right, 1), around(to_left, -1)
    from_left, from_right, own = lax.optimization_barrier((from_left, from_right, messages[0]))
    above, below = shifted(tail, "gy", 1), shifted(head, "gy", -1)
    edges = [jnp.stack((from_left[:, :, at], from_right[:, :, at])) for at in (slice(BY - HALO, BY), slice(0, HALO))]
    halos = [from_left, from_right, above, below, shifted(edges[0], "gy", 1), shifted(edges[1], "gy", -1)]
    second = [own] + [shifted(messages[d], "gx", d) for d in range(1, G)]

    line = (PLANES, 2, ROWS, LANES)
    half = (PLANES, ROWS, LANES)
    lines = [line] * 4 + [(PLANES + 2, 2, TILE, LANES), (CHEB, 2, TILE, LANES)]
    setup = [strip[None], upper_bound]

    def home(solved):
        return [solved[0]] + [shifted(solved[d], "gx", d) for d in range(1, G)]

    *solved_adjoint, kx, ky, kin, kout, diag = call(
        functools.partial(solve_kernel, True),
        [(BOTH, LANES)] * G + [line, line, half, half, line],
        setup,
        [*parts, *halos],
        [line] + lines,
        micros=25,
        mebibytes=24,
    )
    solved_adjoint = home(solved_adjoint)
    solved_state = home(
        call(
            functools.partial(solve_kernel, False),
            [(FIELD, LANES)] * G,
            setup,
            [*second, kx, ky, kin, kout, diag],
            lines,
            micros=25,
            mebibytes=24,
        )
    )

    out = (BX, BY, LANES)
    padded = (BX + 2, BY + 16, LANES)
    ends = (2, BY, LANES)
    here = strip_of(behind)
    adjoint, adj_residual, adj, kap, faces, differences = call(
        adjoint_kernel,
        [out, out, padded, padded, (2,) + out, (2,) + out],
        [here],
        [*solved_adjoint, conductivity, cotangent],
        [ends, ends],
    )
    grad, state, residuals = call(
        state_kernel,
        [out, out, (2,) + out],
        [here],
        [*solved_state, both, adj, kap, faces, differences, adj_residual],
        [padded, ends],
    )
    return grad, adjoint, state, residuals


def body(conductivity, stored_state, row_scales, cotangent, upper_bound):
    strips_fit = (
        lax.axis_size("gx") == G
        and lax.axis_size("pa") == 2
        and conductivity.shape == (BX, BY, BZ)
    )
    run = redistributed if strips_fit else stepwise
    return tuple(run(conductivity, stored_state, row_scales, cotangent, upper_bound))


def solution(mesh):
    return jax.shard_map(
        body,
        mesh=mesh,
        in_specs=(
            P("gx", "gy", "pa"),
            P("gx", "gy", "pa"),
            P("gx", "gy"),
            P("gx", "gy", "pa"),
            P(),
        ),
        out_specs=(
            P("gx", "gy", "pa"),
            P("gx", "gy", "pa"),
            P("gx", "gy", "pa"),
            P(None, "gx", "gy", "pa"),
        ),
        check_vma=False,
    )
```

```python
import functools

import jax
import jax.numpy as jnp
from jax import lax
from jax.experimental import pallas as pl
from jax.experimental.pallas import tpu as pltpu
from jax.sharding import PartitionSpec as P

CHEB = 16
LANES = 128
HALO = CHEB
TIME_STEP = 8.0
F32 = jnp.float32


def with_halo(cells, sides, width):
    for axis, dim in sides:
        count = lax.axis_size(axis)
        head = lax.slice_in_dim(cells, 0, width, axis=dim)
        tail = lax.slice_in_dim(cells, cells.shape[dim] - width, cells.shape[dim], axis=dim)
        cells = jnp.concatenate(
            [
                lax.ppermute(tail, axis, [(i, (i + 1) % count) for i in range(count)]),
                cells,
                lax.ppermute(head, axis, [((i + 1) % count, i) for i in range(count)]),
            ],
            axis=dim,
        )
    return cells


def region(arr, spatial, offset):
    extent = arr.shape[-3:]
    window = [slice(1, length - 1) for length in extent]
    window[spatial] = slice(offset, extent[spatial] - 2 + offset)
    leading = [slice(None)] * (arr.ndim - 3)
    return arr[tuple(leading + window)]


def apply_operator(padded, kpad):
    centre = region(padded, 0, 1)
    kcentre = region(kpad, 0, 1)
    summed = jnp.zeros_like(centre)
    for spatial in range(3):
        for offset in (0, 2):
            summed = summed + 0.5 * (kcentre + region(kpad, spatial, offset)) * (
                centre - region(padded, spatial, offset)
            )
    return centre + TIME_STEP * summed


def stepwise(conductivity, stored_state, row_scales, cotangent, upper_bound):
    upper = upper_bound[0]
    kpad = with_halo(conductivity, (("gx", 0), ("gy", 1), ("pa", 2)), 1)
    count = lax.axis_size("pa")
    partner = lax.ppermute(stored_state, "pa", [(i, (i + count // 2) % count) for i in range(count)])
    previous = partner.astype(F32) * row_scales[:, :, None]
    rhs = jnp.stack((previous, cotangent))
    theta = 0.5 * (upper + 1.0)
    delta = 0.5 * (upper - 1.0)
    sigma = theta / delta
    sides = (("gx", 1), ("gy", 2), ("pa", 3))

    def sweep(step, carry):
        solved, residual, direction, rho = carry
        padded = with_halo(direction, sides, 1)
        solved = solved + direction
        residual = residual - apply_operator(padded, kpad)
        rho_next = 1.0 / (2.0 * sigma - rho)
        direction = rho_next * rho * direction + 2.0 * rho_next / delta * residual
        return (solved, residual, direction, rho_next)

    start = (jnp.zeros_like(rhs), rhs, rhs / theta, 1.0 / sigma)
    solved, residual, _, _ = lax.fori_loop(0, CHEB, sweep, start)
    pair = with_halo(solved, sides, 1)
    centre = region(pair, 0, 1)
    summed = jnp.zeros_like(solved[0])
    for spatial in range(3):
        for offset in (0, 2):
            differ = centre - region(pair, spatial, offset)
            summed = summed + differ[0] * differ[1]
    return (-0.5 * TIME_STEP * summed, solved[1], solved[0], residual)


G = 4
BX = 8
BY = 128
BZ = 128
STRIP = BZ // G
TOP = 8 + HALO
ROWS = BY + 2 * TOP
EXTENDED = BY + 2 * HALO
GROUP = BY + 8
SIDES = 2 * GROUP
FIELD = SIDES + BY
KAP = FIELD + BY
BOTH = KAP + 16
TILE = 8
CHUNK = 32
WIDE = 16

BLOCK = (0, 3, 2, 1)
PLANES = BX


def roll(x, by):
    by %= LANES
    return pltpu.roll(x, by, 1) if by else x


def lanes_of(rows, strip):
    lane = lax.broadcasted_iota(jnp.int32, (rows, LANES), 1)
    return lax.rem(lane // STRIP - strip + 2 * G, G), lax.rem(lane, STRIP)


def pick(group, parts):
    out = parts[0]
    for b in range(1, G):
        out = jnp.where(group == b, parts[b], out)
    return out


def parity_order(transposed):
    src = lax.broadcasted_iota(jnp.int32, (LANES, LANES), 1 if transposed else 0)
    dst = lax.broadcasted_iota(jnp.int32, (LANES, LANES), 0 if transposed else 1)
    within = lax.rem(src, STRIP)
    place = src - within + 16 * lax.rem(within, 2) + within // 2
    return jnp.where(place == dst, 1.0, 0.0).astype(jnp.bfloat16)


def reorder(x, order):
    if x.dtype == jnp.bfloat16:
        return jnp.dot(x, order, preferred_element_type=F32)
    high = x.astype(jnp.bfloat16)
    rest = x - high.astype(F32)
    middle = rest.astype(jnp.bfloat16)
    low = (rest - middle.astype(F32)).astype(jnp.bfloat16)
    return (
        jnp.dot(high, order, preferred_element_type=F32)
        + jnp.dot(middle, order, preferred_element_type=F32)
        + jnp.dot(low, order, preferred_element_type=F32)
    )


def pack_kernel(strips, *refs):
    ins, outs = refs[: len(refs) - G], refs[len(refs) - G :]
    order = parity_order(False)
    groups = [lanes_of(BY, strips[d])[0] for d in range(G)]
    for n, array in enumerate(ins):
        for a in range(2):
            planes = reorder(array[4 * a : 4 * a + 4].reshape(4 * BY, LANES), order)
            parts = [roll(planes[BY * b : BY * (b + 1)], 32 * b) for b in range(4)]
            for d in range(G):
                outs[d][n, a] = pick(groups[d], parts)


def chebyshev_steps(upper, steps):
    bound = jnp.full((TILE, LANES), upper[0])
    theta = 0.5 * (bound + 1.0)
    delta = 0.5 * (bound - 1.0)
    sigma = theta / delta
    rho = 1.0 / sigma
    steps[0, 0] = 1.0 / theta
    steps[0, 1] = jnp.zeros_like(theta)
    for k in range(1, CHEB):
        rho_next = 1.0 / (2.0 * sigma - rho)
        steps[k, 0] = rho_next * rho
        steps[k, 1] = 2.0 * rho_next / delta
        rho = rho_next


def pack_previous_kernel(strips, upper, both, above, below, *outs):
    *outs, steps = outs
    chebyshev_steps(upper, steps)
    src = lax.broadcasted_iota(jnp.int32, (2 * LANES, 2 * LANES), 0)
    dst = lax.broadcasted_iota(jnp.int32, (2 * LANES, 2 * LANES), 1)
    place = LANES * lax.rem(src, 2) + 64 * (src // LANES) + lax.rem(src, LANES) // 2
    order = jnp.where(place == dst, 1.0, 0.0).astype(jnp.bfloat16)

    def give(planes, rows, start):
        groups = [lanes_of(rows, strips[d])[0] for d in range(G)]
        for m in range(4):
            pieces = []
            for i in (2 * m, 2 * m + 1):
                pair = planes[rows * i : rows * (i + 1)]
                for e in range(2):
                    pieces.append(pair[:, LANES * e : LANES * (e + 1)])
            for d in range(G):
                turned = [pltpu.roll(pieces[k], lax.rem(16 * strips[d] + 32 * k + 8, LANES), 1) for k in range(4)]
                outs[d][m, pl.ds(start, rows)] = pick(groups[d], turned)

    @pl.loop(0, BY // CHUNK)
    def _(t):
        r = pl.multiple_of(CHUNK * t, CHUNK)
        halves = [both[half, :, pl.ds(r, CHUNK)].reshape(BX * CHUNK, LANES) for half in range(2)]
        give(reorder(jnp.concatenate(halves, axis=1), order), CHUNK, pl.multiple_of(HALO + CHUNK * t, HALO))

    for start, array in ((0, above), (HALO + BY, below)):
        halves = [array[half].reshape(BX * HALO, LANES) for half in range(2)]
        give(reorder(jnp.concatenate(halves, axis=1), order), HALO, start)


def edge_kernel(places, *refs):
    msgs, (to_left, to_right) = refs[:G], refs[G:]
    lane = lax.broadcasted_iota(jnp.int32, (BY, LANES), 1)
    low = lax.rem(lane, 16) < 8
    for n in range(2):
        for d in range(G):
            first, second = msgs[d][n, 0], msgs[d][n, 1]
            to_left[n, places[0, d]] = jnp.where(low, first, roll(second, 8))
            to_right[n, places[1, d]] = jnp.where(low, roll(second, -8), first)


def rows_kernel(*refs):
    msgs, sides, (head, tail) = refs[:G], refs[G : G + 2], refs[G + 2 :]
    for n in range(2):
        for d in range(G):
            for out, rows in ((head, slice(0, HALO)), (tail, slice(BY - HALO, BY))):
                for a in range(2):
                    out[n, d, a] = msgs[d][n, a, rows]
                    out[n, d, 2 + a] = sides[a][n, d, rows]


def unpack(get_brick, get_edge, group, within, put):
    by_block = [BLOCK.index(q) for q in range(G)]
    edges = [[get_edge(side, d) for d in by_block] for side in range(2)]
    for a in range(2):
        far = 24 if a else 16
        own = [roll(get_brick(by_block[q], a), 32 * q) for q in range(G)]
        below = [roll(edges[0][q], 32 * q + far) for q in range(G)]
        above = [roll(edges[1][q], 32 * q - far) for q in range(G)]
        even = [
            jnp.where(within < 16, own[q], jnp.where(within < 24, above[q], below[(q + 1) % G])) for q in range(G)
        ]
        odd = [
            jnp.where(within < 8, above[(q - 1) % G], jnp.where(within < 16, below[q], own[q])) for q in range(G)
        ]
        for b in range(4):
            for e, parts in enumerate((even, odd)):
                whole = pick(group, [parts[(q - b) % G] for q in range(G)])
                put(4 * a + b, e, roll(whole, -32 * b - 16 * e))


def unpack_strip(get, group, put):
    by_block = [BLOCK.index(q) for q in range(G)]
    for m in range(4):
        turned = [roll(get(by_block[q], m), 32 * q) for q in range(G)]
        for k in range(4):
            whole = pick(group, [turned[(q - k) % G] for q in range(G)])
            put(2 * m + k // 2, k % 2, roll(whole, -32 * k - 8))


def solve_kernel(adjoint, strip, steps, *refs):
    if adjoint:
        bricks, (from_left, from_right, above, below) = refs[:G], refs[G : G + 4]
        outs, coefficients, (kap, *scratch) = refs[G + 4 : 2 * G + 4], refs[2 * G + 4 : 2 * G + 9], refs[2 * G + 9 :]
    else:
        strips_here, coefficients = refs[:G], refs[G : G + 5]
        outs, scratch = refs[G + 5 : 2 * G + 5], refs[2 * G + 5 :]
    kx, ky, kin, kout, diag = coefficients
    rhs, xa, xb, xc, turned, turned_first = scratch
    zero = jnp.zeros((TILE, LANES), F32)
    theta_inv = jnp.concatenate([steps[0, 0]] * 2, axis=0)

    def put_at(dst, to, rows):
        def put(i, e, val):
            dst[i, e, pl.ds(to, rows)] = val

        return put

    for i in range(PLANES):
        for e in range(2):
            for dst in (rhs, xa, xb, xc) + ((kap, ky) if adjoint else ()):
                dst[i, e, 0:TILE] = zero
                dst[i, e, ROWS - TILE : ROWS] = zero
        for dst in (kin, kout) if adjoint else ():
            dst[i, 0:TILE] = zero
            dst[i, ROWS - TILE : ROWS] = zero

    if adjoint:
        sides = (from_left, from_right)

        @pl.loop(0, BY // CHUNK)
        def _(t):
            at = pl.ds(pl.multiple_of(CHUNK * t, CHUNK), CHUNK)
            group, within = lanes_of(CHUNK, strip[0])
            for n, dst in enumerate((kap, rhs)):
                unpack(
                    lambda d, a: bricks[d][n, a, at],
                    lambda side, d: sides[side][n, d, at],
                    group,
                    within,
                    put_at(dst, pl.multiple_of(TOP + CHUNK * t, TILE), CHUNK),
                )

        group_halo, within_halo = lanes_of(HALO, strip[0])
        for n, dst in enumerate((kap, rhs)):
            for rows, start in ((above, TOP - HALO), (below, TOP + BY)):
                unpack(
                    lambda d, a: rows[n, d, a],
                    lambda side, d: rows[n, d, 2 + side],
                    group_halo,
                    within_halo,
                    put_at(dst, start, HALO),
                )
    else:

        @pl.loop(0, EXTENDED // CHUNK)
        def _(t):
            at = pl.ds(pl.multiple_of(CHUNK * t, CHUNK), CHUNK)
            group, _ = lanes_of(CHUNK, strip[0])
            unpack_strip(
                lambda d, m: strips_here[d][m, at],
                group,
                put_at(rhs, pl.multiple_of(TOP - HALO + CHUNK * t, TILE), CHUNK),
            )

    @pl.loop(0, (ROWS // TILE - 2) // 2)
    def _(t):
        rows = 2 * TILE
        r = pl.multiple_of(TILE + rows * t, TILE)
        at = pl.ds(r, rows)
        for i in range(PLANES):
            for e in range(2):
                xb[i, e, at] = rhs[i, e, at] * theta_inv
                xa[i, e, at] = jnp.zeros((rows, LANES), F32)
        if not adjoint:
            return
        first = [kap[0, e, at] for e in range(2)]
        now = first
        before = [4.0 * (k + roll(kap[PLANES - 1, e, at], 32)) for e, k in enumerate(first)]
        for i in range(PLANES):
            after = [kap[i + 1, e, at] if i + 1 < PLANES else roll(first[e], -32) for e in range(2)]
            inner = 4.0 * (now[0] + now[1])
            outer = 4.0 * (now[1] + roll(now[0], -1))
            outer_before = 4.0 * (now[0] + roll(now[1], 1))
            kin[i, at] = inner
            kout[i, at] = outer
            along = (inner + outer_before, inner + outer)
            for e in range(2):
                fx = 4.0 * (now[e] + after[e])
                fy = 4.0 * (now[e] + kap[i, e, pl.ds(r + 1, rows)])
                fym = 4.0 * (now[e] + kap[i, e, pl.ds(r - 1, rows)])
                kx[i, e, at] = fx
                ky[i, e, at] = fy
                diag[i, e, at] = 1.0 + (fx + before[e] + (fy + fym) + along[e])
                before[e] = fx
            now = after

    def turn_lanes(cur, r, turned):
        at = pl.ds(r, TILE)
        for i in range(PLANES):
            turned[i, 0] = roll(kout[i, at] * cur[i, 1, at], 1)
            turned[i, 1] = roll(cur[i, 0, at], -1)
        for e in range(2):
            turned[PLANES, e] = roll(kx[PLANES - 1, e, at] * cur[PLANES - 1, e, at], 32)
            turned[PLANES + 1, e] = roll(cur[0, e, at], -32)

    def advance(alpha, beta, old, cur, new, r, turned):
        at = pl.ds(r, TILE)
        now = [cur[0, e, at] for e in range(2)]
        before = fbefore = None
        for i in range(PLANES):
            fx = [kx[i, e, at] for e in range(2)]
            inner, outer = kin[i, at], kout[i, at]
            if i + 1 < PLANES:
                after = [cur[i + 1, e, at] for e in range(2)]
            else:
                after = [turned[PLANES + 1, e] for e in range(2)]
            for e in range(2):
                near = ky[i, e, at] * cur[i, e, pl.ds(r + 1, TILE)]
                near = near + ky[i, e, pl.ds(r - 1, TILE)] * cur[i, e, pl.ds(r - 1, TILE)]
                side = turned[i, e]
                near = near + (inner * now[1 - e] + (outer * side if e else side))
                behind = fbefore[e] * before[e] if i else turned[PLANES, e]
                near = near + (fx[e] * after[e] + behind)
                near = near + rhs[i, e, at]
                centre = (1.0 + alpha) - beta * diag[i, e, at]
                new[i, e, at] = centre * now[e] - alpha * old[i, e, at] + beta * near
            before, now, fbefore = now, after, fx

    def sweep(k, old, cur, new, span, following):
        alpha, beta = steps[k, 0], steps[k, 1]
        first, count, unroll = span
        for u in range(unroll):
            r = first + TILE * u
            advance(alpha, beta, old, cur, new, r, turned if u else turned_first)
            turn_lanes(cur, r + TILE, turned)
            if u == 2:
                turn_lanes(new, following, turned_first)

        @pl.loop(1, count // unroll)
        def _(t):
            for u in range(unroll):
                r = pl.multiple_of(first + TILE * (unroll * t + u), TILE)
                advance(alpha, beta, old, cur, new, r, turned)
                turn_lanes(cur, r + TILE, turned)

    wide = (TILE, ROWS // TILE - 2, 4)
    narrow = (2 * TILE, ROWS // TILE - 4, 3)

    def three(k, spans, following):
        sweep(k, xa, xb, xc, spans[0], spans[1][0])
        sweep(k + 1, xb, xc, xa, spans[1], spans[2][0])
        sweep(k + 2, xc, xa, xb, spans[2], following[0])

    turn_lanes(xb, wide[0], turned_first)

    @pl.loop(0, 2)
    def _(m):
        three(1 + 3 * m, (wide,) * 3, wide)

    three(7, (wide, narrow, narrow), narrow)

    @pl.loop(0, 2)
    def _(m):
        three(10 + 3 * m, (narrow,) * 3, narrow)

    def mains(whole, group, within):
        parts = [jnp.where(within < 16, even, roll(odd, 16)) for even, odd in whole]
        turned = [roll(parts[i], 32 * (i % 4)) for i in range(PLANES)]
        return parts, [
            [pick(group, [turned[4 * a + (q - d) % G] for q in range(G)]) for a in range(2)] for d in range(G)
        ]

    def beside(whole, parts, group, within):
        tree = [jnp.where(within == 31, odd, even) for even, odd in whole]
        for level in range(3):
            width = 1 << level
            keep = (lax.rem(within + 1, STRIP) < width) | ((within >= 16) & (within < 16 + width))
            tree = [jnp.where(keep, tree[j], roll(tree[j + 1], width)) for j in range(0, len(tree), 2)]
        ends = roll(tree[0], 1)
        groups = (ends, ends, roll(parts[PLANES - 1], 96), roll(parts[0], 64))
        return [pick(group, [groups[(q - d) % G] for q in range(G)]) for d in range(G)]

    def load(field, row, rows):
        return [[field[i, e, pl.ds(row, rows)] for e in range(2)] for i in range(PLANES)]

    @pl.loop(0, BY // CHUNK)
    def _(t):
        row = pl.multiple_of(TOP + CHUNK * t, TILE)
        group, within = lanes_of(CHUNK, strip[0])

        def to(start):
            return pl.ds(pl.multiple_of(start + CHUNK * t, TILE), CHUNK)

        for field, start in ((xb, SIDES),) + (((kap, FIELD),) if adjoint else ()):
            whole = load(field, row, CHUNK)
            parts, main = mains(whole, group, within)
            sides = beside(whole, parts, group, within)
            for d in range(G):
                outs[d][to(start)] = sides[d]
                if field is xb:
                    for a in range(2):
                        outs[d][to(GROUP * a)] = main[d][a]

    sub = lax.broadcasted_iota(jnp.int32, (TILE, LANES), 0)
    group, within = lanes_of(TILE, strip[0])
    for field in (xb, kap) if adjoint else (xb,):
        over = mains(load(field, TOP - TILE, TILE), group, within)[1]
        under = mains(load(field, TOP + BY, TILE), group, within)[1]
        for d in range(G):
            for a in range(2):
                to = GROUP * a + BY if field is xb else KAP + TILE * a
                outs[d][to : to + TILE] = jnp.where(
                    sub == 0, pltpu.roll(over[d][a], 1, 0), pltpu.roll(under[d][a], 1, 0)
                )


def collect(strips, msgs, padded, ends, base, own):
    order = parity_order(True)

    def owners(rows):
        return [lanes_of(rows, strips[d])[0] for d in range(G)]

    def choose(owner, parts, b):
        out = parts[0]
        for d in range(1, G):
            out = jnp.where(owner[d] == b, parts[d], out)
        return roll(out, -32 * b)

    def bricks(row, rows):
        return [roll(msgs[d][pl.ds(row, rows)], -32 * d) for d in range(G)]

    sides_at, tiles_at = (SIDES, (BY, GROUP + BY)) if own is None else (FIELD, (KAP, KAP + TILE))

    @pl.loop(0, BY // CHUNK)
    def _(t):
        to = pl.ds(pl.multiple_of(TILE + CHUNK * t, TILE), CHUNK)
        owner = owners(CHUNK)
        whole, places = [], []
        if own is None:
            for a in range(2):
                parts = bricks(pl.multiple_of(GROUP * a + CHUNK * t, TILE), CHUNK)
                whole += [choose(owner, parts, b) for b in range(4)]
                places += [1 + 4 * a + b for b in range(4)]
        else:
            for c in range(BX):
                padded[1 + c, to] = own[c, pl.ds(pl.multiple_of(CHUNK * t, CHUNK), CHUNK)]
        parts = bricks(pl.multiple_of(sides_at + CHUNK * t, TILE), CHUNK)
        for side, end in enumerate((0, G - 1)):
            val = parts[0]
            for d in range(1, G):
                val = jnp.where(strips[d] == end, parts[d], val)
            ends[side, pl.ds(pl.multiple_of(CHUNK * t, CHUNK), CHUNK)] = val
        whole += [choose(owner, parts, b) for b in (2, 3)]
        places += [0, 1 + BX]
        ordered = reorder(jnp.concatenate(whole, axis=0), order)
        for j, at in enumerate(places):
            padded[at, to] = ordered[CHUNK * j : CHUNK * (j + 1)]

    owner = owners(TILE)
    whole = []
    for a in range(2):
        parts = bricks(tiles_at[a], TILE)
        whole += [choose(owner, parts, b) for b in range(4)]
    ordered = reorder(jnp.concatenate(whole, axis=0), order)
    for c in range(BX):
        val = pltpu.roll(ordered[TILE * c : TILE * (c + 1)], 7, 0)
        padded[1 + c, 0:TILE] = val
        padded[1 + c, TILE + BY : 2 * TILE + BY] = val


def across(padded, c, t):
    r8 = pl.multiple_of(WIDE * t + TILE, TILE)
    return padded[1 + c, pl.ds(r8, WIDE)], [
        padded[c, pl.ds(r8, WIDE)],
        padded[c + 2, pl.ds(r8, WIDE)],
        padded[1 + c, pl.ds(r8 - 1, WIDE)],
        padded[1 + c, pl.ds(r8 + 1, WIDE)],
    ]


def along(cell, ends, c, t):
    lane = lax.broadcasted_iota(jnp.int32, (WIDE, LANES), 1)
    low, high = (ends[side, pl.ds(pl.multiple_of(WIDE * t, WIDE), WIDE)] for side in range(2))
    return [
        jnp.where(lane == 0, roll(low, -c), roll(cell, 1)),
        jnp.where(lane == LANES - 1, roll(high, 14 - c), roll(cell, -1)),
    ]


def adjoint_kernel(strips, m0, m1, m2, m3, cond, cot, adjoint, residual, padded, kap, faces, differences, ends, kends):
    collect(strips, (m0, m1, m2, m3), padded, ends, 0, None)
    collect(strips, (m0, m1, m2, m3), kap, kends, 0, cond)

    @pl.loop(0, BY // WIDE)
    def _(t):
        at = pl.ds(pl.multiple_of(WIDE * t, WIDE), WIDE)
        for c in range(BX):
            k, knear = across(kap, c, t)
            x, xnear = across(padded, c, t)
            total = 0.0
            for kn, xn in zip(knear, xnear):
                total = total + (k + kn) * (x - xn)
            for side, (kn, xn) in enumerate(zip(along(k, kends, c, t), along(x, ends, c, t))):
                face, differ = k + kn, x - xn
                faces[side, c, at] = face
                differences[side, c, at] = differ
                total = total + face * differ
            adjoint[c, at] = x
            residual[c, at] = cot[c, at] - (x + (0.5 * TIME_STEP) * total)


def state_kernel(strips, m0, m1, m2, m3, previous, adj, kap, faces, differences, adj_residual, grad, state, residuals, padded, ends):
    collect(strips, (m0, m1, m2, m3), padded, ends, 0, None)

    @pl.loop(0, BY // WIDE)
    def _(t):
        at = pl.ds(pl.multiple_of(WIDE * t, WIDE), WIDE)
        for c in range(BX):
            k, knear = across(kap, c, t)
            x, xnear = across(padded, c, t)
            y, ynear = across(adj, c, t)
            total = product = 0.0
            for kn, xn, yn in zip(knear, xnear, ynear):
                differ = x - xn
                total = total + (k + kn) * differ
                product = product + differ * (y - yn)
            for side, xn in enumerate(along(x, ends, c, t)):
                differ = x - xn
                total = total + faces[side, c, at] * differ
                product = product + differ * differences[side, c, at]
            grad[c, at] = (-0.5 * TIME_STEP) * product
            state[c, at] = x
            residuals[0, c, at] = previous[0, c, at] - (x + (0.5 * TIME_STEP) * total)
            residuals[1, c, at] = adj_residual[c, at]


def call(kernel, outs, smem, vmem, scratch=(), micros=2, mebibytes=16):
    vm = pl.BlockSpec(memory_space=pltpu.VMEM)
    sm = pl.BlockSpec(memory_space=pltpu.SMEM)
    return pl.pallas_call(
        kernel,
        out_shape=[jax.ShapeDtypeStruct(shape, F32) for shape in outs],
        in_specs=[sm] * len(smem) + [vm] * len(vmem),
        out_specs=[vm] * len(outs),
        scratch_shapes=[pltpu.VMEM(shape, F32) for shape in scratch],
        compiler_params=pltpu.CompilerParams(vmem_limit_bytes=mebibytes * 1024 * 1024),
        cost_estimate=pl.CostEstimate(flops=0, bytes_accessed=micros * 3_000_000, transcendentals=0),
    )(*smem, *vmem)


def shifted(x, axis, by):
    count = lax.axis_size(axis)
    return lax.ppermute(x, axis, [(i, (i + by) % count) for i in range(count)])


def around(x, by):
    order = [2 * g for g in range(G)] + [2 * g + 1 for g in reversed(range(G))]
    return lax.ppermute(x, ("gx", "pa"), [(at, order[(i + by) % len(order)]) for i, at in enumerate(order)])


def redistributed(conductivity, stored_state, row_scales, cotangent, upper_bound):
    g = lax.axis_index("gx")
    pa = lax.axis_index("pa")

    def strip_of(device):
        return jnp.where(pa == 0, device, G - 1 - device)

    steps = jnp.arange(G, dtype=jnp.int32)
    ahead = lax.rem(g + steps, G)
    behind = lax.rem(g - steps + G, G)
    strip = strip_of(g)
    left_g = jnp.where(pa == 0, jnp.maximum(g - 1, 0), jnp.minimum(g + 1, G - 1))
    right_g = jnp.where(pa == 0, jnp.minimum(g + 1, G - 1), jnp.maximum(g - 1, 0))
    places = lax.rem(jnp.stack((left_g - g + steps, right_g - g + steps)) + G, G)

    brick = (2, 2, BY, LANES)
    parts = call(pack_kernel, [brick] * G, [strip_of(ahead)], [conductivity, cotangent])
    parts, stored_state = lax.optimization_barrier((parts, stored_state))
    parts = [parts[0]] + [shifted(parts[d], "gx", d) for d in range(1, G)]
    stored = shifted(stored_state, "pa", 1)
    both = jnp.stack((stored, stored_state)).astype(F32) * row_scales[:, :, None]
    above_rows = shifted(both[:, :, BY - HALO :], "gy", 1)
    below_rows = shifted(both[:, :, :HALO], "gy", -1)
    parts, above_rows, below_rows = lax.optimization_barrier((parts, above_rows, below_rows))
    edge = (2, G, BY, LANES)
    rim = (2, G, 4, HALO, LANES)
    to_left, to_right = call(edge_kernel, [edge, edge], [places], parts)
    to_left, below_rows = lax.optimization_barrier((to_left, below_rows))
    *messages, steps_here = call(
        pack_previous_kernel,
        [(4, EXTENDED, LANES)] * G + [(CHEB, 2, TILE, LANES)],
        [strip_of(ahead), upper_bound],
        [both, above_rows, below_rows],
    )
    from_left, from_right = around(to_right, 1), around(to_left, -1)
    from_left, from_right, own = lax.optimization_barrier((from_left, from_right, messages[0]))
    head, tail = call(rows_kernel, [rim, rim], [], [*parts, from_left, from_right])
    halos = [from_left, from_right, shifted(tail, "gy", 1), shifted(head, "gy", -1)]

    second = [own] + [shifted(messages[d], "gx", d) for d in range(1, G)]

    line = (PLANES, 2, ROWS, LANES)
    half = (PLANES, ROWS, LANES)
    lines = [line] * 4 + [(PLANES + 2, 2, TILE, LANES)] * 2
    setup = [strip[None]]

    def home(solved):
        return [solved[0]] + [shifted(solved[d], "gx", d) for d in range(1, G)]

    *solved_adjoint, kx, ky, kin, kout, diag = call(
        functools.partial(solve_kernel, True),
        [(BOTH, LANES)] * G + [line, line, half, half, line],
        setup,
        [steps_here, *parts, *halos],
        [line] + lines,
        micros=25,
        mebibytes=24,
    )
    solved_adjoint = home(solved_adjoint)
    solved_state = home(
        call(
            functools.partial(solve_kernel, False),
            [(FIELD, LANES)] * G,
            setup,
            [steps_here, *second, kx, ky, kin, kout, diag],
            lines,
            micros=25,
            mebibytes=24,
        )
    )

    out = (BX, BY, LANES)
    padded = (BX + 2, BY + 16, LANES)
    ends = (2, BY, LANES)
    here = strip_of(behind)
    adjoint, adj_residual, adj, kap, faces, differences = call(
        adjoint_kernel,
        [out, out, padded, padded, (2,) + out, (2,) + out],
        [here],
        [*solved_adjoint, conductivity, cotangent],
        [ends, ends],
    )
    grad, state, residuals = call(
        state_kernel,
        [out, out, (2,) + out],
        [here],
        [*solved_state, both, adj, kap, faces, differences, adj_residual],
        [padded, ends],
    )
    return grad, adjoint, state, residuals


def body(conductivity, stored_state, row_scales, cotangent, upper_bound):
    strips_fit = (
        lax.axis_size("gx") == G
        and lax.axis_size("pa") == 2
        and conductivity.shape == (BX, BY, BZ)
    )
    run = redistributed if strips_fit else stepwise
    return tuple(run(conductivity, stored_state, row_scales, cotangent, upper_bound))


def solution(mesh):
    return jax.shard_map(
        body,
        mesh=mesh,
        in_specs=(
            P("gx", "gy", "pa"),
            P("gx", "gy", "pa"),
            P("gx", "gy"),
            P("gx", "gy", "pa"),
            P(),
        ),
        out_specs=(
            P("gx", "gy", "pa"),
            P("gx", "gy", "pa"),
            P("gx", "gy", "pa"),
            P(None, "gx", "gy", "pa"),
        ),
        check_vma=False,
    )
```

```python
import functools

import jax
import jax.numpy as jnp
from jax import lax
from jax.experimental import pallas as pl
from jax.experimental.pallas import tpu as pltpu
from jax.sharding import PartitionSpec as P

CHEB = 16
LANES = 128
HALO = CHEB
TIME_STEP = 8.0
F32 = jnp.float32


def with_halo(cells, sides, width):
    for axis, dim in sides:
        count = lax.axis_size(axis)
        head = lax.slice_in_dim(cells, 0, width, axis=dim)
        tail = lax.slice_in_dim(cells, cells.shape[dim] - width, cells.shape[dim], axis=dim)
        cells = jnp.concatenate(
            [
                lax.ppermute(tail, axis, [(i, (i + 1) % count) for i in range(count)]),
                cells,
                lax.ppermute(head, axis, [((i + 1) % count, i) for i in range(count)]),
            ],
            axis=dim,
        )
    return cells


def region(arr, spatial, offset):
    extent = arr.shape[-3:]
    window = [slice(1, length - 1) for length in extent]
    window[spatial] = slice(offset, extent[spatial] - 2 + offset)
    leading = [slice(None)] * (arr.ndim - 3)
    return arr[tuple(leading + window)]


def apply_operator(padded, kpad):
    centre = region(padded, 0, 1)
    kcentre = region(kpad, 0, 1)
    summed = jnp.zeros_like(centre)
    for spatial in range(3):
        for offset in (0, 2):
            summed = summed + 0.5 * (kcentre + region(kpad, spatial, offset)) * (
                centre - region(padded, spatial, offset)
            )
    return centre + TIME_STEP * summed


def stepwise(conductivity, stored_state, row_scales, cotangent, upper_bound):
    upper = upper_bound[0]
    kpad = with_halo(conductivity, (("gx", 0), ("gy", 1), ("pa", 2)), 1)
    count = lax.axis_size("pa")
    partner = lax.ppermute(stored_state, "pa", [(i, (i + count // 2) % count) for i in range(count)])
    previous = partner.astype(F32) * row_scales[:, :, None]
    rhs = jnp.stack((previous, cotangent))
    theta = 0.5 * (upper + 1.0)
    delta = 0.5 * (upper - 1.0)
    sigma = theta / delta
    sides = (("gx", 1), ("gy", 2), ("pa", 3))

    def sweep(step, carry):
        solved, residual, direction, rho = carry
        padded = with_halo(direction, sides, 1)
        solved = solved + direction
        residual = residual - apply_operator(padded, kpad)
        rho_next = 1.0 / (2.0 * sigma - rho)
        direction = rho_next * rho * direction + 2.0 * rho_next / delta * residual
        return (solved, residual, direction, rho_next)

    start = (jnp.zeros_like(rhs), rhs, rhs / theta, 1.0 / sigma)
    solved, residual, _, _ = lax.fori_loop(0, CHEB, sweep, start)
    pair = with_halo(solved, sides, 1)
    centre = region(pair, 0, 1)
    summed = jnp.zeros_like(solved[0])
    for spatial in range(3):
        for offset in (0, 2):
            differ = centre - region(pair, spatial, offset)
            summed = summed + differ[0] * differ[1]
    return (-0.5 * TIME_STEP * summed, solved[1], solved[0], residual)


G = 4
BX = 8
BY = 128
BZ = 128
STRIP = BZ // G
TOP = 8 + HALO
ROWS = BY + 2 * TOP
EXTENDED = BY + 2 * HALO
TILES = 2 * BY
SIDES = TILES + 8
ENDS = SIDES + BY // 2
FIELD = ENDS + 16
OWN = FIELD - TILES
BOTH = FIELD + OWN
TILE = 8
CHUNK = 32
WIDE = 16

BLOCK = (0, 3, 2, 1)
PLANES = BX


def roll(x, by):
    by %= LANES
    return pltpu.roll(x, by, 1) if by else x


def lanes_of(rows, strip):
    lane = lax.broadcasted_iota(jnp.int32, (rows, LANES), 1)
    return lax.rem(lane // STRIP - strip + 2 * G, G), lax.rem(lane, STRIP)


def pick(group, parts):
    out = parts[0]
    for b in range(1, G):
        out = jnp.where(group == b, parts[b], out)
    return out


def parity_order(transposed):
    src = lax.broadcasted_iota(jnp.int32, (LANES, LANES), 1 if transposed else 0)
    dst = lax.broadcasted_iota(jnp.int32, (LANES, LANES), 0 if transposed else 1)
    within = lax.rem(src, STRIP)
    place = src - within + 16 * lax.rem(within, 2) + within // 2
    return jnp.where(place == dst, 1.0, 0.0).astype(jnp.bfloat16)


def reorder(x, order):
    if x.dtype == jnp.bfloat16:
        return jnp.dot(x, order, preferred_element_type=F32)
    high = x.astype(jnp.bfloat16)
    rest = x - high.astype(F32)
    middle = rest.astype(jnp.bfloat16)
    low = (rest - middle.astype(F32)).astype(jnp.bfloat16)
    return (
        jnp.dot(high, order, preferred_element_type=F32)
        + jnp.dot(middle, order, preferred_element_type=F32)
        + jnp.dot(low, order, preferred_element_type=F32)
    )


def pack_kernel(strips, *refs):
    ins, outs = refs[: len(refs) - G], refs[len(refs) - G :]
    order = parity_order(False)
    groups = [lanes_of(BY, strips[d])[0] for d in range(G)]
    for n, array in enumerate(ins):
        for a in range(2):
            planes = reorder(array[4 * a : 4 * a + 4].reshape(4 * BY, LANES), order)
            parts = [roll(planes[BY * b : BY * (b + 1)], 32 * b) for b in range(4)]
            for d in range(G):
                outs[d][n, a] = pick(groups[d], parts)


def chebyshev_steps(upper, steps):
    bound = jnp.full((TILE, LANES), upper[0])
    theta = 0.5 * (bound + 1.0)
    delta = 0.5 * (bound - 1.0)
    sigma = theta / delta
    rho = 1.0 / sigma
    steps[0, 0] = 1.0 / theta
    steps[0, 1] = jnp.zeros_like(theta)
    for k in range(1, CHEB):
        rho_next = 1.0 / (2.0 * sigma - rho)
        steps[k, 0] = rho_next * rho
        steps[k, 1] = 2.0 * rho_next / delta
        rho = rho_next


def pack_previous_kernel(strips, upper, both, above, below, *outs):
    *outs, steps = outs
    chebyshev_steps(upper, steps)
    src = lax.broadcasted_iota(jnp.int32, (2 * LANES, 2 * LANES), 0)
    dst = lax.broadcasted_iota(jnp.int32, (2 * LANES, 2 * LANES), 1)
    place = LANES * lax.rem(src, 2) + 64 * (src // LANES) + lax.rem(src, LANES) // 2
    order = jnp.where(place == dst, 1.0, 0.0).astype(jnp.bfloat16)

    def give(planes, rows, start):
        groups = [lanes_of(rows, strips[d])[0] for d in range(G)]
        for m in range(4):
            pieces = []
            for i in (2 * m, 2 * m + 1):
                pair = planes[rows * i : rows * (i + 1)]
                for e in range(2):
                    pieces.append(pair[:, LANES * e : LANES * (e + 1)])
            for d in range(G):
                turned = [pltpu.roll(pieces[k], lax.rem(16 * strips[d] + 32 * k + 8, LANES), 1) for k in range(4)]
                outs[d][m, pl.ds(start, rows)] = pick(groups[d], turned)

    @pl.loop(0, BY // CHUNK)
    def _(t):
        r = pl.multiple_of(CHUNK * t, CHUNK)
        halves = [both[half, :, pl.ds(r, CHUNK)].reshape(BX * CHUNK, LANES) for half in range(2)]
        give(reorder(jnp.concatenate(halves, axis=1), order), CHUNK, pl.multiple_of(HALO + CHUNK * t, HALO))

    for start, array in ((0, above), (HALO + BY, below)):
        halves = [array[half].reshape(BX * HALO, LANES) for half in range(2)]
        give(reorder(jnp.concatenate(halves, axis=1), order), HALO, start)


def edge_kernel(places, *refs):
    msgs, (to_left, to_right, head, tail) = refs[:G], refs[G:]
    lane = lax.broadcasted_iota(jnp.int32, (BY, LANES), 1)
    low = lax.rem(lane, 16) < 8
    for n in range(2):
        for d in range(G):
            first, second = msgs[d][n, 0], msgs[d][n, 1]
            to_left[n, places[0, d]] = jnp.where(low, first, roll(second, 8))
            to_right[n, places[1, d]] = jnp.where(low, roll(second, -8), first)
            for a in range(2):
                head[n, d, a] = msgs[d][n, a, :HALO]
                tail[n, d, a] = msgs[d][n, a, BY - HALO :]


def rows_kernel(from_left, from_right, above, below, head, tail, above_out, below_out):
    for n in range(2):
        for d in range(G):
            for out, rows in ((head, slice(0, HALO)), (tail, slice(BY - HALO, BY))):
                for a, side in enumerate((from_left, from_right)):
                    out[n, d, a] = side[n, d, rows]
            above_out[n, d] = above[n, d]
            below_out[n, d] = below[n, d]


def unpack(get_brick, get_edge, group, within, put):
    by_block = [BLOCK.index(q) for q in range(G)]
    edges = [[get_edge(side, d) for d in by_block] for side in range(2)]
    for a in range(2):
        far = 24 if a else 16
        own = [roll(get_brick(by_block[q], a), 32 * q) for q in range(G)]
        below = [roll(edges[0][q], 32 * q + far) for q in range(G)]
        above = [roll(edges[1][q], 32 * q - far) for q in range(G)]
        even = [
            jnp.where(within < 16, own[q], jnp.where(within < 24, above[q], below[(q + 1) % G])) for q in range(G)
        ]
        odd = [
            jnp.where(within < 8, above[(q - 1) % G], jnp.where(within < 16, below[q], own[q])) for q in range(G)
        ]
        for b in range(4):
            for e, parts in enumerate((even, odd)):
                whole = pick(group, [parts[(q - b) % G] for q in range(G)])
                put(4 * a + b, e, roll(whole, -32 * b - 16 * e))


def unpack_strip(get, group, put):
    by_block = [BLOCK.index(q) for q in range(G)]
    for m in range(4):
        turned = [roll(get(by_block[q], m), 32 * q) for q in range(G)]
        for k in range(4):
            whole = pick(group, [turned[(q - k) % G] for q in range(G)])
            put(2 * m + k // 2, k % 2, roll(whole, -32 * k - 8))


def solve_kernel(adjoint, strip, steps, *refs):
    if adjoint:
        bricks, (from_left, from_right, above, below, above_edge, below_edge) = refs[:G], refs[G : G + 6]
        outs, coefficients, (kap, *scratch) = refs[G + 6 : 2 * G + 6], refs[2 * G + 6 : 2 * G + 11], refs[2 * G + 11 :]
    else:
        strips_here, coefficients = refs[:G], refs[G : G + 5]
        outs, scratch = refs[G + 5 : 2 * G + 5], refs[2 * G + 5 :]
    kx, ky, kin, kout, diag = coefficients
    rhs, xa, xb, xc, turned, turned_first = scratch
    zero = jnp.zeros((TILE, LANES), F32)
    theta_inv = jnp.concatenate([steps[0, 0]] * 2, axis=0)

    def put_at(dst, to, rows):
        def put(i, e, val):
            dst[i, e, pl.ds(to, rows)] = val

        return put

    for i in range(PLANES):
        for e in range(2):
            for dst in (rhs, xa, xb, xc) + ((kap, ky) if adjoint else ()):
                dst[i, e, 0:TILE] = zero
                dst[i, e, ROWS - TILE : ROWS] = zero
        for dst in (kin, kout) if adjoint else ():
            dst[i, 0:TILE] = zero
            dst[i, ROWS - TILE : ROWS] = zero

    if adjoint:
        sides = (from_left, from_right)

        @pl.loop(0, BY // CHUNK)
        def _(t):
            at = pl.ds(pl.multiple_of(CHUNK * t, CHUNK), CHUNK)
            group, within = lanes_of(CHUNK, strip[0])
            for n, dst in enumerate((kap, rhs)):
                unpack(
                    lambda d, a: bricks[d][n, a, at],
                    lambda side, d: sides[side][n, d, at],
                    group,
                    within,
                    put_at(dst, pl.multiple_of(TOP + CHUNK * t, TILE), CHUNK),
                )

        group_halo, within_halo = lanes_of(HALO, strip[0])
        for n, dst in enumerate((kap, rhs)):
            for brick, edge, start in ((above, above_edge, TOP - HALO), (below, below_edge, TOP + BY)):
                unpack(
                    lambda d, a: brick[n, d, a],
                    lambda side, d: edge[n, d, side],
                    group_halo,
                    within_halo,
                    put_at(dst, start, HALO),
                )
    else:

        @pl.loop(0, EXTENDED // CHUNK)
        def _(t):
            at = pl.ds(pl.multiple_of(CHUNK * t, CHUNK), CHUNK)
            group, _ = lanes_of(CHUNK, strip[0])
            unpack_strip(
                lambda d, m: strips_here[d][m, at],
                group,
                put_at(rhs, pl.multiple_of(TOP - HALO + CHUNK * t, TILE), CHUNK),
            )

    @pl.loop(0, (ROWS // TILE - 2) // 2)
    def _(t):
        rows = 2 * TILE
        r = pl.multiple_of(TILE + rows * t, TILE)
        at = pl.ds(r, rows)
        for i in range(PLANES):
            for e in range(2):
                xb[i, e, at] = rhs[i, e, at] * theta_inv
                xa[i, e, at] = jnp.zeros((rows, LANES), F32)
        if not adjoint:
            return
        first = [kap[0, e, at] for e in range(2)]
        now = first
        before = [4.0 * (k + roll(kap[PLANES - 1, e, at], 32)) for e, k in enumerate(first)]
        for i in range(PLANES):
            after = [kap[i + 1, e, at] if i + 1 < PLANES else roll(first[e], -32) for e in range(2)]
            inner = 4.0 * (now[0] + now[1])
            outer = 4.0 * (now[1] + roll(now[0], -1))
            outer_before = 4.0 * (now[0] + roll(now[1], 1))
            kin[i, at] = inner
            kout[i, at] = outer
            along = (inner + outer_before, inner + outer)
            for e in range(2):
                fx = 4.0 * (now[e] + after[e])
                fy = 4.0 * (now[e] + kap[i, e, pl.ds(r + 1, rows)])
                fym = 4.0 * (now[e] + kap[i, e, pl.ds(r - 1, rows)])
                kx[i, e, at] = fx
                ky[i, e, at] = fy
                diag[i, e, at] = 1.0 + (fx + before[e] + (fy + fym) + along[e])
                before[e] = fx
            now = after

    def turn_lanes(cur, r, turned):
        at = pl.ds(r, TILE)
        for i in range(PLANES):
            turned[i, 0] = roll(kout[i, at] * cur[i, 1, at], 1)
            turned[i, 1] = roll(cur[i, 0, at], -1)
        for e in range(2):
            turned[PLANES, e] = roll(kx[PLANES - 1, e, at] * cur[PLANES - 1, e, at], 32)
            turned[PLANES + 1, e] = roll(cur[0, e, at], -32)

    def advance(alpha, beta, old, cur, new, r, turned):
        at = pl.ds(r, TILE)
        now = [cur[0, e, at] for e in range(2)]
        before = fbefore = None
        for i in range(PLANES):
            fx = [kx[i, e, at] for e in range(2)]
            inner, outer = kin[i, at], kout[i, at]
            if i + 1 < PLANES:
                after = [cur[i + 1, e, at] for e in range(2)]
            else:
                after = [turned[PLANES + 1, e] for e in range(2)]
            for e in range(2):
                near = ky[i, e, at] * cur[i, e, pl.ds(r + 1, TILE)]
                near = near + ky[i, e, pl.ds(r - 1, TILE)] * cur[i, e, pl.ds(r - 1, TILE)]
                side = turned[i, e]
                near = near + (inner * now[1 - e] + (outer * side if e else side))
                behind = fbefore[e] * before[e] if i else turned[PLANES, e]
                near = near + (fx[e] * after[e] + behind)
                near = near + rhs[i, e, at]
                centre = (1.0 + alpha) - beta * diag[i, e, at]
                new[i, e, at] = centre * now[e] - alpha * old[i, e, at] + beta * near
            before, now, fbefore = now, after, fx

    def sweep(k, old, cur, new, span, following):
        alpha, beta = steps[k, 0], steps[k, 1]
        first, count, unroll = span
        for u in range(unroll):
            r = first + TILE * u
            advance(alpha, beta, old, cur, new, r, turned if u else turned_first)
            turn_lanes(cur, r + TILE, turned)
            if u == 2:
                turn_lanes(new, following, turned_first)

        @pl.loop(1, count // unroll)
        def _(t):
            for u in range(unroll):
                r = pl.multiple_of(first + TILE * (unroll * t + u), TILE)
                advance(alpha, beta, old, cur, new, r, turned)
                turn_lanes(cur, r + TILE, turned)

    wide = (TILE, ROWS // TILE - 2, 4)
    narrow = (2 * TILE, ROWS // TILE - 4, 3)

    def three(k, spans, following):
        sweep(k, xa, xb, xc, spans[0], spans[1][0])
        sweep(k + 1, xb, xc, xa, spans[1], spans[2][0])
        sweep(k + 2, xc, xa, xb, spans[2], following[0])

    turn_lanes(xb, wide[0], turned_first)

    @pl.loop(0, 2)
    def _(m):
        three(1 + 3 * m, (wide,) * 3, wide)

    three(7, (wide, narrow, narrow), narrow)

    @pl.loop(0, 2)
    def _(m):
        three(10 + 3 * m, (narrow,) * 3, narrow)

    def mains(whole, group, within):
        parts = [jnp.where(within < 16, even, roll(odd, 16)) for even, odd in whole]
        turned = [roll(parts[i], 32 * (i % 4)) for i in range(PLANES)]
        return parts, [
            [pick(group, [turned[4 * a + (q - d) % G] for q in range(G)]) for a in range(2)] for d in range(G)
        ]

    def ends_of(whole, within):
        tree = [jnp.where(within == 31, odd, even) for even, odd in whole]
        for level in range(3):
            width = 1 << level
            keep = (lax.rem(within + 1, STRIP) < width) | ((within >= 16) & (within < 16 + width))
            tree = [jnp.where(keep, tree[j], roll(tree[j + 1], width)) for j in range(0, len(tree), 2)]
        return jnp.where(within < 8, roll(tree[0], 1), roll(tree[0], -8))

    def load(field, row, rows):
        return [[field[i, e, pl.ds(row, rows)] for e in range(2)] for i in range(PLANES)]

    fields = ((xb, 0),) + (((kap, FIELD - TILES),) if adjoint else ())

    @pl.loop(0, BY // 2 // CHUNK)
    def _(t):
        group, within = lanes_of(CHUNK, strip[0])
        for field, base in fields:
            beside = []
            for upper_rows in range(2):
                start = BY // 2 * upper_rows
                parts, main = mains(load(field, pl.multiple_of(TOP + start + CHUNK * t, TILE), CHUNK), group, within)
                if field is xb:
                    for d in range(G):
                        for a in range(2):
                            outs[d][pl.ds(pl.multiple_of(BY * a + start + CHUNK * t, TILE), CHUNK)] = main[d][a]
                beside += [roll(parts[PLANES - 1], 32 + 64 * upper_rows), roll(parts[0], 64 * upper_rows)]
            at = pl.ds(pl.multiple_of(base + SIDES + CHUNK * t, TILE), CHUNK)
            for d in range(G):
                outs[d][at] = pick(group, [beside[(q - d) % G] for q in range(G)])

    sub = lax.broadcasted_iota(jnp.int32, (TILE, LANES), 0)
    group, within = lanes_of(TILE, strip[0])
    group_run, within_run = lanes_of(16, strip[0])
    half_run = within_run // 16
    for field, base in fields:
        over = mains(load(field, TOP - TILE, TILE), group, within)[1]
        under = mains(load(field, TOP + BY, TILE), group, within)[1]
        for d in range(G):
            rows = [pltpu.roll(v, by, 0) for a, by in ((0, 1), (1, 3)) for v in (over[d][a], under[d][a])]
            tile = rows[3]
            for j in range(3):
                tile = jnp.where(sub == j, rows[j], tile)
            outs[d][base + TILES : base + TILES + TILE] = tile
        runs = [roll(ends_of(load(field, TOP + 16 * run, 16), within_run), 16 * run) for run in range(8)]
        evens = [pick(group_run, [runs[2 * ((q - d) % G)] for q in range(G)]) for d in range(G)]
        odds = [pick(group_run, [runs[2 * ((q - d) % G) + 1] for q in range(G)]) for d in range(G)]
        for d in range(G):
            outs[d][base + ENDS : base + ENDS + 16] = jnp.where(half_run == 0, evens[d], odds[d])


def collect(strips, msgs, padded, ends, own):
    order = parity_order(True)

    def owners(rows):
        return [lanes_of(rows, strips[d])[0] for d in range(G)]

    def choose(owner, parts, b):
        out = parts[0]
        for d in range(1, G):
            out = jnp.where(owner[d] == b, parts[d], out)
        return roll(out, -32 * b)

    def bricks(row, rows):
        return [roll(msgs[d][pl.ds(row, rows)], -32 * d) for d in range(G)]

    base = 0 if own is None else FIELD - TILES

    @pl.loop(0, BY // CHUNK)
    def _(t):
        to = pl.ds(pl.multiple_of(TILE + CHUNK * t, TILE), CHUNK)
        if own is not None:
            for c in range(BX):
                padded[1 + c, to] = own[c, pl.ds(pl.multiple_of(CHUNK * t, CHUNK), CHUNK)]
            return
        owner = owners(CHUNK)
        whole = []
        for a in range(2):
            parts = bricks(pl.multiple_of(BY * a + CHUNK * t, TILE), CHUNK)
            whole += [choose(owner, parts, b) for b in range(4)]
        ordered = reorder(jnp.concatenate(whole, axis=0), order)
        for c in range(BX):
            padded[1 + c, to] = ordered[CHUNK * c : CHUNK * (c + 1)]

    @pl.loop(0, BY // 2 // CHUNK)
    def _(t):
        owner = owners(CHUNK)
        parts = bricks(pl.multiple_of(base + SIDES + CHUNK * t, TILE), CHUNK)
        ordered = reorder(jnp.concatenate([choose(owner, parts, b) for b in range(4)], axis=0), order)
        for j, (at, start) in enumerate(((0, 0), (1 + BX, 0), (0, BY // 2), (1 + BX, BY // 2))):
            to = pl.ds(pl.multiple_of(TILE + start + CHUNK * t, TILE), CHUNK)
            padded[at, to] = ordered[CHUNK * j : CHUNK * (j + 1)]

    parts = bricks(base + ENDS, 16)
    for side, end in enumerate((0, G - 1)):
        val = parts[0]
        for d in range(1, G):
            val = jnp.where(strips[d] == end, parts[d], val)
        ends[side] = val

    owner = owners(TILE)
    parts = bricks(base + TILES, TILE)
    ordered = reorder(jnp.concatenate([choose(owner, parts, b) for b in range(4)], axis=0), order)
    for c in range(BX):
        val = pltpu.roll(ordered[TILE * (c % 4) : TILE * (c % 4 + 1)], 5 if c >= 4 else 7, 0)
        padded[1 + c, 0:TILE] = val
        padded[1 + c, TILE + BY : 2 * TILE + BY] = val


def across(padded, c, t):
    r8 = pl.multiple_of(WIDE * t + TILE, TILE)
    return padded[1 + c, pl.ds(r8, WIDE)], [
        padded[c, pl.ds(r8, WIDE)],
        padded[c + 2, pl.ds(r8, WIDE)],
        padded[1 + c, pl.ds(r8 - 1, WIDE)],
        padded[1 + c, pl.ds(r8 + 1, WIDE)],
    ]


def along(cell, ends, c, t):
    lane = lax.broadcasted_iota(jnp.int32, (WIDE, LANES), 1)
    low = pltpu.roll(ends[0], lax.rem(LANES - 16 * t - c + LANES, LANES), 1)
    high = pltpu.roll(ends[1], lax.rem(23 - 16 * t - c + 2 * LANES, LANES), 1)
    return [
        jnp.where(lane == 0, low, roll(cell, 1)),
        jnp.where(lane == LANES - 1, high, roll(cell, -1)),
    ]


def adjoint_kernel(strips, m0, m1, m2, m3, cond, cot, adjoint, residual, padded, kap, faces, differences, ends, kends):
    collect(strips, (m0, m1, m2, m3), padded, ends, None)
    collect(strips, (m0, m1, m2, m3), kap, kends, cond)

    @pl.loop(0, BY // WIDE)
    def _(t):
        at = pl.ds(pl.multiple_of(WIDE * t, WIDE), WIDE)
        for c in range(BX):
            k, knear = across(kap, c, t)
            x, xnear = across(padded, c, t)
            total = 0.0
            for kn, xn in zip(knear, xnear):
                total = total + (k + kn) * (x - xn)
            for side, (kn, xn) in enumerate(zip(along(k, kends, c, t), along(x, ends, c, t))):
                face, differ = k + kn, x - xn
                faces[side, c, at] = face
                differences[side, c, at] = differ
                total = total + face * differ
            adjoint[c, at] = x
            residual[c, at] = cot[c, at] - (x + (0.5 * TIME_STEP) * total)


def state_kernel(strips, m0, m1, m2, m3, previous, adj, kap, faces, differences, adj_residual, grad, state, residuals, padded, ends):
    collect(strips, (m0, m1, m2, m3), padded, ends, None)

    @pl.loop(0, BY // WIDE)
    def _(t):
        at = pl.ds(pl.multiple_of(WIDE * t, WIDE), WIDE)
        for c in range(BX):
            k, knear = across(kap, c, t)
            x, xnear = across(padded, c, t)
            y, ynear = across(adj, c, t)
            total = product = 0.0
            for kn, xn, yn in zip(knear, xnear, ynear):
                differ = x - xn
                total = total + (k + kn) * differ
                product = product + differ * (y - yn)
            for side, xn in enumerate(along(x, ends, c, t)):
                differ = x - xn
                total = total + faces[side, c, at] * differ
                product = product + differ * differences[side, c, at]
            grad[c, at] = (-0.5 * TIME_STEP) * product
            state[c, at] = x
            residuals[0, c, at] = previous[0, c, at] - (x + (0.5 * TIME_STEP) * total)
            residuals[1, c, at] = adj_residual[c, at]


def call(kernel, outs, smem, vmem, scratch=(), micros=2, mebibytes=16):
    vm = pl.BlockSpec(memory_space=pltpu.VMEM)
    sm = pl.BlockSpec(memory_space=pltpu.SMEM)
    return pl.pallas_call(
        kernel,
        out_shape=[jax.ShapeDtypeStruct(shape, F32) for shape in outs],
        in_specs=[sm] * len(smem) + [vm] * len(vmem),
        out_specs=[vm] * len(outs),
        scratch_shapes=[pltpu.VMEM(shape, F32) for shape in scratch],
        compiler_params=pltpu.CompilerParams(vmem_limit_bytes=mebibytes * 1024 * 1024),
        cost_estimate=pl.CostEstimate(flops=0, bytes_accessed=micros * 3_000_000, transcendentals=0),
    )(*smem, *vmem)


def shifted(x, axis, by):
    count = lax.axis_size(axis)
    return lax.ppermute(x, axis, [(i, (i + by) % count) for i in range(count)])


def around(x, by):
    order = [2 * g for g in range(G)] + [2 * g + 1 for g in reversed(range(G))]
    return lax.ppermute(x, ("gx", "pa"), [(at, order[(i + by) % len(order)]) for i, at in enumerate(order)])


def redistributed(conductivity, stored_state, row_scales, cotangent, upper_bound):
    g = lax.axis_index("gx")
    pa = lax.axis_index("pa")

    def strip_of(device):
        return jnp.where(pa == 0, device, G - 1 - device)

    steps = jnp.arange(G, dtype=jnp.int32)
    ahead = lax.rem(g + steps, G)
    behind = lax.rem(g - steps + G, G)
    strip = strip_of(g)
    left_g = jnp.where(pa == 0, jnp.maximum(g - 1, 0), jnp.minimum(g + 1, G - 1))
    right_g = jnp.where(pa == 0, jnp.minimum(g + 1, G - 1), jnp.maximum(g - 1, 0))
    places = lax.rem(jnp.stack((left_g - g + steps, right_g - g + steps)) + G, G)

    brick = (2, 2, BY, LANES)
    parts = call(pack_kernel, [brick] * G, [strip_of(ahead)], [conductivity, cotangent])
    parts, stored_state = lax.optimization_barrier((parts, stored_state))
    parts = [parts[0]] + [shifted(parts[d], "gx", d) for d in range(1, G)]
    stored = shifted(stored_state, "pa", 1)
    both = jnp.stack((stored, stored_state)).astype(F32) * row_scales[:, :, None]
    above_rows = shifted(both[:, :, BY - HALO :], "gy", 1)
    below_rows = shifted(both[:, :, :HALO], "gy", -1)
    parts, above_rows, below_rows = lax.optimization_barrier((parts, above_rows, below_rows))
    edge = (2, G, BY, LANES)
    rim = (2, G, 2, HALO, LANES)
    to_left, to_right, head, tail = call(edge_kernel, [edge, edge, rim, rim], [places], parts)
    to_left, below_rows = lax.optimization_barrier((to_left, below_rows))
    *messages, steps_here = call(
        pack_previous_kernel,
        [(4, EXTENDED, LANES)] * G + [(CHEB, 2, TILE, LANES)],
        [strip_of(ahead), upper_bound],
        [both, above_rows, below_rows],
    )
    from_left, from_right = around(to_right, 1), around(to_left, -1)
    above, below = shifted(tail, "gy", 1), shifted(head, "gy", -1)
    from_left, from_right, own = lax.optimization_barrier((from_left, from_right, messages[0]))
    head, tail, above, below = call(rows_kernel, [rim] * 4, [], [from_left, from_right, above, below])
    halos = [from_left, from_right, above, below, shifted(tail, "gy", 1), shifted(head, "gy", -1)]

    second = [own] + [shifted(messages[d], "gx", d) for d in range(1, G)]

    line = (PLANES, 2, ROWS, LANES)
    half = (PLANES, ROWS, LANES)
    lines = [line] * 4 + [(PLANES + 2, 2, TILE, LANES)] * 2
    setup = [strip[None]]

    def home(solved):
        return [solved[0]] + [shifted(solved[d], "gx", d) for d in range(1, G)]

    *solved_adjoint, kx, ky, kin, kout, diag = call(
        functools.partial(solve_kernel, True),
        [(BOTH, LANES)] * G + [line, line, half, half, line],
        setup,
        [steps_here, *parts, *halos],
        [line] + lines,
        micros=25,
        mebibytes=24,
    )
    solved_adjoint = home(solved_adjoint)
    solved_state = home(
        call(
            functools.partial(solve_kernel, False),
            [(FIELD, LANES)] * G,
            setup,
            [steps_here, *second, kx, ky, kin, kout, diag],
            lines,
            micros=25,
            mebibytes=24,
        )
    )

    out = (BX, BY, LANES)
    padded = (BX + 2, BY + 16, LANES)
    ends = (2, 16, LANES)
    here = strip_of(behind)
    adjoint, adj_residual, adj, kap, faces, differences = call(
        adjoint_kernel,
        [out, out, padded, padded, (2,) + out, (2,) + out],
        [here],
        [*solved_adjoint, conductivity, cotangent],
        [ends, ends],
    )
    grad, state, residuals = call(
        state_kernel,
        [out, out, (2,) + out],
        [here],
        [*solved_state, both, adj, kap, faces, differences, adj_residual],
        [padded, ends],
    )
    return grad, adjoint, state, residuals


def body(conductivity, stored_state, row_scales, cotangent, upper_bound):
    strips_fit = (
        lax.axis_size("gx") == G
        and lax.axis_size("pa") == 2
        and conductivity.shape == (BX, BY, BZ)
    )
    run = redistributed if strips_fit else stepwise
    return tuple(run(conductivity, stored_state, row_scales, cotangent, upper_bound))


def solution(mesh):
    return jax.shard_map(
        body,
        mesh=mesh,
        in_specs=(
            P("gx", "gy", "pa"),
            P("gx", "gy", "pa"),
            P("gx", "gy"),
            P("gx", "gy", "pa"),
            P(),
        ),
        out_specs=(
            P("gx", "gy", "pa"),
            P("gx", "gy", "pa"),
            P("gx", "gy", "pa"),
            P(None, "gx", "gy", "pa"),
        ),
        check_vma=False,
    )
```

```python
import functools

import jax
import jax.numpy as jnp
from jax import lax
from jax.experimental import pallas as pl
from jax.experimental.pallas import tpu as pltpu
from jax.sharding import PartitionSpec as P

CHEB = 16
LANES = 128
HALO = CHEB
TIME_STEP = 8.0
F32 = jnp.float32


def with_halo(cells, sides, width):
    for axis, dim in sides:
        count = lax.axis_size(axis)
        head = lax.slice_in_dim(cells, 0, width, axis=dim)
        tail = lax.slice_in_dim(cells, cells.shape[dim] - width, cells.shape[dim], axis=dim)
        cells = jnp.concatenate(
            [
                lax.ppermute(tail, axis, [(i, (i + 1) % count) for i in range(count)]),
                cells,
                lax.ppermute(head, axis, [((i + 1) % count, i) for i in range(count)]),
            ],
            axis=dim,
        )
    return cells


def region(arr, spatial, offset):
    extent = arr.shape[-3:]
    window = [slice(1, length - 1) for length in extent]
    window[spatial] = slice(offset, extent[spatial] - 2 + offset)
    leading = [slice(None)] * (arr.ndim - 3)
    return arr[tuple(leading + window)]


def apply_operator(padded, kpad):
    centre = region(padded, 0, 1)
    kcentre = region(kpad, 0, 1)
    summed = jnp.zeros_like(centre)
    for spatial in range(3):
        for offset in (0, 2):
            summed = summed + 0.5 * (kcentre + region(kpad, spatial, offset)) * (
                centre - region(padded, spatial, offset)
            )
    return centre + TIME_STEP * summed


def stepwise(conductivity, stored_state, row_scales, cotangent, upper_bound):
    upper = upper_bound[0]
    kpad = with_halo(conductivity, (("gx", 0), ("gy", 1), ("pa", 2)), 1)
    count = lax.axis_size("pa")
    partner = lax.ppermute(stored_state, "pa", [(i, (i + count // 2) % count) for i in range(count)])
    previous = partner.astype(F32) * row_scales[:, :, None]
    rhs = jnp.stack((previous, cotangent))
    theta = 0.5 * (upper + 1.0)
    delta = 0.5 * (upper - 1.0)
    sigma = theta / delta
    sides = (("gx", 1), ("gy", 2), ("pa", 3))

    def sweep(step, carry):
        solved, residual, direction, rho = carry
        padded = with_halo(direction, sides, 1)
        solved = solved + direction
        residual = residual - apply_operator(padded, kpad)
        rho_next = 1.0 / (2.0 * sigma - rho)
        direction = rho_next * rho * direction + 2.0 * rho_next / delta * residual
        return (solved, residual, direction, rho_next)

    start = (jnp.zeros_like(rhs), rhs, rhs / theta, 1.0 / sigma)
    solved, residual, _, _ = lax.fori_loop(0, CHEB, sweep, start)
    pair = with_halo(solved, sides, 1)
    centre = region(pair, 0, 1)
    summed = jnp.zeros_like(solved[0])
    for spatial in range(3):
        for offset in (0, 2):
            differ = centre - region(pair, spatial, offset)
            summed = summed + differ[0] * differ[1]
    return (-0.5 * TIME_STEP * summed, solved[1], solved[0], residual)


G = 4
BX = 8
BY = 128
BZ = 128
STRIP = BZ // G
TOP = 8 + HALO
ROWS = BY + 2 * TOP
EXTENDED = BY + 2 * HALO
TILES = 2 * BY
SIDES = TILES + 8
ENDS = SIDES + BY // 2
FIELD = ENDS + 16
OWN = FIELD - TILES
BOTH = FIELD + OWN
TILE = 8
CHUNK = 32
WIDE = 16

BLOCK = (0, 3, 2, 1)
PLANES = BX


def roll(x, by):
    by %= LANES
    return pltpu.roll(x, by, 1) if by else x


def lanes_of(rows, strip):
    lane = lax.broadcasted_iota(jnp.int32, (rows, LANES), 1)
    return lax.rem(lane // STRIP - strip + 2 * G, G), lax.rem(lane, STRIP)


def pick(group, parts):
    out = parts[0]
    for b in range(1, G):
        out = jnp.where(group == b, parts[b], out)
    return out


def parity_order(transposed):
    src = lax.broadcasted_iota(jnp.int32, (LANES, LANES), 1 if transposed else 0)
    dst = lax.broadcasted_iota(jnp.int32, (LANES, LANES), 0 if transposed else 1)
    within = lax.rem(src, STRIP)
    place = src - within + 16 * lax.rem(within, 2) + within // 2
    return jnp.where(place == dst, 1.0, 0.0).astype(jnp.bfloat16)


def reorder(x, order):
    if x.dtype == jnp.bfloat16:
        return jnp.dot(x, order, preferred_element_type=F32)
    high = x.astype(jnp.bfloat16)
    rest = x - high.astype(F32)
    middle = rest.astype(jnp.bfloat16)
    low = (rest - middle.astype(F32)).astype(jnp.bfloat16)
    return (
        jnp.dot(high, order, preferred_element_type=F32)
        + jnp.dot(middle, order, preferred_element_type=F32)
        + jnp.dot(low, order, preferred_element_type=F32)
    )


def pack_kernel(strips, *refs):
    ins, outs = refs[: len(refs) - G], refs[len(refs) - G :]
    order = parity_order(False)
    groups = [lanes_of(BY, strips[d])[0] for d in range(G)]
    for n, array in enumerate(ins):
        for a in range(2):
            planes = reorder(array[4 * a : 4 * a + 4].reshape(4 * BY, LANES), order)
            parts = [roll(planes[BY * b : BY * (b + 1)], 32 * b) for b in range(4)]
            for d in range(G):
                outs[d][n, a] = pick(groups[d], parts)


def chebyshev_steps(upper, steps):
    bound = jnp.full((TILE, LANES), upper[0])
    theta = 0.5 * (bound + 1.0)
    delta = 0.5 * (bound - 1.0)
    sigma = theta / delta
    rho = 1.0 / sigma
    steps[0, 0] = 1.0 / theta
    steps[0, 1] = jnp.zeros_like(theta)
    for k in range(1, CHEB):
        rho_next = 1.0 / (2.0 * sigma - rho)
        steps[k, 0] = rho_next * rho
        steps[k, 1] = 2.0 * rho_next / delta
        rho = rho_next


def pack_previous_kernel(strips, upper, both, above, below, *outs):
    *outs, steps = outs
    chebyshev_steps(upper, steps)
    src = lax.broadcasted_iota(jnp.int32, (2 * LANES, 2 * LANES), 0)
    dst = lax.broadcasted_iota(jnp.int32, (2 * LANES, 2 * LANES), 1)
    place = LANES * lax.rem(src, 2) + 64 * (src // LANES) + lax.rem(src, LANES) // 2
    order = jnp.where(place == dst, 1.0, 0.0).astype(jnp.bfloat16)

    def give(planes, rows, start):
        groups = [lanes_of(rows, strips[d])[0] for d in range(G)]
        for m in range(4):
            pieces = []
            for i in (2 * m, 2 * m + 1):
                pair = planes[rows * i : rows * (i + 1)]
                for e in range(2):
                    pieces.append(pair[:, LANES * e : LANES * (e + 1)])
            for d in range(G):
                turned = [pltpu.roll(pieces[k], lax.rem(16 * strips[d] + 32 * k + 8, LANES), 1) for k in range(4)]
                outs[d][m, pl.ds(start, rows)] = pick(groups[d], turned)

    @pl.loop(0, BY // CHUNK)
    def _(t):
        r = pl.multiple_of(CHUNK * t, CHUNK)
        halves = [both[half, :, pl.ds(r, CHUNK)].reshape(BX * CHUNK, LANES) for half in range(2)]
        give(reorder(jnp.concatenate(halves, axis=1), order), CHUNK, pl.multiple_of(HALO + CHUNK * t, HALO))

    for start, array in ((0, above), (HALO + BY, below)):
        halves = [array[half].reshape(BX * HALO, LANES) for half in range(2)]
        give(reorder(jnp.concatenate(halves, axis=1), order), HALO, start)


def edge_kernel(places, *refs):
    msgs, (to_left, to_right) = refs[:G], refs[G:]
    lane = lax.broadcasted_iota(jnp.int32, (BY, LANES), 1)
    low = lax.rem(lane, 16) < 8
    for n in range(2):
        for d in range(G):
            first, second = msgs[d][n, 0], msgs[d][n, 1]
            to_left[n, places[0, d]] = jnp.where(low, first, roll(second, 8))
            to_right[n, places[1, d]] = jnp.where(low, roll(second, -8), first)


def rows_kernel(*refs):
    msgs, sides, (head, tail) = refs[:G], refs[G : G + 2], refs[G + 2 :]
    for n in range(2):
        for d in range(G):
            for out, rows in ((head, slice(0, HALO)), (tail, slice(BY - HALO, BY))):
                for a in range(2):
                    out[n, d, a] = msgs[d][n, a, rows]
                    out[n, d, 2 + a] = sides[a][n, d, rows]


def unpack(get_brick, get_edge, group, within, put):
    by_block = [BLOCK.index(q) for q in range(G)]
    edges = [[get_edge(side, d) for d in by_block] for side in range(2)]
    for a in range(2):
        far = 24 if a else 16
        own = [roll(get_brick(by_block[q], a), 32 * q) for q in range(G)]
        below = [roll(edges[0][q], 32 * q + far) for q in range(G)]
        above = [roll(edges[1][q], 32 * q - far) for q in range(G)]
        even = [
            jnp.where(within < 16, own[q], jnp.where(within < 24, above[q], below[(q + 1) % G])) for q in range(G)
        ]
        odd = [
            jnp.where(within < 8, above[(q - 1) % G], jnp.where(within < 16, below[q], own[q])) for q in range(G)
        ]
        for b in range(4):
            for e, parts in enumerate((even, odd)):
                whole = pick(group, [parts[(q - b) % G] for q in range(G)])
                put(4 * a + b, e, roll(whole, -32 * b - 16 * e))


def unpack_strip(get, group, put):
    by_block = [BLOCK.index(q) for q in range(G)]
    for m in range(4):
        turned = [roll(get(by_block[q], m), 32 * q) for q in range(G)]
        for k in range(4):
            whole = pick(group, [turned[(q - k) % G] for q in range(G)])
            put(2 * m + k // 2, k % 2, roll(whole, -32 * k - 8))


def solve_kernel(adjoint, strip, steps, *refs):
    if adjoint:
        bricks, (from_left, from_right, above, below) = refs[:G], refs[G : G + 4]
        outs, coefficients, (kap, *scratch) = refs[G + 4 : 2 * G + 4], refs[2 * G + 4 : 2 * G + 9], refs[2 * G + 9 :]
    else:
        strips_here, coefficients = refs[:G], refs[G : G + 5]
        outs, scratch = refs[G + 5 : 2 * G + 5], refs[2 * G + 5 :]
    kx, ky, kin, kout, diag = coefficients
    rhs, xa, xb, xc, turned, turned_first = scratch
    zero = jnp.zeros((TILE, LANES), F32)
    theta_inv = jnp.concatenate([steps[0, 0]] * 2, axis=0)

    def put_at(dst, to, rows):
        def put(i, e, val):
            dst[i, e, pl.ds(to, rows)] = val

        return put

    for i in range(PLANES):
        for e in range(2):
            for dst in (rhs, xa, xb, xc) + ((kap, ky) if adjoint else ()):
                dst[i, e, 0:TILE] = zero
                dst[i, e, ROWS - TILE : ROWS] = zero
        for dst in (kin, kout) if adjoint else ():
            dst[i, 0:TILE] = zero
            dst[i, ROWS - TILE : ROWS] = zero

    if adjoint:
        sides = (from_left, from_right)

        @pl.loop(0, BY // CHUNK)
        def _(t):
            at = pl.ds(pl.multiple_of(CHUNK * t, CHUNK), CHUNK)
            group, within = lanes_of(CHUNK, strip[0])
            for n, dst in enumerate((kap, rhs)):
                unpack(
                    lambda d, a: bricks[d][n, a, at],
                    lambda side, d: sides[side][n, d, at],
                    group,
                    within,
                    put_at(dst, pl.multiple_of(TOP + CHUNK * t, TILE), CHUNK),
                )

        group_halo, within_halo = lanes_of(HALO, strip[0])
        for n, dst in enumerate((kap, rhs)):
            for rows, start in ((above, TOP - HALO), (below, TOP + BY)):
                unpack(
                    lambda d, a: rows[n, d, a],
                    lambda side, d: rows[n, d, 2 + side],
                    group_halo,
                    within_halo,
                    put_at(dst, start, HALO),
                )
    else:

        @pl.loop(0, EXTENDED // CHUNK)
        def _(t):
            at = pl.ds(pl.multiple_of(CHUNK * t, CHUNK), CHUNK)
            group, _ = lanes_of(CHUNK, strip[0])
            unpack_strip(
                lambda d, m: strips_here[d][m, at],
                group,
                put_at(rhs, pl.multiple_of(TOP - HALO + CHUNK * t, TILE), CHUNK),
            )

    @pl.loop(0, (ROWS // TILE - 2) // 2)
    def _(t):
        rows = 2 * TILE
        r = pl.multiple_of(TILE + rows * t, TILE)
        at = pl.ds(r, rows)
        for i in range(PLANES):
            for e in range(2):
                xb[i, e, at] = rhs[i, e, at] * theta_inv
                xa[i, e, at] = jnp.zeros((rows, LANES), F32)
        if not adjoint:
            return
        first = [kap[0, e, at] for e in range(2)]
        now = first
        before = [4.0 * (k + roll(kap[PLANES - 1, e, at], 32)) for e, k in enumerate(first)]
        for i in range(PLANES):
            after = [kap[i + 1, e, at] if i + 1 < PLANES else roll(first[e], -32) for e in range(2)]
            inner = 4.0 * (now[0] + now[1])
            outer = 4.0 * (now[1] + roll(now[0], -1))
            outer_before = 4.0 * (now[0] + roll(now[1], 1))
            kin[i, at] = inner
            kout[i, at] = outer
            along = (inner + outer_before, inner + outer)
            for e in range(2):
                fx = 4.0 * (now[e] + after[e])
                fy = 4.0 * (now[e] + kap[i, e, pl.ds(r + 1, rows)])
                fym = 4.0 * (now[e] + kap[i, e, pl.ds(r - 1, rows)])
                kx[i, e, at] = fx
                ky[i, e, at] = fy
                diag[i, e, at] = 1.0 + (fx + before[e] + (fy + fym) + along[e])
                before[e] = fx
            now = after

    def turn_lanes(cur, r, turned):
        at = pl.ds(r, TILE)
        for i in range(PLANES):
            turned[i, 0] = roll(kout[i, at] * cur[i, 1, at], 1)
            turned[i, 1] = roll(cur[i, 0, at], -1)
        for e in range(2):
            turned[PLANES, e] = roll(kx[PLANES - 1, e, at] * cur[PLANES - 1, e, at], 32)
            turned[PLANES + 1, e] = roll(cur[0, e, at], -32)

    def advance(alpha, beta, old, cur, new, r, turned):
        at = pl.ds(r, TILE)
        now = [cur[0, e, at] for e in range(2)]
        before = fbefore = None
        for i in range(PLANES):
            fx = [kx[i, e, at] for e in range(2)]
            inner, outer = kin[i, at], kout[i, at]
            if i + 1 < PLANES:
                after = [cur[i + 1, e, at] for e in range(2)]
            else:
                after = [turned[PLANES + 1, e] for e in range(2)]
            for e in range(2):
                near = ky[i, e, at] * cur[i, e, pl.ds(r + 1, TILE)]
                near = near + ky[i, e, pl.ds(r - 1, TILE)] * cur[i, e, pl.ds(r - 1, TILE)]
                side = turned[i, e]
                near = near + (inner * now[1 - e] + (outer * side if e else side))
                behind = fbefore[e] * before[e] if i else turned[PLANES, e]
                near = near + (fx[e] * after[e] + behind)
                near = near + rhs[i, e, at]
                centre = (1.0 + alpha) - beta * diag[i, e, at]
                new[i, e, at] = centre * now[e] - alpha * old[i, e, at] + beta * near
            before, now, fbefore = now, after, fx

    def sweep(k, old, cur, new, span, following):
        alpha, beta = steps[k, 0], steps[k, 1]
        first, count, unroll = span
        for u in range(unroll):
            r = first + TILE * u
            advance(alpha, beta, old, cur, new, r, turned if u else turned_first)
            turn_lanes(cur, r + TILE, turned)
            if u == 2:
                turn_lanes(new, following, turned_first)

        @pl.loop(1, count // unroll)
        def _(t):
            for u in range(unroll):
                r = pl.multiple_of(first + TILE * (unroll * t + u), TILE)
                advance(alpha, beta, old, cur, new, r, turned)
                turn_lanes(cur, r + TILE, turned)

    wide = (TILE, ROWS // TILE - 2, 4)
    narrow = (2 * TILE, ROWS // TILE - 4, 3)

    def three(k, spans, following):
        sweep(k, xa, xb, xc, spans[0], spans[1][0])
        sweep(k + 1, xb, xc, xa, spans[1], spans[2][0])
        sweep(k + 2, xc, xa, xb, spans[2], following[0])

    turn_lanes(xb, wide[0], turned_first)

    @pl.loop(0, 2)
    def _(m):
        three(1 + 3 * m, (wide,) * 3, wide)

    three(7, (wide, narrow, narrow), narrow)

    @pl.loop(0, 2)
    def _(m):
        three(10 + 3 * m, (narrow,) * 3, narrow)

    def mains(whole, group, within):
        parts = [jnp.where(within < 16, even, roll(odd, 16)) for even, odd in whole]
        turned = [roll(parts[i], 32 * (i % 4)) for i in range(PLANES)]
        return parts, [
            [pick(group, [turned[4 * a + (q - d) % G] for q in range(G)]) for a in range(2)] for d in range(G)
        ]

    def ends_of(whole, within):
        tree = [jnp.where(within == 31, odd, even) for even, odd in whole]
        for level in range(3):
            width = 1 << level
            keep = (lax.rem(within + 1, STRIP) < width) | ((within >= 16) & (within < 16 + width))
            tree = [jnp.where(keep, tree[j], roll(tree[j + 1], width)) for j in range(0, len(tree), 2)]
        return jnp.where(within < 8, roll(tree[0], 1), roll(tree[0], -8))

    def load(field, row, rows):
        return [[field[i, e, pl.ds(row, rows)] for e in range(2)] for i in range(PLANES)]

    fields = ((xb, 0),) + (((kap, FIELD - TILES),) if adjoint else ())

    @pl.loop(0, BY // 2 // CHUNK)
    def _(t):
        group, within = lanes_of(CHUNK, strip[0])
        for field, base in fields:
            beside = []
            for upper_rows in range(2):
                start = BY // 2 * upper_rows
                parts, main = mains(load(field, pl.multiple_of(TOP + start + CHUNK * t, TILE), CHUNK), group, within)
                if field is xb:
                    for d in range(G):
                        for a in range(2):
                            outs[d][pl.ds(pl.multiple_of(BY * a + start + CHUNK * t, TILE), CHUNK)] = main[d][a]
                beside += [roll(parts[PLANES - 1], 32 + 64 * upper_rows), roll(parts[0], 64 * upper_rows)]
            at = pl.ds(pl.multiple_of(base + SIDES + CHUNK * t, TILE), CHUNK)
            for d in range(G):
                outs[d][at] = pick(group, [beside[(q - d) % G] for q in range(G)])

    sub = lax.broadcasted_iota(jnp.int32, (TILE, LANES), 0)
    group, within = lanes_of(TILE, strip[0])
    group_run, within_run = lanes_of(16, strip[0])
    half_run = within_run // 16
    for field, base in fields:
        over = mains(load(field, TOP - TILE, TILE), group, within)[1]
        under = mains(load(field, TOP + BY, TILE), group, within)[1]
        for d in range(G):
            rows = [pltpu.roll(v, by, 0) for a, by in ((0, 1), (1, 3)) for v in (over[d][a], under[d][a])]
            tile = rows[3]
            for j in range(3):
                tile = jnp.where(sub == j, rows[j], tile)
            outs[d][base + TILES : base + TILES + TILE] = tile
        runs = [roll(ends_of(load(field, TOP + 16 * run, 16), within_run), 16 * run) for run in range(8)]
        evens = [pick(group_run, [runs[2 * ((q - d) % G)] for q in range(G)]) for d in range(G)]
        odds = [pick(group_run, [runs[2 * ((q - d) % G) + 1] for q in range(G)]) for d in range(G)]
        for d in range(G):
            outs[d][base + ENDS : base + ENDS + 16] = jnp.where(half_run == 0, evens[d], odds[d])


def collect(strips, msgs, padded, ends, own):
    order = parity_order(True)

    def owners(rows):
        return [lanes_of(rows, strips[d])[0] for d in range(G)]

    def choose(owner, parts, b):
        out = parts[0]
        for d in range(1, G):
            out = jnp.where(owner[d] == b, parts[d], out)
        return roll(out, -32 * b)

    def bricks(row, rows):
        return [roll(msgs[d][pl.ds(row, rows)], -32 * d) for d in range(G)]

    base = 0 if own is None else FIELD - TILES

    @pl.loop(0, BY // CHUNK)
    def _(t):
        to = pl.ds(pl.multiple_of(TILE + CHUNK * t, TILE), CHUNK)
        if own is not None:
            for c in range(BX):
                padded[1 + c, to] = own[c, pl.ds(pl.multiple_of(CHUNK * t, CHUNK), CHUNK)]
            return
        owner = owners(CHUNK)
        whole = []
        for a in range(2):
            parts = bricks(pl.multiple_of(BY * a + CHUNK * t, TILE), CHUNK)
            whole += [choose(owner, parts, b) for b in range(4)]
        ordered = reorder(jnp.concatenate(whole, axis=0), order)
        for c in range(BX):
            padded[1 + c, to] = ordered[CHUNK * c : CHUNK * (c + 1)]

    @pl.loop(0, BY // 2 // CHUNK)
    def _(t):
        owner = owners(CHUNK)
        parts = bricks(pl.multiple_of(base + SIDES + CHUNK * t, TILE), CHUNK)
        ordered = reorder(jnp.concatenate([choose(owner, parts, b) for b in range(4)], axis=0), order)
        for j, (at, start) in enumerate(((0, 0), (1 + BX, 0), (0, BY // 2), (1 + BX, BY // 2))):
            to = pl.ds(pl.multiple_of(TILE + start + CHUNK * t, TILE), CHUNK)
            padded[at, to] = ordered[CHUNK * j : CHUNK * (j + 1)]

    parts = bricks(base + ENDS, 16)
    for side, end in enumerate((0, G - 1)):
        val = parts[0]
        for d in range(1, G):
            val = jnp.where(strips[d] == end, parts[d], val)
        ends[side] = val

    owner = owners(TILE)
    parts = bricks(base + TILES, TILE)
    ordered = reorder(jnp.concatenate([choose(owner, parts, b) for b in range(4)], axis=0), order)
    for c in range(BX):
        val = pltpu.roll(ordered[TILE * (c % 4) : TILE * (c % 4 + 1)], 5 if c >= 4 else 7, 0)
        padded[1 + c, 0:TILE] = val
        padded[1 + c, TILE + BY : 2 * TILE + BY] = val


def across(padded, c, t):
    r8 = pl.multiple_of(WIDE * t + TILE, TILE)
    return padded[1 + c, pl.ds(r8, WIDE)], [
        padded[c, pl.ds(r8, WIDE)],
        padded[c + 2, pl.ds(r8, WIDE)],
        padded[1 + c, pl.ds(r8 - 1, WIDE)],
        padded[1 + c, pl.ds(r8 + 1, WIDE)],
    ]


def along(cell, ends, c, t):
    lane = lax.broadcasted_iota(jnp.int32, (WIDE, LANES), 1)
    low = pltpu.roll(ends[0], lax.rem(LANES - 16 * t - c + LANES, LANES), 1)
    high = pltpu.roll(ends[1], lax.rem(23 - 16 * t - c + 2 * LANES, LANES), 1)
    return [
        jnp.where(lane == 0, low, roll(cell, 1)),
        jnp.where(lane == LANES - 1, high, roll(cell, -1)),
    ]


def adjoint_kernel(strips, m0, m1, m2, m3, cond, cot, adjoint, residual, padded, kap, faces, differences, ends, kends):
    collect(strips, (m0, m1, m2, m3), padded, ends, None)
    collect(strips, (m0, m1, m2, m3), kap, kends, cond)

    @pl.loop(0, BY // WIDE)
    def _(t):
        at = pl.ds(pl.multiple_of(WIDE * t, WIDE), WIDE)
        for c in range(BX):
            k, knear = across(kap, c, t)
            x, xnear = across(padded, c, t)
            total = 0.0
            for kn, xn in zip(knear, xnear):
                total = total + (k + kn) * (x - xn)
            for side, (kn, xn) in enumerate(zip(along(k, kends, c, t), along(x, ends, c, t))):
                face, differ = k + kn, x - xn
                faces[side, c, at] = face
                differences[side, c, at] = differ
                total = total + face * differ
            adjoint[c, at] = x
            residual[c, at] = cot[c, at] - (x + (0.5 * TIME_STEP) * total)


def state_kernel(strips, m0, m1, m2, m3, previous, adj, kap, faces, differences, adj_residual, grad, state, residuals, padded, ends):
    collect(strips, (m0, m1, m2, m3), padded, ends, None)

    @pl.loop(0, BY // WIDE)
    def _(t):
        at = pl.ds(pl.multiple_of(WIDE * t, WIDE), WIDE)
        for c in range(BX):
            k, knear = across(kap, c, t)
            x, xnear = across(padded, c, t)
            y, ynear = across(adj, c, t)
            total = product = 0.0
            for kn, xn, yn in zip(knear, xnear, ynear):
                differ = x - xn
                total = total + (k + kn) * differ
                product = product + differ * (y - yn)
            for side, xn in enumerate(along(x, ends, c, t)):
                differ = x - xn
                total = total + faces[side, c, at] * differ
                product = product + differ * differences[side, c, at]
            grad[c, at] = (-0.5 * TIME_STEP) * product
            state[c, at] = x
            residuals[0, c, at] = previous[0, c, at] - (x + (0.5 * TIME_STEP) * total)
            residuals[1, c, at] = adj_residual[c, at]


def call(kernel, outs, smem, vmem, scratch=(), micros=2, mebibytes=16):
    vm = pl.BlockSpec(memory_space=pltpu.VMEM)
    sm = pl.BlockSpec(memory_space=pltpu.SMEM)
    return pl.pallas_call(
        kernel,
        out_shape=[jax.ShapeDtypeStruct(shape, F32) for shape in outs],
        in_specs=[sm] * len(smem) + [vm] * len(vmem),
        out_specs=[vm] * len(outs),
        scratch_shapes=[pltpu.VMEM(shape, F32) for shape in scratch],
        compiler_params=pltpu.CompilerParams(vmem_limit_bytes=mebibytes * 1024 * 1024),
        cost_estimate=pl.CostEstimate(flops=0, bytes_accessed=micros * 3_000_000, transcendentals=0),
    )(*smem, *vmem)


def shifted(x, axis, by):
    count = lax.axis_size(axis)
    return lax.ppermute(x, axis, [(i, (i + by) % count) for i in range(count)])


def around(x, by):
    order = [2 * g for g in range(G)] + [2 * g + 1 for g in reversed(range(G))]
    return lax.ppermute(x, ("gx", "pa"), [(at, order[(i + by) % len(order)]) for i, at in enumerate(order)])


def redistributed(conductivity, stored_state, row_scales, cotangent, upper_bound):
    g = lax.axis_index("gx")
    pa = lax.axis_index("pa")

    def strip_of(device):
        return jnp.where(pa == 0, device, G - 1 - device)

    steps = jnp.arange(G, dtype=jnp.int32)
    ahead = lax.rem(g + steps, G)
    behind = lax.rem(g - steps + G, G)
    strip = strip_of(g)
    left_g = jnp.where(pa == 0, jnp.maximum(g - 1, 0), jnp.minimum(g + 1, G - 1))
    right_g = jnp.where(pa == 0, jnp.minimum(g + 1, G - 1), jnp.maximum(g - 1, 0))
    places = lax.rem(jnp.stack((left_g - g + steps, right_g - g + steps)) + G, G)

    brick = (2, 2, BY, LANES)
    parts = call(pack_kernel, [brick] * G, [strip_of(ahead)], [conductivity, cotangent])
    parts, stored_state = lax.optimization_barrier((parts, stored_state))
    parts = [parts[0]] + [shifted(parts[d], "gx", d) for d in range(1, G)]
    stored = shifted(stored_state, "pa", 1)
    both = jnp.stack((stored, stored_state)).astype(F32) * row_scales[:, :, None]
    above_rows = shifted(both[:, :, BY - HALO :], "gy", 1)
    below_rows = shifted(both[:, :, :HALO], "gy", -1)
    parts, above_rows, below_rows = lax.optimization_barrier((parts, above_rows, below_rows))
    edge = (2, G, BY, LANES)
    rim = (2, G, 4, HALO, LANES)
    to_left, to_right = call(edge_kernel, [edge, edge], [places], parts)
    to_left, below_rows = lax.optimization_barrier((to_left, below_rows))
    *messages, steps_here = call(
        pack_previous_kernel,
        [(4, EXTENDED, LANES)] * G + [(CHEB, 2, TILE, LANES)],
        [strip_of(ahead), upper_bound],
        [both, above_rows, below_rows],
    )
    from_left, from_right = around(to_right, 1), around(to_left, -1)
    from_left, from_right, own = lax.optimization_barrier((from_left, from_right, messages[0]))
    head, tail = call(rows_kernel, [rim, rim], [], [*parts, from_left, from_right])
    halos = [from_left, from_right, shifted(tail, "gy", 1), shifted(head, "gy", -1)]

    second = [own] + [shifted(messages[d], "gx", d) for d in range(1, G)]

    line = (PLANES, 2, ROWS, LANES)
    half = (PLANES, ROWS, LANES)
    lines = [line] * 4 + [(PLANES + 2, 2, TILE, LANES)] * 2
    setup = [strip[None]]

    def home(solved):
        return [solved[0]] + [shifted(solved[d], "gx", d) for d in range(1, G)]

    *solved_adjoint, kx, ky, kin, kout, diag = call(
        functools.partial(solve_kernel, True),
        [(BOTH, LANES)] * G + [line, line, half, half, line],
        setup,
        [steps_here, *parts, *halos],
        [line] + lines,
        micros=25,
        mebibytes=24,
    )
    solved_adjoint = home(solved_adjoint)
    solved_state = home(
        call(
            functools.partial(solve_kernel, False),
            [(FIELD, LANES)] * G,
            setup,
            [steps_here, *second, kx, ky, kin, kout, diag],
            lines,
            micros=25,
            mebibytes=24,
        )
    )

    out = (BX, BY, LANES)
    padded = (BX + 2, BY + 16, LANES)
    ends = (2, 16, LANES)
    here = strip_of(behind)
    adjoint, adj_residual, adj, kap, faces, differences = call(
        adjoint_kernel,
        [out, out, padded, padded, (2,) + out, (2,) + out],
        [here],
        [*solved_adjoint, conductivity, cotangent],
        [ends, ends],
    )
    grad, state, residuals = call(
        state_kernel,
        [out, out, (2,) + out],
        [here],
        [*solved_state, both, adj, kap, faces, differences, adj_residual],
        [padded, ends],
    )
    return grad, adjoint, state, residuals


def body(conductivity, stored_state, row_scales, cotangent, upper_bound):
    strips_fit = (
        lax.axis_size("gx") == G
        and lax.axis_size("pa") == 2
        and conductivity.shape == (BX, BY, BZ)
    )
    run = redistributed if strips_fit else stepwise
    return tuple(run(conductivity, stored_state, row_scales, cotangent, upper_bound))


def solution(mesh):
    return jax.shard_map(
        body,
        mesh=mesh,
        in_specs=(
            P("gx", "gy", "pa"),
            P("gx", "gy", "pa"),
            P("gx", "gy"),
            P("gx", "gy", "pa"),
            P(),
        ),
        out_specs=(
            P("gx", "gy", "pa"),
            P("gx", "gy", "pa"),
            P("gx", "gy", "pa"),
            P(None, "gx", "gy", "pa"),
        ),
        check_vma=False,
    )
```

```python
import functools

import jax
import jax.numpy as jnp
from jax import lax
from jax.experimental import pallas as pl
from jax.experimental.pallas import tpu as pltpu
from jax.sharding import PartitionSpec as P

CHEB = 16
LANES = 128
HALO = CHEB
TIME_STEP = 8.0
F32 = jnp.float32


def with_halo(cells, sides, width):
    for axis, dim in sides:
        count = lax.axis_size(axis)
        head = lax.slice_in_dim(cells, 0, width, axis=dim)
        tail = lax.slice_in_dim(cells, cells.shape[dim] - width, cells.shape[dim], axis=dim)
        cells = jnp.concatenate(
            [
                lax.ppermute(tail, axis, [(i, (i + 1) % count) for i in range(count)]),
                cells,
                lax.ppermute(head, axis, [((i + 1) % count, i) for i in range(count)]),
            ],
            axis=dim,
        )
    return cells


def region(arr, spatial, offset):
    extent = arr.shape[-3:]
    window = [slice(1, length - 1) for length in extent]
    window[spatial] = slice(offset, extent[spatial] - 2 + offset)
    leading = [slice(None)] * (arr.ndim - 3)
    return arr[tuple(leading + window)]


def apply_operator(padded, kpad):
    centre = region(padded, 0, 1)
    kcentre = region(kpad, 0, 1)
    summed = jnp.zeros_like(centre)
    for spatial in range(3):
        for offset in (0, 2):
            summed = summed + 0.5 * (kcentre + region(kpad, spatial, offset)) * (
                centre - region(padded, spatial, offset)
            )
    return centre + TIME_STEP * summed


def stepwise(conductivity, stored_state, row_scales, cotangent, upper_bound):
    upper = upper_bound[0]
    kpad = with_halo(conductivity, (("gx", 0), ("gy", 1), ("pa", 2)), 1)
    count = lax.axis_size("pa")
    partner = lax.ppermute(stored_state, "pa", [(i, (i + count // 2) % count) for i in range(count)])
    previous = partner.astype(F32) * row_scales[:, :, None]
    rhs = jnp.stack((previous, cotangent))
    theta = 0.5 * (upper + 1.0)
    delta = 0.5 * (upper - 1.0)
    sigma = theta / delta
    sides = (("gx", 1), ("gy", 2), ("pa", 3))

    def sweep(step, carry):
        solved, residual, direction, rho = carry
        padded = with_halo(direction, sides, 1)
        solved = solved + direction
        residual = residual - apply_operator(padded, kpad)
        rho_next = 1.0 / (2.0 * sigma - rho)
        direction = rho_next * rho * direction + 2.0 * rho_next / delta * residual
        return (solved, residual, direction, rho_next)

    start = (jnp.zeros_like(rhs), rhs, rhs / theta, 1.0 / sigma)
    solved, residual, _, _ = lax.fori_loop(0, CHEB, sweep, start)
    pair = with_halo(solved, sides, 1)
    centre = region(pair, 0, 1)
    summed = jnp.zeros_like(solved[0])
    for spatial in range(3):
        for offset in (0, 2):
            differ = centre - region(pair, spatial, offset)
            summed = summed + differ[0] * differ[1]
    return (-0.5 * TIME_STEP * summed, solved[1], solved[0], residual)


G = 4
BX = 8
BY = 128
BZ = 128
STRIP = BZ // G
TOP = 8 + HALO
ROWS = BY + 2 * TOP
EXTENDED = BY + 2 * HALO
TILES = 2 * BY
SIDES = TILES + 8
ENDS = SIDES + BY // 2
FIELD = ENDS + 16
OWN = FIELD - TILES
BOTH = FIELD + OWN
TILE = 8
CHUNK = 32
SPAN = 64
WIDE = 16

BLOCK = (0, 3, 2, 1)
PLANES = BX


def roll(x, by):
    by %= LANES
    return pltpu.roll(x, by, 1) if by else x


def lanes_of(rows, strip):
    lane = lax.broadcasted_iota(jnp.int32, (rows, LANES), 1)
    return lax.rem(lane // STRIP - strip + 2 * G, G), lax.rem(lane, STRIP)


def pick(group, parts):
    out = parts[0]
    for b in range(1, G):
        out = jnp.where(group == b, parts[b], out)
    return out


def parity_order(transposed):
    src = lax.broadcasted_iota(jnp.int32, (LANES, LANES), 1 if transposed else 0)
    dst = lax.broadcasted_iota(jnp.int32, (LANES, LANES), 0 if transposed else 1)
    within = lax.rem(src, STRIP)
    place = src - within + 16 * lax.rem(within, 2) + within // 2
    return jnp.where(place == dst, 1.0, 0.0).astype(jnp.bfloat16)


def reorder(x, order):
    if x.dtype == jnp.bfloat16:
        return jnp.dot(x, order, preferred_element_type=F32)
    high = x.astype(jnp.bfloat16)
    rest = x - high.astype(F32)
    middle = rest.astype(jnp.bfloat16)
    low = (rest - middle.astype(F32)).astype(jnp.bfloat16)
    return (
        jnp.dot(high, order, preferred_element_type=F32)
        + jnp.dot(middle, order, preferred_element_type=F32)
        + jnp.dot(low, order, preferred_element_type=F32)
    )


def pack_kernel(strips, *refs):
    ins, outs = refs[: len(refs) - G], refs[len(refs) - G :]
    order = parity_order(False)
    groups = [lanes_of(BY, strips[d])[0] for d in range(G)]
    for n, array in enumerate(ins):
        for a in range(2):
            planes = reorder(array[4 * a : 4 * a + 4].reshape(4 * BY, LANES), order)
            parts = [roll(planes[BY * b : BY * (b + 1)], 32 * b) for b in range(4)]
            for d in range(G):
                outs[d][n, a] = pick(groups[d], parts)


def chebyshev_steps(upper, steps):
    bound = jnp.full((TILE, LANES), upper[0])
    theta = 0.5 * (bound + 1.0)
    delta = 0.5 * (bound - 1.0)
    sigma = theta / delta
    rho = 1.0 / sigma
    steps[0, 0] = 1.0 / theta
    steps[0, 1] = jnp.zeros_like(theta)
    for k in range(1, CHEB):
        rho_next = 1.0 / (2.0 * sigma - rho)
        steps[k, 0] = rho_next * rho
        steps[k, 1] = 2.0 * rho_next / delta
        rho = rho_next


def pack_previous_kernel(strips, upper, both, above, below, *outs):
    *outs, steps = outs
    chebyshev_steps(upper, steps)
    src = lax.broadcasted_iota(jnp.int32, (2 * LANES, 2 * LANES), 0)
    dst = lax.broadcasted_iota(jnp.int32, (2 * LANES, 2 * LANES), 1)
    place = LANES * lax.rem(src, 2) + 64 * (src // LANES) + lax.rem(src, LANES) // 2
    order = jnp.where(place == dst, 1.0, 0.0).astype(jnp.bfloat16)

    def give(planes, rows, start):
        groups = [lanes_of(rows, strips[d])[0] for d in range(G)]
        for m in range(4):
            pieces = []
            for i in (2 * m, 2 * m + 1):
                pair = planes[rows * i : rows * (i + 1)]
                for e in range(2):
                    pieces.append(pair[:, LANES * e : LANES * (e + 1)])
            for d in range(G):
                turned = [pltpu.roll(pieces[k], lax.rem(16 * strips[d] + 32 * k + 8, LANES), 1) for k in range(4)]
                outs[d][m, pl.ds(start, rows)] = pick(groups[d], turned)

    @pl.loop(0, BY // CHUNK)
    def _(t):
        r = pl.multiple_of(CHUNK * t, CHUNK)
        halves = [both[half, :, pl.ds(r, CHUNK)].reshape(BX * CHUNK, LANES) for half in range(2)]
        give(reorder(jnp.concatenate(halves, axis=1), order), CHUNK, pl.multiple_of(HALO + CHUNK * t, HALO))

    for start, array in ((0, above), (HALO + BY, below)):
        halves = [array[half].reshape(BX * HALO, LANES) for half in range(2)]
        give(reorder(jnp.concatenate(halves, axis=1), order), HALO, start)


def edge_kernel(places, *refs):
    msgs, (to_left, to_right) = refs[:G], refs[G:]
    lane = lax.broadcasted_iota(jnp.int32, (BY, LANES), 1)
    low = lax.rem(lane, 16) < 8
    for n in range(2):
        for d in range(G):
            first, second = msgs[d][n, 0], msgs[d][n, 1]
            to_left[n, places[0, d]] = jnp.where(low, first, roll(second, 8))
            to_right[n, places[1, d]] = jnp.where(low, roll(second, -8), first)


def rows_kernel(*refs):
    msgs, sides, (head, tail) = refs[:G], refs[G : G + 2], refs[G + 2 :]
    for n in range(2):
        for d in range(G):
            for out, rows in ((head, slice(0, HALO)), (tail, slice(BY - HALO, BY))):
                for a in range(2):
                    out[n, d, a] = msgs[d][n, a, rows]
                    out[n, d, 2 + a] = sides[a][n, d, rows]


def unpack(get_brick, get_edge, group, within, put):
    by_block = [BLOCK.index(q) for q in range(G)]
    edges = [[get_edge(side, d) for d in by_block] for side in range(2)]
    for a in range(2):
        far = 24 if a else 16
        own = [roll(get_brick(by_block[q], a), 32 * q) for q in range(G)]
        below = [roll(edges[0][q], 32 * q + far) for q in range(G)]
        above = [roll(edges[1][q], 32 * q - far) for q in range(G)]
        even = [
            jnp.where(within < 16, own[q], jnp.where(within < 24, above[q], below[(q + 1) % G])) for q in range(G)
        ]
        odd = [
            jnp.where(within < 8, above[(q - 1) % G], jnp.where(within < 16, below[q], own[q])) for q in range(G)
        ]
        for b in range(4):
            for e, parts in enumerate((even, odd)):
                whole = pick(group, [parts[(q - b) % G] for q in range(G)])
                put(4 * a + b, e, roll(whole, -32 * b - 16 * e))


def unpack_strip(get, group, put):
    by_block = [BLOCK.index(q) for q in range(G)]
    for m in range(4):
        turned = [roll(get(by_block[q], m), 32 * q) for q in range(G)]
        for k in range(4):
            whole = pick(group, [turned[(q - k) % G] for q in range(G)])
            put(2 * m + k // 2, k % 2, roll(whole, -32 * k - 8))


def solve_kernel(adjoint, strip, steps, *refs):
    if adjoint:
        bricks, (from_left, from_right, above, below) = refs[:G], refs[G : G + 4]
        outs, coefficients, (kap, *scratch) = refs[G + 4 : 2 * G + 4], refs[2 * G + 4 : 2 * G + 9], refs[2 * G + 9 :]
    else:
        strips_here, coefficients = refs[:G], refs[G : G + 5]
        outs, scratch = refs[G + 5 : 2 * G + 5], refs[2 * G + 5 :]
    kx, ky, kin, kout, diag = coefficients
    rhs, xa, xb, xc, turned, turned_first = scratch
    zero = jnp.zeros((TILE, LANES), F32)
    theta_inv = jnp.concatenate([steps[0, 0]] * 2, axis=0)

    def put_at(dst, to, rows):
        def put(i, e, val):
            dst[i, e, pl.ds(to, rows)] = val

        return put

    for i in range(PLANES):
        for e in range(2):
            for dst in (rhs, xa, xb, xc) + ((kap, ky) if adjoint else ()):
                dst[i, e, 0:TILE] = zero
                dst[i, e, ROWS - TILE : ROWS] = zero
        for dst in (kin, kout) if adjoint else ():
            dst[i, 0:TILE] = zero
            dst[i, ROWS - TILE : ROWS] = zero

    if adjoint:
        sides = (from_left, from_right)

        @pl.loop(0, BY // CHUNK)
        def _(t):
            at = pl.ds(pl.multiple_of(CHUNK * t, CHUNK), CHUNK)
            group, within = lanes_of(CHUNK, strip[0])
            for n, dst in enumerate((kap, rhs)):
                unpack(
                    lambda d, a: bricks[d][n, a, at],
                    lambda side, d: sides[side][n, d, at],
                    group,
                    within,
                    put_at(dst, pl.multiple_of(TOP + CHUNK * t, TILE), CHUNK),
                )

        group_halo, within_halo = lanes_of(HALO, strip[0])
        for n, dst in enumerate((kap, rhs)):
            for rows, start in ((above, TOP - HALO), (below, TOP + BY)):
                unpack(
                    lambda d, a: rows[n, d, a],
                    lambda side, d: rows[n, d, 2 + side],
                    group_halo,
                    within_halo,
                    put_at(dst, start, HALO),
                )
    else:

        @pl.loop(0, EXTENDED // CHUNK)
        def _(t):
            at = pl.ds(pl.multiple_of(CHUNK * t, CHUNK), CHUNK)
            group, _ = lanes_of(CHUNK, strip[0])
            unpack_strip(
                lambda d, m: strips_here[d][m, at],
                group,
                put_at(rhs, pl.multiple_of(TOP - HALO + CHUNK * t, TILE), CHUNK),
            )

    @pl.loop(0, (ROWS // TILE - 2) // 2)
    def _(t):
        rows = 2 * TILE
        r = pl.multiple_of(TILE + rows * t, TILE)
        at = pl.ds(r, rows)
        for i in range(PLANES):
            for e in range(2):
                xb[i, e, at] = rhs[i, e, at] * theta_inv
                xa[i, e, at] = jnp.zeros((rows, LANES), F32)
        if not adjoint:
            return
        first = [kap[0, e, at] for e in range(2)]
        now = first
        before = [4.0 * (k + roll(kap[PLANES - 1, e, at], 32)) for e, k in enumerate(first)]
        for i in range(PLANES):
            after = [kap[i + 1, e, at] if i + 1 < PLANES else roll(first[e], -32) for e in range(2)]
            inner = 4.0 * (now[0] + now[1])
            outer = 4.0 * (now[1] + roll(now[0], -1))
            outer_before = 4.0 * (now[0] + roll(now[1], 1))
            kin[i, at] = inner
            kout[i, at] = outer
            along = (inner + outer_before, inner + outer)
            for e in range(2):
                fx = 4.0 * (now[e] + after[e])
                fy = 4.0 * (now[e] + kap[i, e, pl.ds(r + 1, rows)])
                fym = 4.0 * (now[e] + kap[i, e, pl.ds(r - 1, rows)])
                kx[i, e, at] = fx
                ky[i, e, at] = fy
                diag[i, e, at] = 1.0 + (fx + before[e] + (fy + fym) + along[e])
                before[e] = fx
            now = after

    def turn_lanes(cur, r, turned):
        at = pl.ds(r, TILE)
        for i in range(PLANES):
            turned[i, 0] = roll(kout[i, at] * cur[i, 1, at], 1)
            turned[i, 1] = roll(cur[i, 0, at], -1)
        for e in range(2):
            turned[PLANES, e] = roll(kx[PLANES - 1, e, at] * cur[PLANES - 1, e, at], 32)
            turned[PLANES + 1, e] = roll(cur[0, e, at], -32)

    def advance(alpha, beta, old, cur, new, r, turned):
        at = pl.ds(r, TILE)
        now = [cur[0, e, at] for e in range(2)]
        before = fbefore = None
        for i in range(PLANES):
            fx = [kx[i, e, at] for e in range(2)]
            inner, outer = kin[i, at], kout[i, at]
            if i + 1 < PLANES:
                after = [cur[i + 1, e, at] for e in range(2)]
            else:
                after = [turned[PLANES + 1, e] for e in range(2)]
            for e in range(2):
                near = ky[i, e, at] * cur[i, e, pl.ds(r + 1, TILE)]
                near = near + ky[i, e, pl.ds(r - 1, TILE)] * cur[i, e, pl.ds(r - 1, TILE)]
                side = turned[i, e]
                near = near + (inner * now[1 - e] + (outer * side if e else side))
                behind = fbefore[e] * before[e] if i else turned[PLANES, e]
                near = near + (fx[e] * after[e] + behind)
                near = near + rhs[i, e, at]
                centre = (1.0 + alpha) - beta * diag[i, e, at]
                new[i, e, at] = centre * now[e] - alpha * old[i, e, at] + beta * near
            before, now, fbefore = now, after, fx

    def sweep(k, old, cur, new, span, following):
        alpha, beta = steps[k, 0], steps[k, 1]
        first, count, unroll = span
        for u in range(unroll):
            r = first + TILE * u
            advance(alpha, beta, old, cur, new, r, turned if u else turned_first)
            turn_lanes(cur, r + TILE, turned)
            if u == 2:
                turn_lanes(new, following, turned_first)

        @pl.loop(1, count // unroll)
        def _(t):
            for u in range(unroll):
                r = pl.multiple_of(first + TILE * (unroll * t + u), TILE)
                advance(alpha, beta, old, cur, new, r, turned)
                turn_lanes(cur, r + TILE, turned)

    wide = (TILE, ROWS // TILE - 2, 4)
    narrow = (2 * TILE, ROWS // TILE - 4, 3)

    def three(k, spans, following):
        sweep(k, xa, xb, xc, spans[0], spans[1][0])
        sweep(k + 1, xb, xc, xa, spans[1], spans[2][0])
        sweep(k + 2, xc, xa, xb, spans[2], following[0])

    turn_lanes(xb, wide[0], turned_first)

    @pl.loop(0, 2)
    def _(m):
        three(1 + 3 * m, (wide,) * 3, wide)

    three(7, (wide, narrow, narrow), narrow)

    @pl.loop(0, 2)
    def _(m):
        three(10 + 3 * m, (narrow,) * 3, narrow)

    def mains(whole, group, within):
        parts = [jnp.where(within < 16, even, roll(odd, 16)) for even, odd in whole]
        turned = [roll(parts[i], 32 * (i % 4)) for i in range(PLANES)]
        return parts, [
            [pick(group, [turned[4 * a + (q - d) % G] for q in range(G)]) for a in range(2)] for d in range(G)
        ]

    def ends_of(whole, within):
        tree = [jnp.where(within == 31, odd, even) for even, odd in whole]
        for level in range(3):
            width = 1 << level
            keep = (lax.rem(within + 1, STRIP) < width) | ((within >= 16) & (within < 16 + width))
            tree = [jnp.where(keep, tree[j], roll(tree[j + 1], width)) for j in range(0, len(tree), 2)]
        return jnp.where(within < 8, roll(tree[0], 1), roll(tree[0], -8))

    def load(field, row, rows):
        return [[field[i, e, pl.ds(row, rows)] for e in range(2)] for i in range(PLANES)]

    fields = ((xb, 0),) + (((kap, FIELD - TILES),) if adjoint else ())

    @pl.loop(0, BY // 2 // CHUNK)
    def _(t):
        group, within = lanes_of(CHUNK, strip[0])
        for field, base in fields:
            beside = []
            for upper_rows in range(2):
                start = BY // 2 * upper_rows
                parts, main = mains(load(field, pl.multiple_of(TOP + start + CHUNK * t, TILE), CHUNK), group, within)
                if field is xb:
                    for d in range(G):
                        for a in range(2):
                            outs[d][pl.ds(pl.multiple_of(BY * a + start + CHUNK * t, TILE), CHUNK)] = main[d][a]
                beside += [roll(parts[PLANES - 1], 32 + 64 * upper_rows), roll(parts[0], 64 * upper_rows)]
            at = pl.ds(pl.multiple_of(base + SIDES + CHUNK * t, TILE), CHUNK)
            for d in range(G):
                outs[d][at] = pick(group, [beside[(q - d) % G] for q in range(G)])

    sub = lax.broadcasted_iota(jnp.int32, (TILE, LANES), 0)
    group, within = lanes_of(TILE, strip[0])
    group_run, within_run = lanes_of(16, strip[0])
    half_run = within_run // 16
    for field, base in fields:
        over = mains(load(field, TOP - TILE, TILE), group, within)[1]
        under = mains(load(field, TOP + BY, TILE), group, within)[1]
        for d in range(G):
            rows = [pltpu.roll(v, by, 0) for a, by in ((0, 1), (1, 3)) for v in (over[d][a], under[d][a])]
            tile = rows[3]
            for j in range(3):
                tile = jnp.where(sub == j, rows[j], tile)
            outs[d][base + TILES : base + TILES + TILE] = tile
        runs = [roll(ends_of(load(field, TOP + 16 * run, 16), within_run), 16 * run) for run in range(8)]
        evens = [pick(group_run, [runs[2 * ((q - d) % G)] for q in range(G)]) for d in range(G)]
        odds = [pick(group_run, [runs[2 * ((q - d) % G) + 1] for q in range(G)]) for d in range(G)]
        for d in range(G):
            outs[d][base + ENDS : base + ENDS + 16] = jnp.where(half_run == 0, evens[d], odds[d])


def collect(strips, msgs, padded, ends, own):
    order = parity_order(True)

    def owners(rows):
        return [lanes_of(rows, strips[d])[0] for d in range(G)]

    def choose(owner, parts, b):
        out = parts[0]
        for d in range(1, G):
            out = jnp.where(owner[d] == b, parts[d], out)
        return roll(out, -32 * b)

    def bricks(row, rows):
        return [roll(msgs[d][pl.ds(row, rows)], -32 * d) for d in range(G)]

    base = 0 if own is None else FIELD - TILES

    @pl.loop(0, BY // SPAN)
    def _(t):
        to = pl.ds(pl.multiple_of(TILE + SPAN * t, TILE), SPAN)
        if own is not None:
            for c in range(BX):
                padded[1 + c, to] = own[c, pl.ds(pl.multiple_of(SPAN * t, SPAN), SPAN)]
            return
        owner = owners(SPAN)
        whole = []
        for a in range(2):
            parts = bricks(pl.multiple_of(BY * a + SPAN * t, TILE), SPAN)
            whole += [choose(owner, parts, b) for b in range(4)]
        ordered = reorder(jnp.concatenate(whole, axis=0), order)
        for c in range(BX):
            padded[1 + c, to] = ordered[SPAN * c : SPAN * (c + 1)]

    @pl.loop(0, BY // 2 // SPAN)
    def _(t):
        owner = owners(SPAN)
        parts = bricks(pl.multiple_of(base + SIDES + SPAN * t, TILE), SPAN)
        ordered = reorder(jnp.concatenate([choose(owner, parts, b) for b in range(4)], axis=0), order)
        for j, (at, start) in enumerate(((0, 0), (1 + BX, 0), (0, BY // 2), (1 + BX, BY // 2))):
            to = pl.ds(pl.multiple_of(TILE + start + SPAN * t, TILE), SPAN)
            padded[at, to] = ordered[SPAN * j : SPAN * (j + 1)]

    parts = bricks(base + ENDS, 16)
    for side, end in enumerate((0, G - 1)):
        val = parts[0]
        for d in range(1, G):
            val = jnp.where(strips[d] == end, parts[d], val)
        ends[side] = val

    owner = owners(TILE)
    parts = bricks(base + TILES, TILE)
    ordered = reorder(jnp.concatenate([choose(owner, parts, b) for b in range(4)], axis=0), order)
    for c in range(BX):
        val = pltpu.roll(ordered[TILE * (c % 4) : TILE * (c % 4 + 1)], 5 if c >= 4 else 7, 0)
        padded[1 + c, 0:TILE] = val
        padded[1 + c, TILE + BY : 2 * TILE + BY] = val


def across(padded, c, t):
    r8 = pl.multiple_of(WIDE * t + TILE, TILE)
    return padded[1 + c, pl.ds(r8, WIDE)], [
        padded[c, pl.ds(r8, WIDE)],
        padded[c + 2, pl.ds(r8, WIDE)],
        padded[1 + c, pl.ds(r8 - 1, WIDE)],
        padded[1 + c, pl.ds(r8 + 1, WIDE)],
    ]


def along(cell, ends, c, t):
    lane = lax.broadcasted_iota(jnp.int32, (WIDE, LANES), 1)
    low = pltpu.roll(ends[0], lax.rem(LANES - 16 * t - c + LANES, LANES), 1)
    high = pltpu.roll(ends[1], lax.rem(23 - 16 * t - c + 2 * LANES, LANES), 1)
    return [
        jnp.where(lane == 0, low, roll(cell, 1)),
        jnp.where(lane == LANES - 1, high, roll(cell, -1)),
    ]


def adjoint_kernel(strips, m0, m1, m2, m3, cond, cot, adjoint, residual, padded, kap, faces, differences, ends, kends):
    collect(strips, (m0, m1, m2, m3), padded, ends, None)
    collect(strips, (m0, m1, m2, m3), kap, kends, cond)

    @pl.loop(0, BY // WIDE)
    def _(t):
        at = pl.ds(pl.multiple_of(WIDE * t, WIDE), WIDE)
        for c in range(BX):
            k, knear = across(kap, c, t)
            x, xnear = across(padded, c, t)
            total = 0.0
            for kn, xn in zip(knear, xnear):
                total = total + (k + kn) * (x - xn)
            for side, (kn, xn) in enumerate(zip(along(k, kends, c, t), along(x, ends, c, t))):
                face, differ = k + kn, x - xn
                faces[side, c, at] = face
                differences[side, c, at] = differ
                total = total + face * differ
            adjoint[c, at] = x
            residual[c, at] = cot[c, at] - (x + (0.5 * TIME_STEP) * total)


def state_kernel(strips, m0, m1, m2, m3, previous, adj, kap, faces, differences, adj_residual, grad, state, residuals, padded, ends):
    collect(strips, (m0, m1, m2, m3), padded, ends, None)

    @pl.loop(0, BY // WIDE)
    def _(t):
        at = pl.ds(pl.multiple_of(WIDE * t, WIDE), WIDE)
        for c in range(BX):
            k, knear = across(kap, c, t)
            x, xnear = across(padded, c, t)
            y, ynear = across(adj, c, t)
            total = product = 0.0
            for kn, xn, yn in zip(knear, xnear, ynear):
                differ = x - xn
                total = total + (k + kn) * differ
                product = product + differ * (y - yn)
            for side, xn in enumerate(along(x, ends, c, t)):
                differ = x - xn
                total = total + faces[side, c, at] * differ
                product = product + differ * differences[side, c, at]
            grad[c, at] = (-0.5 * TIME_STEP) * product
            state[c, at] = x
            residuals[0, c, at] = previous[0, c, at] - (x + (0.5 * TIME_STEP) * total)
            residuals[1, c, at] = adj_residual[c, at]


def call(kernel, outs, smem, vmem, scratch=(), micros=2, mebibytes=16):
    vm = pl.BlockSpec(memory_space=pltpu.VMEM)
    sm = pl.BlockSpec(memory_space=pltpu.SMEM)
    return pl.pallas_call(
        kernel,
        out_shape=[jax.ShapeDtypeStruct(shape, F32) for shape in outs],
        in_specs=[sm] * len(smem) + [vm] * len(vmem),
        out_specs=[vm] * len(outs),
        scratch_shapes=[pltpu.VMEM(shape, F32) for shape in scratch],
        compiler_params=pltpu.CompilerParams(vmem_limit_bytes=mebibytes * 1024 * 1024),
        cost_estimate=pl.CostEstimate(flops=0, bytes_accessed=micros * 3_000_000, transcendentals=0),
    )(*smem, *vmem)


def shifted(x, axis, by):
    count = lax.axis_size(axis)
    return lax.ppermute(x, axis, [(i, (i + by) % count) for i in range(count)])


def around(x, by):
    order = [2 * g for g in range(G)] + [2 * g + 1 for g in reversed(range(G))]
    return lax.ppermute(x, ("gx", "pa"), [(at, order[(i + by) % len(order)]) for i, at in enumerate(order)])


def redistributed(conductivity, stored_state, row_scales, cotangent, upper_bound):
    g = lax.axis_index("gx")
    pa = lax.axis_index("pa")

    def strip_of(device):
        return jnp.where(pa == 0, device, G - 1 - device)

    steps = jnp.arange(G, dtype=jnp.int32)
    ahead = lax.rem(g + steps, G)
    behind = lax.rem(g - steps + G, G)
    strip = strip_of(g)
    left_g = jnp.where(pa == 0, jnp.maximum(g - 1, 0), jnp.minimum(g + 1, G - 1))
    right_g = jnp.where(pa == 0, jnp.minimum(g + 1, G - 1), jnp.maximum(g - 1, 0))
    places = lax.rem(jnp.stack((left_g - g + steps, right_g - g + steps)) + G, G)

    brick = (2, 2, BY, LANES)
    parts = call(pack_kernel, [brick] * G, [strip_of(ahead)], [conductivity, cotangent])
    parts, stored_state = lax.optimization_barrier((parts, stored_state))
    parts = [parts[0]] + [shifted(parts[d], "gx", d) for d in range(1, G)]
    stored = shifted(stored_state, "pa", 1)
    both = jnp.stack((stored, stored_state)).astype(F32) * row_scales[:, :, None]
    above_rows = shifted(both[:, :, BY - HALO :], "gy", 1)
    below_rows = shifted(both[:, :, :HALO], "gy", -1)
    parts, above_rows, below_rows = lax.optimization_barrier((parts, above_rows, below_rows))
    edge = (2, G, BY, LANES)
    rim = (2, G, 4, HALO, LANES)
    to_left, to_right = call(edge_kernel, [edge, edge], [places], parts)
    to_left, below_rows = lax.optimization_barrier((to_left, below_rows))
    *messages, steps_here = call(
        pack_previous_kernel,
        [(4, EXTENDED, LANES)] * G + [(CHEB, 2, TILE, LANES)],
        [strip_of(ahead), upper_bound],
        [both, above_rows, below_rows],
    )
    from_left, from_right = around(to_right, 1), around(to_left, -1)
    from_left, from_right, own = lax.optimization_barrier((from_left, from_right, messages[0]))
    head, tail = call(rows_kernel, [rim, rim], [], [*parts, from_left, from_right])
    halos = [from_left, from_right, shifted(tail, "gy", 1), shifted(head, "gy", -1)]

    second = [own] + [shifted(messages[d], "gx", d) for d in range(1, G)]

    line = (PLANES, 2, ROWS, LANES)
    half = (PLANES, ROWS, LANES)
    lines = [line] * 4 + [(PLANES + 2, 2, TILE, LANES)] * 2
    setup = [strip[None]]

    def home(solved):
        return [solved[0]] + [shifted(solved[d], "gx", d) for d in range(1, G)]

    *solved_adjoint, kx, ky, kin, kout, diag = call(
        functools.partial(solve_kernel, True),
        [(BOTH, LANES)] * G + [line, line, half, half, line],
        setup,
        [steps_here, *parts, *halos],
        [line] + lines,
        micros=25,
        mebibytes=24,
    )
    solved_adjoint = home(solved_adjoint)
    solved_state = home(
        call(
            functools.partial(solve_kernel, False),
            [(FIELD, LANES)] * G,
            setup,
            [steps_here, *second, kx, ky, kin, kout, diag],
            lines,
            micros=25,
            mebibytes=24,
        )
    )

    out = (BX, BY, LANES)
    padded = (BX + 2, BY + 16, LANES)
    ends = (2, 16, LANES)
    here = strip_of(behind)
    adjoint, adj_residual, adj, kap, faces, differences = call(
        adjoint_kernel,
        [out, out, padded, padded, (2,) + out, (2,) + out],
        [here],
        [*solved_adjoint, conductivity, cotangent],
        [ends, ends],
    )
    grad, state, residuals = call(
        state_kernel,
        [out, out, (2,) + out],
        [here],
        [*solved_state, both, adj, kap, faces, differences, adj_residual],
        [padded, ends],
    )
    return grad, adjoint, state, residuals


def body(conductivity, stored_state, row_scales, cotangent, upper_bound):
    strips_fit = (
        lax.axis_size("gx") == G
        and lax.axis_size("pa") == 2
        and conductivity.shape == (BX, BY, BZ)
    )
    run = redistributed if strips_fit else stepwise
    return tuple(run(conductivity, stored_state, row_scales, cotangent, upper_bound))


def solution(mesh):
    return jax.shard_map(
        body,
        mesh=mesh,
        in_specs=(
            P("gx", "gy", "pa"),
            P("gx", "gy", "pa"),
            P("gx", "gy"),
            P("gx", "gy", "pa"),
            P(),
        ),
        out_specs=(
            P("gx", "gy", "pa"),
            P("gx", "gy", "pa"),
            P("gx", "gy", "pa"),
            P(None, "gx", "gy", "pa"),
        ),
        check_vma=False,
    )
```
